32 devices in a mesh: gx: 8 (over z, core), gy: 4 (over y, x).
Axes of the slice: x: 2, y: 2, z: 4, core: 2. Of those that a mesh axis runs over, the one named last changes fastest.
Arguments:
- design: float32 [64, 32, 128], P('gx', 'gy'), may hold values from 0.06 to 0.9
- passive: int32 [64, 32, 128], P('gx', 'gy'), may hold values 0 or 1
- basis_pairs: float32 [4, 2, 3, 64, 32, 128], P(None, None, None, 'gx', 'gy'), may hold values from -6 to 6
- supports: int32 [64, 32, 128], P('gx', 'gy'), may hold values 0 or 1
- stiffness: float32 [24, 24], replicated, may hold values from -1.25 to 1.25
- mass_matrix: float32 [24, 24], replicated, may hold values from -1.25 to 1.25
- volume_fraction: float32 [64], replicated, may hold values from 0.26 to 0.36
Outputs:
- sensitivity: float32 [64, 32, 128], P('gx', 'gy')
- design_next: float32 [64, 32, 128], P('gx', 'gy')
The draws below stay inside these ranges and needn't reach their ends.
All inputs are finite; a program needn't handle non-finite values. No bound on the sum of `passive` or of `supports` on one device may be relied on, other than what follows from the above.
Results may differ from the reference program's by a relative error of at most 0.0003.
Values sent between devices are 32-bit elements; how exact they have to be, the bound alone decides.
A program may use at most 64 MiB of HBM per device.

```python
import math
import jax
import jax.numpy as jnp
from jax import lax

EX = 8
NB = 4
BISECT = 6
REGIONS = 64
NX = 64
NY = 32
NZ = 128
N_GX = 8


def draw_design(key, part):
    across = jnp.arange(NX, dtype=jnp.float32) / max(NX - 1, 1)
    ramp = 0.3 + 0.6 * across
    base = jax.random.uniform(key, (NX, NY, NZ), jnp.float32, 0.2, 1.0)
    return (ramp[:, None, None] * base).astype(jnp.float32)


def plant(values, rng, least, largest):
    extent = values.shape
    index_at = [jax.random.randint(jax.random.fold_in(rng, axis), (), 0, extent[axis]) for axis in range(len(extent))]
    values = values.at[tuple(index_at)].set(least)
    longest = extent.index(max(extent))
    index_at[longest] = (index_at[longest] + 1) % extent[longest]
    return values.at[tuple(index_at)].set(largest)


def block_levels(key, extent, split, low, high):
    gain, own = 1.0, jax.random.fold_in(key, 6)
    for dim, blocks in split:
        steps = jnp.exp(jax.random.uniform(jax.random.fold_in(own, dim), (blocks,), jnp.float32, low / len(split), high / len(split)))
        gain = gain * jnp.repeat(steps, extent[dim] // blocks).reshape([-1 if axis == dim else 1 for axis in range(len(extent))])
    return gain


def bell_draw(rng, dims, deviation, bound, split=(), kind=jnp.bfloat16):
    level = block_levels(rng, dims, split, -0.22, 0.18) if split else 1.0
    entries = jax.random.normal(rng, dims, jnp.float32) * deviation * level
    return jnp.minimum(jnp.maximum(entries, -bound), bound).astype(kind)


def setup_inputs(seed: int = 0) -> dict:
    key_of = jax.random.split(jax.random.key(seed), 8)
    return {
        "design": draw_design(jax.random.fold_in(key_of[7], 71), 0),
        "passive": plant((jax.random.randint(key_of[1], (NX, NY, NZ), 0, 16) < 1).astype(jnp.int32), jax.random.fold_in(key_of[1], 1), 0, 1),
        "basis_pairs": bell_draw(key_of[2], (NB, 2, 3, NX, NY, NZ), 1.0, 6.0, ((3, 8), (4, 4)), jnp.float32),
        "supports": plant((jax.random.randint(key_of[3], (NX, NY, NZ), 0, 16) < 1).astype(jnp.int32), jax.random.fold_in(key_of[3], 1), 0, 1),
        "stiffness": bell_draw(key_of[4], (24, 24), 24 ** -0.5, 1.25, (), jnp.float32),
        "mass_matrix": bell_draw(key_of[5], (24, 24), 24 ** -0.5, 1.25, (), jnp.float32),
        "volume_fraction": jnp.clip(jax.random.uniform(key_of[6], (REGIONS,), jnp.float32, 0.26, 0.36), 0.26, 0.36),
    }


PENALTY_SCALE = 3.0 * (1.0 - 0.001)
OMEGA_SQUARED = 0.5
MOVE_LIMIT = 0.2

def filter_taps():
    tap_list = []
    for offset_x in range(-2, 3):
        for offset_y in range(-2, 3):
            for offset_z in range(-2, 3):
                weight = 3.0 - math.sqrt(offset_x * offset_x + offset_y * offset_y + offset_z * offset_z)
                if weight > 0.0:
                    tap_list.append((offset_x, offset_y, offset_z, weight))
    return tap_list

def stencil(padded, block_shape):
    result = jnp.zeros(block_shape, jnp.float32)
    for offset_x, offset_y, offset_z, weight in filter_taps():
        result = result + weight * padded[2 + offset_x:2 + offset_x + block_shape[0], 2 + offset_y:2 + offset_y + block_shape[1], 2 + offset_z:2 + offset_z + block_shape[2]]
    return result

def element_terms(extended, stiffness, mass_matrix):
    pair_count = extended.shape[0]
    cells_x = extended.shape[3] - 1
    cells_y = extended.shape[4] - 1
    cells_z = extended.shape[5] - 1
    stiff_energy = jnp.zeros((cells_x * cells_y * cells_z,), jnp.float32)
    mass_energy = jnp.zeros((cells_x * cells_y * cells_z,), jnp.float32)
    for pair_index in range(pair_count):
        vectors = []
        for member in range(2):
            row_list = []
            for corner_x in (0, 1):
                for corner_y in (0, 1):
                    for corner_z in (0, 1):
                        for component in range(3):
                            row_list.append(extended[pair_index, member, component, corner_x:corner_x + cells_x, corner_y:corner_y + cells_y, corner_z:corner_z + cells_z].reshape(-1))
            vectors.append(jnp.stack(row_list))
        state_rows, adjoint_rows = vectors
        stiff_energy = stiff_energy + lax.optimization_barrier(jnp.sum(state_rows * jnp.dot(stiffness, adjoint_rows, precision=lax.Precision.HIGHEST), axis=0))
        mass_energy = mass_energy + lax.optimization_barrier(jnp.sum(state_rows * jnp.dot(mass_matrix, adjoint_rows, precision=lax.Precision.HIGHEST), axis=0))
    return (stiff_energy.reshape(cells_x, cells_y, cells_z), mass_energy.reshape(cells_x, cells_y, cells_z))

def reference(design, passive, basis_pairs, supports, stiffness, mass_matrix, volume_fraction):
    block_shape = design.shape
    weight_sum = stencil(jnp.pad(jnp.ones(block_shape, jnp.float32), 2), block_shape)
    physical = jnp.where(passive == 1, 1.0, stencil(jnp.pad(design, 2), block_shape) / weight_sum)
    fields = basis_pairs * (1 - supports).astype(jnp.float32)
    extended = jnp.pad(fields, ((0, 0), (0, 0), (0, 0), (0, 1), (0, 1), (0, 1)))

    def block_terms(block_index):
        block_piece = lax.dynamic_slice_in_dim(extended, block_index * EX, EX + 1, axis=3)
        return element_terms(block_piece, stiffness, mass_matrix)
    stiff_parts, mass_parts = lax.map(block_terms, jnp.arange(N_GX, dtype=jnp.int32))
    stiff_energy = stiff_parts.reshape(block_shape)
    mass_energy = mass_parts.reshape(block_shape)
    raw_sensitivity = -(PENALTY_SCALE * physical * physical * stiff_energy - OMEGA_SQUARED * mass_energy)
    raw_sensitivity = jnp.where(passive == 1, 0.0, raw_sensitivity)
    sensitivity = stencil(jnp.pad(raw_sensitivity / weight_sum, 2), block_shape)
    benefit = jnp.maximum(-sensitivity, 0.0)
    floor_value = jnp.maximum(design - MOVE_LIMIT, 0.0)
    ceiling = jnp.minimum(design + MOVE_LIMIT, 1.0)
    band_cells = NZ // REGIONS
    target = volume_fraction * float(NX * NY * band_cells)

    def candidate(multiplier):
        per_cell = jnp.repeat(multiplier, band_cells)[None, None, :]
        trial = design * jnp.sqrt(benefit / per_cell)
        return jnp.where(passive == 1, 1.0, jnp.minimum(ceiling, jnp.maximum(floor_value, trial)))

    def region_sum(field):
        return lax.optimization_barrier(jnp.sum(field, axis=(0, 1))).reshape(REGIONS, band_cells).sum(axis=1)

    def bisect_step(step_index, bracket):
        low_end, high_end = bracket
        middle = jnp.sqrt(low_end * high_end)
        heavier = region_sum(candidate(middle)) > target
        return (jnp.where(heavier, middle, low_end), jnp.where(heavier, high_end, middle))
    start = (jnp.full((REGIONS,), 0.0001, jnp.float32), jnp.full((REGIONS,), 10000.0, jnp.float32))
    low_end, high_end = lax.fori_loop(0, BISECT, bisect_step, start)
    design_next = candidate(jnp.sqrt(low_end * high_end))
    return (sensitivity, design_next)
```

```python
import functools
import math

import jax
import jax.numpy as jnp
from jax import lax
from jax.experimental import pallas as pl
from jax.experimental.pallas import tpu as pltpu
from jax.sharding import PartitionSpec as P

PENALTY_SCALE = 3.0 * (1.0 - 0.001)
OMEGA_SQUARED = 0.5
MOVE_LIMIT = 0.2
LEVELS = 3
ROUNDS = 2
MESH = pl.DeviceIdType.MESH
AROUND = ((-1, 0), (1, 0), (0, -1), (0, 1), (-1, -1), (-1, 1), (1, -1), (1, 1))


def opposite(slot):
    dx, dy = AROUND[slot]
    return AROUND.index((-dx, -dy))


def z_shift(value, step):
    axis = value.ndim - 1
    size = value.shape[axis]
    lane = lax.broadcasted_iota(jnp.int32, value.shape, axis)
    moved = pltpu.roll(value, (-step) % size, axis)
    keep = lane < size - step if step > 0 else lane >= -step
    return jnp.where(keep, moved, 0.0)


def stencil(rows_at, size_x):
    spread = [[None] * (size_x + 4) for _ in range(3)]
    for plane in range(size_x + 4):
        tiles = [rows_at(plane, oy) for oy in range(-2, 3)]
        folded_y = (tiles[2], tiles[1] + tiles[3], tiles[0] + tiles[4])
        parts = [[], [], []]
        for cy, tile in enumerate(folded_y):
            folded_z = (
                tile,
                z_shift(tile, 1) + z_shift(tile, -1),
                z_shift(tile, 2) + z_shift(tile, -2),
            )
            for cz, entry in enumerate(folded_z):
                for cx in range(3):
                    weight = 3.0 - math.sqrt(cx * cx + cy * cy + cz * cz)
                    if weight > 0.0:
                        parts[cx].append(weight * entry)
        for cx in range(3):
            spread[cx][plane] = functools.reduce(lambda a, b: a + b, parts[cx])
    return [
        spread[0][i + 2]
        + (spread[1][i + 1] + spread[1][i + 3])
        + (spread[2][i] + spread[2][i + 4])
        for i in range(size_x)
    ]


def kernel(
    nx, ny, size_x, size_y, size_z, pairs, regions,
    design, passive, basis, supports, stiffness, mass_matrix, fraction,
    sensitivity, design_next,
    fields, send_x, send_y, send_c, recv_x, recv_y, recv_c,
    edge_send, edge_recv, wide, scaled, weights_hi, weights_lo, weight_sum, physical, energy,
    gather_y, gather_x,
    basis_send_sem, basis_recv_sem, halo_send_sem, halo_recv_sem,
    gy_send_sem, gy_recv_sem, gx_send_sem, gx_recv_sem,
):
    ix, iy = lax.axis_index("gx"), lax.axis_index("gy")
    pitch = 2 * size_y
    cells = size_x * size_y

    def there(dx, dy):
        return (
            (ix + dx >= 0) & (ix + dx < nx) & (iy + dy >= 0) & (iy + dy < ny)
        )

    barrier = pltpu.get_barrier_semaphore()
    for step in range(1, ny):
        pl.semaphore_signal(barrier, inc=1, device_id=(ix, lax.rem(iy + step, ny)), device_id_type=MESH)
    for step in range(1, nx):
        pl.semaphore_signal(barrier, inc=1, device_id=(lax.rem(ix + step, nx), iy), device_id_type=MESH)
    for dx, dy in AROUND[4:]:
        @pl.when(there(dx, dy))
        def _(dx=dx, dy=dy):
            pl.semaphore_signal(barrier, inc=1, device_id=(ix + dx, iy + dy), device_id_type=MESH)
    corners = sum(there(dx, dy).astype(jnp.int32) for dx, dy in AROUND[4:])

    free = 1.0 - supports[...].astype(jnp.float32)
    send_x[...] = basis[:, 0:size_y, :] * free[0:size_y][None]
    free_y = 1.0 - supports[pl.ds(0, size_x, stride=size_y), :].astype(jnp.float32)
    for f in range(6 * pairs):
        rows = basis[f, pl.ds(0, size_x, stride=size_y), :] * free_y
        send_y[f] = rows
        send_c[pl.ds(f, 1), :] = rows[0:1]

    def pack_edges(source, which):
        for x in range(2):
            edge_send[which, 2, x] = source[pl.ds(x * size_y, size_y), :]
            edge_send[which, 3, x] = source[pl.ds((size_x - 2 + x) * size_y, size_y), :]
        for y in range(2):
            edge_send[which, 0, y] = source[pl.ds(y, size_x, stride=size_y), :]
            edge_send[which, 1, y] = source[pl.ds(size_y - 2 + y, size_x, stride=size_y), :]

    def edge_copies(which):
        copies = []
        for slot, (dx, dy) in enumerate(AROUND):
            if dy == 0:
                src = edge_send.at[which, 2 if dx < 0 else 3]
            else:
                src = edge_send.at[which, 0 if dy < 0 else 1]
            copies.append(pltpu.make_async_remote_copy(
                src_ref=src,
                dst_ref=edge_recv.at[which, opposite(slot)],
                send_sem=halo_send_sem.at[which, slot],
                recv_sem=halo_recv_sem.at[which, opposite(slot)],
                device_id=(ix + dx, iy + dy),
                device_id_type=MESH,
            ))
        return copies

    def edge_start(copies):
        for (dx, dy), copy in zip(AROUND, copies):
            @pl.when(there(dx, dy))
            def _(copy=copy):
                copy.start()

    def edge_receive(copies, which):
        for slot, (dx, dy) in enumerate(AROUND):
            copy = copies[opposite(slot)]

            @pl.when(there(dx, dy))
            def _(copy=copy):
                copy.wait_recv()

            @pl.when(jnp.logical_not(there(dx, dy)))
            def _(slot=slot):
                edge_recv[which, slot] = jnp.zeros((2, size_y, size_z), jnp.float32)

    def edge_finish(copies):
        for (dx, dy), copy in zip(AROUND, copies):
            @pl.when(there(dx, dy))
            def _(copy=copy):
                copy.wait_send()

    span = 3 * size_y

    def assemble(source, which):
        for x in range(size_x):
            wide[pl.ds((x + 2) * span + size_y, size_y), :] = source[pl.ds(x * size_y, size_y), :]
        for x in range(2):
            wide[pl.ds(x * span + size_y, size_y), :] = edge_recv[which, 0, x]
            wide[pl.ds((size_x + 2 + x) * span + size_y, size_y), :] = edge_recv[which, 1, x]
        for y in range(2):
            low, high = size_y - 2 + y, 2 * size_y + y
            wide[pl.ds(2 * span + low, size_x, stride=span), :] = edge_recv[which, 2, y]
            wide[pl.ds(2 * span + high, size_x, stride=span), :] = edge_recv[which, 3, y]
            for x in range(2):
                for slot, row in ((4, low), (5, high)):
                    wide[pl.ds(x * span + row, 1), :] = edge_recv[which, slot, y, size_x - 2 + x : size_x - 1 + x, :]
                for slot, row in ((6, low), (7, high)):
                    wide[pl.ds((size_x + 2 + x) * span + row, 1), :] = edge_recv[which, slot, y, x : x + 1, :]

    def wide_rows(plane, oy):
        return wide[pl.ds(plane * span + size_y + oy, size_y), :]

    pack_edges(design, 0)

    pl.semaphore_wait(barrier, (nx - 1) + (ny - 1) + corners)

    design_copies = edge_copies(0)
    edge_start(design_copies)
    basis_steps = ((-1, 0), (0, -1), (-1, -1))
    basis_copies = [
        pltpu.make_async_remote_copy(
            src_ref=src, dst_ref=dst, send_sem=basis_send_sem.at[k], recv_sem=basis_recv_sem.at[k],
            device_id=(ix + dx, iy + dy), device_id_type=MESH,
        )
        for k, ((dx, dy), src, dst) in enumerate(
            zip(basis_steps, (send_x, send_y, send_c), (recv_x, recv_y, recv_c))
        )
    ]
    for (dx, dy), copy in zip(basis_steps, basis_copies):
        @pl.when(there(dx, dy))
        def _(copy=copy):
            copy.start()

    for x in range(size_x):
        fields[:, x * pitch : x * pitch + size_y, :] = (
            basis[:, x * size_y : (x + 1) * size_y, :] * free[x * size_y : (x + 1) * size_y][None]
        )

    wide_n, narrow_n = 24 * size_y, 24
    row = lax.broadcasted_iota(jnp.int32, (wide_n, narrow_n), 0)
    col = lax.broadcasted_iota(jnp.int32, (wide_n, narrow_n), 1)
    expand = (row // size_y == col).astype(jnp.float32).astype(jnp.bfloat16)
    row_t = lax.broadcasted_iota(jnp.int32, (narrow_n, wide_n), 0)
    col_t = lax.broadcasted_iota(jnp.int32, (narrow_n, wide_n), 1)
    expand_t = (col_t // size_y == row_t).astype(jnp.float32).astype(jnp.bfloat16)
    same = (
        lax.broadcasted_iota(jnp.int32, (wide_n, wide_n), 0) % size_y
        == lax.broadcasted_iota(jnp.int32, (wide_n, wide_n), 1) % size_y
    )

    def spread_matrix(piece):
        tall = jnp.dot(expand, piece, preferred_element_type=jnp.float32).astype(jnp.bfloat16)
        full = jnp.dot(tall, expand_t, preferred_element_type=jnp.float32)
        return jnp.where(same, full, 0.0).astype(jnp.bfloat16)

    for k, matrix in enumerate((stiffness, mass_matrix)):
        value = matrix[...]
        high = value.astype(jnp.bfloat16)
        low = (value - high.astype(jnp.float32)).astype(jnp.bfloat16)
        weights_hi[pl.ds(k * wide_n, wide_n), :] = spread_matrix(high)
        weights_lo[pl.ds(k * wide_n, wide_n), :] = spread_matrix(low)

    row_y = lax.broadcasted_iota(jnp.int32, (size_y, size_z), 0)
    grid_x, grid_y = nx * size_x, ny * size_y

    def inside(plane, oy):
        at_x = ix * size_x + plane - 2
        at_y = row_y + (iy * size_y + oy)
        ok = (at_y >= 0) & (at_y < grid_y) & (at_x >= 0) & (at_x < grid_x)
        return jnp.where(ok, 1.0, 0.0)

    for x, tile in enumerate(stencil(inside, size_x)):
        weight_sum[pl.ds(x * size_y, size_y), :] = tile

    edge_receive(design_copies, 0)
    assemble(design, 0)
    for x, tile in enumerate(stencil(wide_rows, size_x)):
        at = pl.ds(x * size_y, size_y)
        physical[at, :] = jnp.where(passive[at, :] == 1, 1.0, tile / weight_sum[at, :])

    for (dx, dy), copy, buffer in zip(basis_steps, basis_copies, (recv_x, recv_y, recv_c)):
        @pl.when(there(-dx, -dy))
        def _(copy=copy):
            copy.wait_recv()

        @pl.when(jnp.logical_not(there(-dx, -dy)))
        def _(buffer=buffer):
            buffer[...] = jnp.zeros(buffer.shape, jnp.float32)

    fields[:, size_x * pitch : size_x * pitch + size_y, :] = recv_x[...]
    for f in range(6 * pairs):
        fields[f, pl.ds(size_y, size_x, stride=pitch), :] = recv_y[f]
        fields[f, pl.ds(size_x * pitch + size_y, 1), :] = recv_c[pl.ds(f, 1), :]

    energy[...] = jnp.zeros((2 * cells, size_z), jnp.float32)

    def pair_step(pair, carry):
        def corner_tiles(member):
            tiles = {}
            for c in range(3):
                f = pair * 6 + member * 3 + c
                for x in range(size_x + 1):
                    for b in range(2):
                        tile = fields[f, x * pitch + b : x * pitch + b + size_y, :]
                        tiles[c, x, b, 0] = tile
                        tiles[c, x, b, 1] = z_shift(tile, 1)
            return tiles

        order = [(a, b, d, c) for a in range(2) for b in range(2) for d in range(2) for c in range(3)]
        adjoint = corner_tiles(1)
        operand = jnp.concatenate(
            [
                jnp.concatenate([adjoint[c, x + a, b, d] for x in range(size_x)], axis=1)
                for a, b, d, c in order
            ],
            axis=0,
        )
        high = operand.astype(jnp.bfloat16)
        low = (operand - high.astype(jnp.float32)).astype(jnp.bfloat16)
        product = (
            jnp.dot(weights_hi[...], high, preferred_element_type=jnp.float32)
            + jnp.dot(weights_hi[...], low, preferred_element_type=jnp.float32)
            + jnp.dot(weights_lo[...], high, preferred_element_type=jnp.float32)
        )
        state = corner_tiles(0)
        for x in range(size_x):
            for k in range(2):
                total = energy[pl.ds((k * size_x + x) * size_y, size_y), :]
                for r, (a, b, d, c) in enumerate(order):
                    at = k * wide_n + r * size_y
                    total = total + state[c, x + a, b, d] * product[at : at + size_y, x * size_z : (x + 1) * size_z]
                energy[pl.ds((k * size_x + x) * size_y, size_y), :] = total
        return carry

    lax.fori_loop(0, pairs, pair_step, 0)

    solid = passive[...] == 1
    density = physical[...]
    raw = -(
        PENALTY_SCALE * density * density * energy[0:cells, :]
        - OMEGA_SQUARED * energy[cells : 2 * cells, :]
    )
    scaled[...] = jnp.where(solid, 0.0, raw) / weight_sum[...]

    pack_edges(scaled, 1)
    scaled_copies = edge_copies(1)
    edge_start(scaled_copies)
    edge_receive(scaled_copies, 1)
    assemble(scaled, 1)
    for x, tile in enumerate(stencil(wide_rows, size_x)):
        sensitivity[pl.ds(x * size_y, size_y), :] = tile

    value = design[...]
    gain = value * jnp.sqrt(jnp.maximum(-sensitivity[...], 0.0))
    floor_value = jnp.maximum(value - MOVE_LIMIT, 0.0)
    ceiling = jnp.minimum(value + MOVE_LIMIT, 1.0)

    def candidate(multiplier):
        trial = gain * (1.0 / jnp.sqrt(multiplier))
        return jnp.where(solid, 1.0, jnp.minimum(ceiling, jnp.maximum(floor_value, trial)))

    band = size_z // regions
    pick = (
        lax.broadcasted_iota(jnp.int32, (regions, size_z), 1) // band
        == lax.broadcasted_iota(jnp.int32, (regions, size_z), 0)
    ).astype(jnp.float32).astype(jnp.bfloat16)
    rest = jnp.broadcast_to(fraction[...], (8, regions))
    target = jnp.zeros((8, size_z), jnp.float32)
    for _ in range(3):
        piece = rest.astype(jnp.bfloat16)
        target = target + jnp.dot(piece, pick, preferred_element_type=jnp.float32)
        rest = rest - piece.astype(jnp.float32)
    target = target[0:1] * float(grid_x * grid_y * band)

    lane = lax.broadcasted_iota(jnp.int32, (8, size_z), 1)
    slot_row = lax.broadcasted_iota(jnp.int32, (8, size_z), 0)
    low_end = jnp.full((1, size_z), 1e-4, jnp.float32)
    high_end = jnp.full((1, size_z), 1e4, jnp.float32)
    pending = []

    def line_sum(part, buffer, round_index, count, me, target_of, send_sem, recv_sem):
        buffer[round_index, pl.ds(me, 1)] = part[None]
        copies = []
        for step in range(1, count):
            copy = pltpu.make_async_remote_copy(
                src_ref=buffer.at[round_index, me],
                dst_ref=buffer.at[round_index, me],
                send_sem=send_sem.at[round_index, step],
                recv_sem=recv_sem.at[round_index, step],
                device_id=target_of(lax.rem(me + step, count)),
                device_id_type=MESH,
            )
            copy.start()
            copies.append(copy)
        for copy in copies:
            copy.wait_recv()
        pending.extend(copies)
        return functools.reduce(lambda a, b: a + b, [buffer[round_index, k] for k in range(count)])

    for round_index in range(ROUNDS):
        nodes = [(low_end, high_end)]
        middles = []
        for level in range(LEVELS):
            following = []
            for node_low, node_high in nodes:
                middle = jnp.sqrt(node_low * node_high)
                middles.append(middle)
                following += [(node_low, middle), (middle, node_high)]
            nodes = following
        volumes = jnp.zeros((8, size_z), jnp.float32)
        for k, middle in enumerate(middles):
            trial = candidate(middle).reshape(size_x, size_y, size_z)
            column = jnp.sum(jnp.sum(trial, axis=0), axis=0, keepdims=True)
            volumes = jnp.where(slot_row == k, column, volumes)
        volumes = line_sum(
            volumes, gather_y, round_index, ny, iy, lambda at: (ix, at), gy_send_sem, gy_recv_sem
        )
        volumes = line_sum(
            volumes, gather_x, round_index, nx, ix, lambda at: (at, iy), gx_send_sem, gx_recv_sem
        )
        paired = volumes
        reach = 1
        while reach < band:
            other = jnp.where(
                (lane // reach) % 2 == 0,
                pltpu.roll(paired, size_z - reach, 1),
                pltpu.roll(paired, reach, 1),
            )
            paired = paired + other
            reach *= 2
        heavier = [paired[k : k + 1] > target for k in range(len(middles))]
        options = [(h, m) for h, m in zip(heavier, middles)]

        def descend(index, level, low, high):
            over, middle = options[index]
            if level == LEVELS - 1:
                return jnp.where(over, middle, low), jnp.where(over, high, middle)
            left = descend(2 * index + 1, level + 1, low, middle)
            right = descend(2 * index + 2, level + 1, middle, high)
            return jnp.where(over, right[0], left[0]), jnp.where(over, right[1], left[1])

        low_end, high_end = descend(0, 0, low_end, high_end)

    design_next[...] = candidate(jnp.sqrt(low_end * high_end))

    edge_finish(design_copies)
    edge_finish(scaled_copies)
    for (dx, dy), copy in zip(basis_steps, basis_copies):
        @pl.when(there(dx, dy))
        def _(copy=copy):
            copy.wait_send()
    for copy in pending:
        copy.wait_send()


def shards(nx, ny, design, passive, basis_pairs, supports, stiffness, mass_matrix, volume_fraction):
    size_x, size_y, size_z = design.shape
    pairs = basis_pairs.shape[0]
    regions = volume_fraction.shape[0]
    cells = size_x * size_y
    fields_n = 6 * pairs
    flat = (cells, size_z)
    vmem = pl.BlockSpec(memory_space=pltpu.VMEM)
    f32, bf16 = jnp.float32, jnp.bfloat16
    dma = pltpu.SemaphoreType.DMA
    outs = pl.pallas_call(
        functools.partial(kernel, nx, ny, size_x, size_y, size_z, pairs, regions),
        out_shape=(jax.ShapeDtypeStruct(flat, f32), jax.ShapeDtypeStruct(flat, f32)),
        in_specs=[vmem] * 7,
        out_specs=(vmem, vmem),
        scratch_shapes=[
            pltpu.VMEM((fields_n, (size_x + 1) * 2 * size_y, size_z), f32),
            pltpu.VMEM((fields_n, size_y, size_z), f32),
            pltpu.VMEM((fields_n, size_x, size_z), f32),
            pltpu.VMEM((fields_n, size_z), f32),
            pltpu.VMEM((fields_n, size_y, size_z), f32),
            pltpu.VMEM((fields_n, size_x, size_z), f32),
            pltpu.VMEM((fields_n, size_z), f32),
            pltpu.VMEM((2, 4, 2, size_x, size_z), f32),
            pltpu.VMEM((2, 8, 2, size_y, size_z), f32),
            pltpu.VMEM(((size_x + 4) * 3 * size_y, size_z), f32),
            pltpu.VMEM(flat, f32),
            pltpu.VMEM((48 * size_y, 24 * size_y), bf16),
            pltpu.VMEM((48 * size_y, 24 * size_y), bf16),
            pltpu.VMEM(flat, f32),
            pltpu.VMEM(flat, f32),
            pltpu.VMEM((2 * cells, size_z), f32),
            pltpu.VMEM((ROUNDS, ny, 8, size_z), f32),
            pltpu.VMEM((ROUNDS, nx, 8, size_z), f32),
            dma((3,)),
            dma((3,)),
            dma((2, 8)),
            dma((2, 8)),
            dma((ROUNDS, ny)),
            dma((ROUNDS, ny)),
            dma((ROUNDS, nx)),
            dma((ROUNDS, nx)),
        ],
        compiler_params=pltpu.CompilerParams(
            collective_id=0, has_side_effects=True, vmem_limit_bytes=48 * 1024 * 1024
        ),
        name="sensitivity_update",
    )(
        design.reshape(flat),
        passive.reshape(flat),
        basis_pairs.reshape(fields_n, cells, size_z),
        supports.reshape(flat),
        stiffness,
        mass_matrix,
        volume_fraction.reshape(1, regions),
    )
    return tuple(out.reshape(design.shape) for out in outs)


def solution(mesh):
    placed = (
        P("gx", "gy", None),
        P("gx", "gy", None),
        P(None, None, None, "gx", "gy", None),
        P("gx", "gy", None),
        P(),
        P(),
        P(),
    )
    return jax.shard_map(
        functools.partial(shards, mesh.shape["gx"], mesh.shape["gy"]),
        mesh=mesh,
        in_specs=placed,
        out_specs=(P("gx", "gy", None), P("gx", "gy", None)),
        check_vma=False,
    )
```

```python
import functools
import math

import jax
import jax.numpy as jnp
import numpy as np
from jax import lax
from jax.experimental import pallas as pl
from jax.experimental.pallas import tpu as pltpu
from jax.sharding import PartitionSpec as P

PENALTY_SCALE = 3.0 * (1.0 - 0.001)
OMEGA_SQUARED = 0.5
MOVE_LIMIT = 0.2
BISECT = 6
TRIALS = 2**BISECT
MESH = pl.DeviceIdType.MESH
AROUND = ((-1, 0), (1, 0), (0, -1), (0, 1), (-1, -1), (-1, 1), (1, -1), (1, 1))


def tree_ends():
    ends = [np.float32(1e-4), np.float32(1e4)]
    for _ in range(BISECT):
        inner = [np.sqrt(p * q) for p, q in zip(ends, ends[1:])]
        ends = [ends[0]] + [e for pair in zip(inner, ends[1:]) for e in pair]
    return ends


ENDS = tree_ends()
INVERSE_MIDDLES = [float(np.float32(1.0) / np.sqrt(e)) for e in ENDS[1:-1]]
INVERSE_LEAVES = [
    float(np.float32(1.0) / np.sqrt(np.sqrt(p * q))) for p, q in zip(ENDS, ENDS[1:])
]


def opposite(slot):
    dx, dy = AROUND[slot]
    return AROUND.index((-dx, -dy))


def z_shift(value, step):
    axis = value.ndim - 1
    size = value.shape[axis]
    lane = lax.broadcasted_iota(jnp.int32, value.shape, axis)
    moved = pltpu.roll(value, (-step) % size, axis)
    keep = lane < size - step if step > 0 else lane >= -step
    return jnp.where(keep, moved, 0.0)


def stencil(rows_at, size_x):
    spread = [[None] * (size_x + 4) for _ in range(3)]
    for plane in range(size_x + 4):
        tiles = [rows_at(plane, oy) for oy in range(-2, 3)]
        folded_y = (tiles[2], tiles[1] + tiles[3], tiles[0] + tiles[4])
        parts = [[], [], []]
        for cy, tile in enumerate(folded_y):
            folded_z = (
                tile,
                z_shift(tile, 1) + z_shift(tile, -1),
                z_shift(tile, 2) + z_shift(tile, -2),
            )
            for cz, entry in enumerate(folded_z):
                for cx in range(3):
                    weight = 3.0 - math.sqrt(cx * cx + cy * cy + cz * cz)
                    if weight > 0.0:
                        parts[cx].append(weight * entry)
        for cx in range(3):
            spread[cx][plane] = functools.reduce(lambda a, b: a + b, parts[cx])
    return [
        spread[0][i + 2]
        + (spread[1][i + 1] + spread[1][i + 3])
        + (spread[2][i] + spread[2][i + 4])
        for i in range(size_x)
    ]


def kernel(
    nx, ny, size_x, size_y, size_z, pairs, regions,
    design_hbm, passive_hbm, basis_hbm, supports_hbm, stiffness_hbm, mass_hbm, fraction_hbm,
    sensitivity, design_next,
    design, passive, basis, supports, stiffness, mass_matrix, fraction,
    fields, send_x, send_y, send_c, recv_x, recv_y, recv_c,
    edge_send, edge_recv, wide, scaled, weights_hi, weights_lo, weight_sum, physical, energy,
    share_send, share_recv, gather_x, gather_y, leaf_table,
    load_sem,
    basis_send_sem, basis_recv_sem, halo_send_sem, halo_recv_sem,
    share_send_sem, share_recv_sem, gx_send_sem, gx_recv_sem, gy_send_sem, gy_recv_sem,
):
    ix, iy = lax.axis_index("gx"), lax.axis_index("gy")
    pitch = 2 * size_y
    cells = size_x * size_y

    def there(dx, dy):
        return (
            (ix + dx >= 0) & (ix + dx < nx) & (iy + dy >= 0) & (iy + dy < ny)
        )

    barrier = pltpu.get_barrier_semaphore()
    for step in range(1, ny):
        pl.semaphore_signal(barrier, inc=1, device_id=(ix, lax.rem(iy + step, ny)), device_id_type=MESH)
    for step in range(1, nx):
        pl.semaphore_signal(barrier, inc=1, device_id=(lax.rem(ix + step, nx), iy), device_id_type=MESH)
    for dx, dy in AROUND[4:]:
        @pl.when(there(dx, dy))
        def _(dx=dx, dy=dy):
            pl.semaphore_signal(barrier, inc=1, device_id=(ix + dx, iy + dy), device_id_type=MESH)
    corners = sum(there(dx, dy).astype(jnp.int32) for dx, dy in AROUND[4:])

    loads = [
        pltpu.make_async_copy(src, dst, load_sem.at[k])
        for k, (src, dst) in enumerate((
            (supports_hbm, supports), (basis_hbm, basis), (design_hbm, design), (passive_hbm, passive),
            (stiffness_hbm, stiffness), (mass_hbm, mass_matrix), (fraction_hbm, fraction),
        ))
    ]
    for load in loads:
        load.start()
    for load in loads:
        load.wait()

    free = 1.0 - supports[...].astype(jnp.float32)
    send_x[...] = basis[:, 0:size_y, :] * free[0:size_y][None]
    free_y = 1.0 - supports[pl.ds(0, size_x, stride=size_y), :].astype(jnp.float32)
    for f in range(6 * pairs):
        rows = basis[f, pl.ds(0, size_x, stride=size_y), :] * free_y
        send_y[f] = rows
        send_c[pl.ds(f, 1), :] = rows[0:1]

    def pack_edges(source, which):
        for x in range(2):
            edge_send[which, 2, x] = source[pl.ds(x * size_y, size_y), :]
            edge_send[which, 3, x] = source[pl.ds((size_x - 2 + x) * size_y, size_y), :]
        for y in range(2):
            edge_send[which, 0, y] = source[pl.ds(y, size_x, stride=size_y), :]
            edge_send[which, 1, y] = source[pl.ds(size_y - 2 + y, size_x, stride=size_y), :]

    def edge_copies(which):
        copies = []
        for slot, (dx, dy) in enumerate(AROUND):
            if dy == 0:
                src = edge_send.at[which, 2 if dx < 0 else 3]
            else:
                src = edge_send.at[which, 0 if dy < 0 else 1]
            copies.append(pltpu.make_async_remote_copy(
                src_ref=src,
                dst_ref=edge_recv.at[which, opposite(slot)],
                send_sem=halo_send_sem.at[which, slot],
                recv_sem=halo_recv_sem.at[which, opposite(slot)],
                device_id=(ix + dx, iy + dy),
                device_id_type=MESH,
            ))
        return copies

    def edge_start(copies):
        for (dx, dy), copy in zip(AROUND, copies):
            @pl.when(there(dx, dy))
            def _(copy=copy):
                copy.start()

    def edge_receive(copies, which):
        for slot, (dx, dy) in enumerate(AROUND):
            copy = copies[opposite(slot)]

            @pl.when(there(dx, dy))
            def _(copy=copy):
                copy.wait_recv()

            @pl.when(jnp.logical_not(there(dx, dy)))
            def _(slot=slot):
                edge_recv[which, slot] = jnp.zeros((2, size_y, size_z), jnp.float32)

    def edge_finish(copies):
        for (dx, dy), copy in zip(AROUND, copies):
            @pl.when(there(dx, dy))
            def _(copy=copy):
                copy.wait_send()

    span = 3 * size_y

    def assemble(source, which):
        for x in range(size_x):
            wide[pl.ds((x + 2) * span + size_y, size_y), :] = source[pl.ds(x * size_y, size_y), :]
        for x in range(2):
            wide[pl.ds(x * span + size_y, size_y), :] = edge_recv[which, 0, x]
            wide[pl.ds((size_x + 2 + x) * span + size_y, size_y), :] = edge_recv[which, 1, x]
        for y in range(2):
            low, high = size_y - 2 + y, 2 * size_y + y
            wide[pl.ds(2 * span + low, size_x, stride=span), :] = edge_recv[which, 2, y]
            wide[pl.ds(2 * span + high, size_x, stride=span), :] = edge_recv[which, 3, y]
            for x in range(2):
                for slot, row in ((4, low), (5, high)):
                    wide[pl.ds(x * span + row, 1), :] = edge_recv[which, slot, y, size_x - 2 + x : size_x - 1 + x, :]
                for slot, row in ((6, low), (7, high)):
                    wide[pl.ds((size_x + 2 + x) * span + row, 1), :] = edge_recv[which, slot, y, x : x + 1, :]

    def wide_rows(plane, oy):
        return wide[pl.ds(plane * span + size_y + oy, size_y), :]

    pack_edges(design, 0)

    pl.semaphore_wait(barrier, (nx - 1) + (ny - 1) + corners)

    design_copies = edge_copies(0)
    edge_start(design_copies)
    basis_steps = ((-1, 0), (0, -1), (-1, -1))
    basis_copies = [
        pltpu.make_async_remote_copy(
            src_ref=src, dst_ref=dst, send_sem=basis_send_sem.at[k], recv_sem=basis_recv_sem.at[k],
            device_id=(ix + dx, iy + dy), device_id_type=MESH,
        )
        for k, ((dx, dy), src, dst) in enumerate(
            zip(basis_steps, (send_x, send_y, send_c), (recv_x, recv_y, recv_c))
        )
    ]
    for (dx, dy), copy in zip(basis_steps, basis_copies):
        @pl.when(there(dx, dy))
        def _(copy=copy):
            copy.start()

    for x in range(size_x):
        fields[:, x * pitch : x * pitch + size_y, :] = (
            basis[:, x * size_y : (x + 1) * size_y, :] * free[x * size_y : (x + 1) * size_y][None]
        )

    wide_n, narrow_n = 24 * size_y, 24
    row = lax.broadcasted_iota(jnp.int32, (wide_n, narrow_n), 0)
    col = lax.broadcasted_iota(jnp.int32, (wide_n, narrow_n), 1)
    expand = (row // size_y == col).astype(jnp.float32).astype(jnp.bfloat16)
    row_t = lax.broadcasted_iota(jnp.int32, (narrow_n, wide_n), 0)
    col_t = lax.broadcasted_iota(jnp.int32, (narrow_n, wide_n), 1)
    expand_t = (col_t // size_y == row_t).astype(jnp.float32).astype(jnp.bfloat16)
    same = (
        lax.broadcasted_iota(jnp.int32, (wide_n, wide_n), 0) % size_y
        == lax.broadcasted_iota(jnp.int32, (wide_n, wide_n), 1) % size_y
    )

    def spread_matrix(piece):
        tall = jnp.dot(expand, piece, preferred_element_type=jnp.float32).astype(jnp.bfloat16)
        full = jnp.dot(tall, expand_t, preferred_element_type=jnp.float32)
        return jnp.where(same, full, 0.0).astype(jnp.bfloat16)

    for k, matrix in enumerate((stiffness, mass_matrix)):
        value = matrix[...]
        high = value.astype(jnp.bfloat16)
        low = (value - high.astype(jnp.float32)).astype(jnp.bfloat16)
        weights_hi[pl.ds(k * wide_n, wide_n), :] = spread_matrix(high)
        weights_lo[pl.ds(k * wide_n, wide_n), :] = spread_matrix(low)

    row_y = lax.broadcasted_iota(jnp.int32, (size_y, size_z), 0)
    grid_x, grid_y = nx * size_x, ny * size_y

    def inside(plane, oy):
        at_x = ix * size_x + plane - 2
        at_y = row_y + (iy * size_y + oy)
        ok = (at_y >= 0) & (at_y < grid_y) & (at_x >= 0) & (at_x < grid_x)
        return jnp.where(ok, 1.0, 0.0)

    for x, tile in enumerate(stencil(inside, size_x)):
        weight_sum[pl.ds(x * size_y, size_y), :] = tile

    band = size_z // regions
    width, group_rows = size_z // ny, TRIALS // ny
    lane = lax.broadcasted_iota(jnp.int32, (group_rows, size_z), 1)
    lane8 = lax.broadcasted_iota(jnp.int32, (8, size_z), 1)
    slot_row = lax.broadcasted_iota(jnp.int32, (8, size_z), 0)
    group = lane // width
    pick = (
        lax.broadcasted_iota(jnp.int32, (regions, size_z), 1) // band
        == lax.broadcasted_iota(jnp.int32, (regions, size_z), 0)
    ).astype(jnp.float32).astype(jnp.bfloat16)
    rest = jnp.broadcast_to(fraction[...], (8, regions))
    target = jnp.zeros((8, size_z), jnp.float32)
    for _ in range(3):
        piece = rest.astype(jnp.bfloat16)
        target = target + jnp.dot(piece, pick, preferred_element_type=jnp.float32)
        rest = rest - piece.astype(jnp.float32)
    target = target * float(grid_x * grid_y * band)
    own_target = jnp.where(lane8 // width == iy, target, 0.0)
    reach = width
    while reach < size_z:
        own_target = own_target + pltpu.roll(own_target, reach, 1)
        reach *= 2
    for r in range(group_rows):
        line = jnp.full((1, size_z), INVERSE_LEAVES[0], jnp.float32)
        for g in range(ny):
            j = min(g * group_rows + r + 1, TRIALS - 1)
            line = jnp.where(lane8[0:1] // width == g, INVERSE_LEAVES[j], line)
        leaf_table[pl.ds(r, 1), :] = line

    edge_receive(design_copies, 0)
    assemble(design, 0)
    for x, tile in enumerate(stencil(wide_rows, size_x)):
        at = pl.ds(x * size_y, size_y)
        physical[at, :] = jnp.where(passive[at, :] == 1, 1.0, tile / weight_sum[at, :])

    for (dx, dy), copy, buffer in zip(basis_steps, basis_copies, (recv_x, recv_y, recv_c)):
        @pl.when(there(-dx, -dy))
        def _(copy=copy):
            copy.wait_recv()

        @pl.when(jnp.logical_not(there(-dx, -dy)))
        def _(buffer=buffer):
            buffer[...] = jnp.zeros(buffer.shape, jnp.float32)

    fields[:, size_x * pitch : size_x * pitch + size_y, :] = recv_x[...]
    for f in range(6 * pairs):
        fields[f, pl.ds(size_y, size_x, stride=pitch), :] = recv_y[f]
        fields[f, pl.ds(size_x * pitch + size_y, 1), :] = recv_c[pl.ds(f, 1), :]

    energy[...] = jnp.zeros((2 * cells, size_z), jnp.float32)

    def pair_step(pair, carry):
        def corner_tiles(member):
            tiles = {}
            for c in range(3):
                f = pair * 6 + member * 3 + c
                for x in range(size_x + 1):
                    for b in range(2):
                        tile = fields[f, x * pitch + b : x * pitch + b + size_y, :]
                        tiles[c, x, b, 0] = tile
                        tiles[c, x, b, 1] = z_shift(tile, 1)
            return tiles

        order = [(a, b, d, c) for a in range(2) for b in range(2) for d in range(2) for c in range(3)]
        adjoint = corner_tiles(1)
        operand = jnp.concatenate(
            [
                jnp.concatenate([adjoint[c, x + a, b, d] for x in range(size_x)], axis=1)
                for a, b, d, c in order
            ],
            axis=0,
        )
        high = operand.astype(jnp.bfloat16)
        low = (operand - high.astype(jnp.float32)).astype(jnp.bfloat16)
        product = (
            jnp.dot(weights_hi[...], high, preferred_element_type=jnp.float32)
            + jnp.dot(weights_hi[...], low, preferred_element_type=jnp.float32)
            + jnp.dot(weights_lo[...], high, preferred_element_type=jnp.float32)
        )
        state = corner_tiles(0)
        for x in range(size_x):
            for k in range(2):
                total = energy[pl.ds((k * size_x + x) * size_y, size_y), :]
                for r, (a, b, d, c) in enumerate(order):
                    at = k * wide_n + r * size_y
                    total = total + state[c, x + a, b, d] * product[at : at + size_y, x * size_z : (x + 1) * size_z]
                energy[pl.ds((k * size_x + x) * size_y, size_y), :] = total
        return carry

    lax.fori_loop(0, pairs, pair_step, 0)

    solid = passive[...] == 1
    density = physical[...]
    raw = -(
        PENALTY_SCALE * density * density * energy[0:cells, :]
        - OMEGA_SQUARED * energy[cells : 2 * cells, :]
    )
    scaled[...] = jnp.where(solid, 0.0, raw) / weight_sum[...]

    pack_edges(scaled, 1)
    scaled_copies = edge_copies(1)
    edge_start(scaled_copies)
    edge_receive(scaled_copies, 1)
    assemble(scaled, 1)
    for x, tile in enumerate(stencil(wide_rows, size_x)):
        sensitivity[pl.ds(x * size_y, size_y), :] = tile

    value = design[...]
    gain = value * jnp.sqrt(jnp.maximum(-sensitivity[...], 0.0))
    floor_value = jnp.where(solid, 1.0, jnp.maximum(value - MOVE_LIMIT, 0.0))
    ceiling = jnp.where(solid, 1.0, jnp.minimum(value + MOVE_LIMIT, 1.0))

    def candidate(inverse_root):
        return jnp.minimum(ceiling, jnp.maximum(floor_value, gain * inverse_root))

    def total_over_x(j):
        trial = candidate(INVERSE_MIDDLES[j])
        return functools.reduce(
            lambda p, q: p + q, [trial[x * size_y : (x + 1) * size_y] for x in range(size_x)]
        )

    volumes = []
    for first in range(0, TRIALS, 8):
        tiles = [
            total_over_x(j) if j < TRIALS - 1 else jnp.zeros((8, size_z), jnp.float32)
            for j in range(first, first + 8)
        ]
        reach = 4
        while reach:
            lower = (slot_row & reach) == 0
            tiles = [
                jnp.where(lower, p, q)
                + jnp.where(lower, pltpu.roll(p, 8 - reach, 0), pltpu.roll(q, reach, 0))
                for p, q in zip(tiles[:reach], tiles[reach:])
            ]
            reach //= 2
        volumes.append(tiles[0])
    volumes = jnp.concatenate(volumes, axis=0)

    for q in range(ny):
        packed = jnp.zeros((group_rows, size_z), jnp.float32)
        for g in range(ny):
            part = volumes[g * group_rows : (g + 1) * group_rows]
            turn = (width * (g - q)) % size_z
            if turn:
                part = pltpu.roll(part, turn, 1)
            packed = jnp.where(group == g, part, packed)
        share_send[q] = packed
    share_recv[pl.ds(iy, 1)] = share_send[pl.ds(iy, 1)]
    pending = []

    def along(count, me, place, source, buffer, send_sem, recv_sem):
        copies = []
        for step in range(1, count):
            peer = lax.rem(me + step, count)
            copy = pltpu.make_async_remote_copy(
                src_ref=source(peer),
                dst_ref=buffer.at[me],
                send_sem=send_sem.at[step],
                recv_sem=recv_sem.at[step],
                device_id=place(peer),
                device_id_type=MESH,
            )
            copy.start()
            copies.append(copy)
        for copy in copies:
            copy.wait_recv()
        pending.extend(copies)

    along(ny, iy, lambda at: (ix, at), lambda at: share_send.at[at], share_recv, share_send_sem, share_recv_sem)
    share = functools.reduce(lambda p, q: p + q, [share_recv[k] for k in range(ny)])
    gather_x[pl.ds(ix, 1)] = share[None]
    along(nx, ix, lambda at: (at, iy), lambda at: gather_x.at[ix], gather_x, gx_send_sem, gx_recv_sem)
    share = functools.reduce(lambda p, q: p + q, [gather_x[k] for k in range(nx)])

    reach = 1
    while reach < band:
        share = share + jnp.where(
            (lane // reach) % 2 == 0,
            pltpu.roll(share, size_z - reach, 1),
            pltpu.roll(share, reach, 1),
        )
        reach *= 2
    chosen = jnp.where(share > own_target[0:1], leaf_table[...], INVERSE_LEAVES[0])
    chosen = jnp.min(chosen, axis=0, keepdims=True)
    reach = width
    while reach < size_z:
        chosen = jnp.minimum(chosen, pltpu.roll(chosen, reach, 1))
        reach *= 2
    gather_y[pl.ds(iy, 1)] = jnp.broadcast_to(chosen, (8, size_z))[None]
    along(ny, iy, lambda at: (ix, at), lambda at: gather_y.at[iy], gather_y, gy_send_sem, gy_recv_sem)
    multiplier = gather_y[0]
    for q in range(1, ny):
        multiplier = jnp.where(lane8 // width == q, gather_y[q], multiplier)
    design_next[...] = candidate(multiplier[0:1])

    edge_finish(design_copies)
    edge_finish(scaled_copies)
    for (dx, dy), copy in zip(basis_steps, basis_copies):
        @pl.when(there(dx, dy))
        def _(copy=copy):
            copy.wait_send()
    for copy in pending:
        copy.wait_send()


def shards(nx, ny, design, passive, basis_pairs, supports, stiffness, mass_matrix, volume_fraction):
    size_x, size_y, size_z = design.shape
    pairs = basis_pairs.shape[0]
    regions = volume_fraction.shape[0]
    cells = size_x * size_y
    fields_n = 6 * pairs
    flat = (cells, size_z)
    vmem = pl.BlockSpec(memory_space=pltpu.VMEM)
    f32, bf16 = jnp.float32, jnp.bfloat16
    dma = pltpu.SemaphoreType.DMA
    outs = pl.pallas_call(
        functools.partial(kernel, nx, ny, size_x, size_y, size_z, pairs, regions),
        out_shape=(jax.ShapeDtypeStruct(flat, f32), jax.ShapeDtypeStruct(flat, f32)),
        in_specs=[pl.BlockSpec(memory_space=pltpu.HBM)] * 7,
        out_specs=(vmem, vmem),
        scratch_shapes=[
            pltpu.VMEM(flat, f32),
            pltpu.VMEM(flat, jnp.int32),
            pltpu.VMEM((fields_n, cells, size_z), f32),
            pltpu.VMEM(flat, jnp.int32),
            pltpu.VMEM(stiffness.shape, f32),
            pltpu.VMEM(mass_matrix.shape, f32),
            pltpu.VMEM((1, regions), f32),
            pltpu.VMEM((fields_n, (size_x + 1) * 2 * size_y, size_z), f32),
            pltpu.VMEM((fields_n, size_y, size_z), f32),
            pltpu.VMEM((fields_n, size_x, size_z), f32),
            pltpu.VMEM((fields_n, size_z), f32),
            pltpu.VMEM((fields_n, size_y, size_z), f32),
            pltpu.VMEM((fields_n, size_x, size_z), f32),
            pltpu.VMEM((fields_n, size_z), f32),
            pltpu.VMEM((2, 4, 2, size_x, size_z), f32),
            pltpu.VMEM((2, 8, 2, size_y, size_z), f32),
            pltpu.VMEM(((size_x + 4) * 3 * size_y, size_z), f32),
            pltpu.VMEM(flat, f32),
            pltpu.VMEM((48 * size_y, 24 * size_y), bf16),
            pltpu.VMEM((48 * size_y, 24 * size_y), bf16),
            pltpu.VMEM(flat, f32),
            pltpu.VMEM(flat, f32),
            pltpu.VMEM((2 * cells, size_z), f32),
            pltpu.VMEM((ny, TRIALS // ny, size_z), f32),
            pltpu.VMEM((ny, TRIALS // ny, size_z), f32),
            pltpu.VMEM((nx, TRIALS // ny, size_z), f32),
            pltpu.VMEM((ny, 8, size_z), f32),
            pltpu.VMEM((TRIALS // ny, size_z), f32),
            dma((7,)),
            dma((3,)),
            dma((3,)),
            dma((2, 8)),
            dma((2, 8)),
            dma((ny,)),
            dma((ny,)),
            dma((nx,)),
            dma((nx,)),
            dma((ny,)),
            dma((ny,)),
        ],
        compiler_params=pltpu.CompilerParams(
            collective_id=0, has_side_effects=True, vmem_limit_bytes=48 * 1024 * 1024
        ),
        name="sensitivity_update",
    )(
        design.reshape(flat),
        passive.reshape(flat),
        basis_pairs.reshape(fields_n, cells, size_z),
        supports.reshape(flat),
        stiffness,
        mass_matrix,
        volume_fraction.reshape(1, regions),
    )
    return tuple(out.reshape(design.shape) for out in outs)


def solution(mesh):
    placed = (
        P("gx", "gy", None),
        P("gx", "gy", None),
        P(None, None, None, "gx", "gy", None),
        P("gx", "gy", None),
        P(),
        P(),
        P(),
    )
    return jax.shard_map(
        functools.partial(shards, mesh.shape["gx"], mesh.shape["gy"]),
        mesh=mesh,
        in_specs=placed,
        out_specs=(P("gx", "gy", None), P("gx", "gy", None)),
        check_vma=False,
    )
```

```python
import functools
import math

import jax
import jax.numpy as jnp
import numpy as np
from jax import lax
from jax.experimental import pallas as pl
from jax.experimental.pallas import tpu as pltpu
from jax.sharding import PartitionSpec as P

PENALTY_SCALE = 3.0 * (1.0 - 0.001)
OMEGA_SQUARED = 0.5
MOVE_LIMIT = 0.2
BISECT = 6
TRIALS = 2**BISECT
MESH = pl.DeviceIdType.MESH
AROUND = ((-1, 0), (1, 0), (0, -1), (0, 1), (-1, -1), (-1, 1), (1, -1), (1, 1))


def tree_ends():
    ends = [np.float32(1e-4), np.float32(1e4)]
    for _ in range(BISECT):
        inner = [np.sqrt(p * q) for p, q in zip(ends, ends[1:])]
        ends = [ends[0]] + [e for pair in zip(inner, ends[1:]) for e in pair]
    return ends


ENDS = tree_ends()
INVERSE_MIDDLES = [float(np.float32(1.0) / np.sqrt(e)) for e in ENDS[1:-1]]
INVERSE_LEAVES = [
    float(np.float32(1.0) / np.sqrt(np.sqrt(p * q))) for p, q in zip(ENDS, ENDS[1:])
]


def opposite(slot):
    dx, dy = AROUND[slot]
    return AROUND.index((-dx, -dy))


def z_shift(value, step):
    axis = value.ndim - 1
    size = value.shape[axis]
    lane = lax.broadcasted_iota(jnp.int32, value.shape, axis)
    moved = pltpu.roll(value, (-step) % size, axis)
    keep = lane < size - step if step > 0 else lane >= -step
    return jnp.where(keep, moved, 0.0)


def stencil(rows_at, size_x):
    spread = [[None] * (size_x + 4) for _ in range(3)]
    for plane in range(size_x + 4):
        tiles = [rows_at(plane, oy) for oy in range(-2, 3)]
        folded_y = (tiles[2], tiles[1] + tiles[3], tiles[0] + tiles[4])
        parts = [[], [], []]
        for cy, tile in enumerate(folded_y):
            folded_z = (
                tile,
                z_shift(tile, 1) + z_shift(tile, -1),
                z_shift(tile, 2) + z_shift(tile, -2),
            )
            for cz, entry in enumerate(folded_z):
                for cx in range(3):
                    weight = 3.0 - math.sqrt(cx * cx + cy * cy + cz * cz)
                    if weight > 0.0:
                        parts[cx].append(weight * entry)
        for cx in range(3):
            spread[cx][plane] = functools.reduce(lambda a, b: a + b, parts[cx])
    return [
        spread[0][i + 2]
        + (spread[1][i + 1] + spread[1][i + 3])
        + (spread[2][i] + spread[2][i + 4])
        for i in range(size_x)
    ]


def kernel(
    nx, ny, size_x, size_y, size_z, pairs, regions,
    design_hbm, passive_hbm, basis_hbm, supports_hbm, stiffness_hbm, mass_hbm, fraction_hbm,
    benefit_hbm, chosen_out,
    benefit, design, passive, basis, supports, stiffness, mass_matrix, fraction,
    fields, send_x, send_y, send_c, recv_x, recv_y, recv_c,
    edge_send, edge_recv, wide, scaled, weights_hi, weights_lo, weight_sum, physical, energy,
    share_send, share_recv, gather_x, gather_y, leaf_table,
    load_sem, out_sem,
    basis_send_sem, basis_recv_sem, halo_send_sem, halo_recv_sem,
    share_send_sem, share_recv_sem, gx_send_sem, gx_recv_sem, gy_send_sem, gy_recv_sem,
):
    ix, iy = lax.axis_index("gx"), lax.axis_index("gy")
    pitch = 2 * size_y
    cells = size_x * size_y

    def there(dx, dy):
        return (
            (ix + dx >= 0) & (ix + dx < nx) & (iy + dy >= 0) & (iy + dy < ny)
        )

    barrier = pltpu.get_barrier_semaphore()
    for step in range(1, ny):
        pl.semaphore_signal(barrier, inc=1, device_id=(ix, lax.rem(iy + step, ny)), device_id_type=MESH)
    for step in range(1, nx):
        pl.semaphore_signal(barrier, inc=1, device_id=(lax.rem(ix + step, nx), iy), device_id_type=MESH)
    for dx, dy in AROUND[4:]:
        @pl.when(there(dx, dy))
        def _(dx=dx, dy=dy):
            pl.semaphore_signal(barrier, inc=1, device_id=(ix + dx, iy + dy), device_id_type=MESH)
    corners = sum(there(dx, dy).astype(jnp.int32) for dx, dy in AROUND[4:])

    loads = [
        pltpu.make_async_copy(src, dst, load_sem.at[k])
        for k, (src, dst) in enumerate((
            (supports_hbm, supports), (basis_hbm, basis), (design_hbm, design), (passive_hbm, passive),
            (stiffness_hbm, stiffness), (mass_hbm, mass_matrix), (fraction_hbm, fraction),
        ))
    ]
    for load in loads:
        load.start()
    for load in loads:
        load.wait()

    free = 1.0 - supports[...].astype(jnp.float32)
    send_x[...] = basis[:, 0:size_y, :] * free[0:size_y][None]
    free_y = 1.0 - supports[pl.ds(0, size_x, stride=size_y), :].astype(jnp.float32)
    for f in range(6 * pairs):
        rows = basis[f, pl.ds(0, size_x, stride=size_y), :] * free_y
        send_y[f] = rows
        send_c[f // 6, pl.ds(f % 6, 1), :] = rows[0:1]

    def pack_edges(source, which):
        for x in range(2):
            edge_send[which, 2, x] = source[pl.ds(x * size_y, size_y), :]
            edge_send[which, 3, x] = source[pl.ds((size_x - 2 + x) * size_y, size_y), :]
        for y in range(2):
            edge_send[which, 0, y] = source[pl.ds(y, size_x, stride=size_y), :]
            edge_send[which, 1, y] = source[pl.ds(size_y - 2 + y, size_x, stride=size_y), :]

    def edge_copies(which):
        copies = []
        for slot, (dx, dy) in enumerate(AROUND):
            if dy == 0:
                src = edge_send.at[which, 2 if dx < 0 else 3]
            else:
                src = edge_send.at[which, 0 if dy < 0 else 1]
            copies.append(pltpu.make_async_remote_copy(
                src_ref=src,
                dst_ref=edge_recv.at[which, opposite(slot)],
                send_sem=halo_send_sem.at[which, slot],
                recv_sem=halo_recv_sem.at[which, opposite(slot)],
                device_id=(ix + dx, iy + dy),
                device_id_type=MESH,
            ))
        return copies

    def edge_start(copies):
        for (dx, dy), copy in zip(AROUND, copies):
            @pl.when(there(dx, dy))
            def _(copy=copy):
                copy.start()

    def edge_receive(copies, which):
        for slot, (dx, dy) in enumerate(AROUND):
            copy = copies[opposite(slot)]

            @pl.when(there(dx, dy))
            def _(copy=copy):
                copy.wait_recv()

            @pl.when(jnp.logical_not(there(dx, dy)))
            def _(slot=slot):
                edge_recv[which, slot] = jnp.zeros((2, size_y, size_z), jnp.float32)

    def edge_finish(copies):
        for (dx, dy), copy in zip(AROUND, copies):
            @pl.when(there(dx, dy))
            def _(copy=copy):
                copy.wait_send()

    span = 3 * size_y

    def assemble(source, which):
        for x in range(size_x):
            wide[pl.ds((x + 2) * span + size_y, size_y), :] = source[pl.ds(x * size_y, size_y), :]
        for x in range(2):
            wide[pl.ds(x * span + size_y, size_y), :] = edge_recv[which, 0, x]
            wide[pl.ds((size_x + 2 + x) * span + size_y, size_y), :] = edge_recv[which, 1, x]
        for y in range(2):
            low, high = size_y - 2 + y, 2 * size_y + y
            wide[pl.ds(2 * span + low, size_x, stride=span), :] = edge_recv[which, 2, y]
            wide[pl.ds(2 * span + high, size_x, stride=span), :] = edge_recv[which, 3, y]
            for x in range(2):
                for slot, row in ((4, low), (5, high)):
                    wide[pl.ds(x * span + row, 1), :] = edge_recv[which, slot, y, size_x - 2 + x : size_x - 1 + x, :]
                for slot, row in ((6, low), (7, high)):
                    wide[pl.ds((size_x + 2 + x) * span + row, 1), :] = edge_recv[which, slot, y, x : x + 1, :]

    def wide_rows(plane, oy):
        return wide[pl.ds(plane * span + size_y + oy, size_y), :]

    pack_edges(design, 0)

    grid_x, grid_y = nx * size_x, ny * size_y
    wide_n, narrow_n = 24 * size_y, 24
    bits_y = size_y.bit_length() - 1
    row = lax.broadcasted_iota(jnp.int32, (wide_n, narrow_n), 0)
    col = lax.broadcasted_iota(jnp.int32, (wide_n, narrow_n), 1)
    expand = (lax.shift_right_logical(row, bits_y) == col).astype(jnp.float32).astype(jnp.bfloat16)
    row_t = lax.broadcasted_iota(jnp.int32, (narrow_n, wide_n), 0)
    col_t = lax.broadcasted_iota(jnp.int32, (narrow_n, wide_n), 1)
    expand_t = (lax.shift_right_logical(col_t, bits_y) == row_t).astype(jnp.float32).astype(jnp.bfloat16)
    same = (
        lax.broadcasted_iota(jnp.int32, (wide_n, wide_n), 0) & (size_y - 1)
        == lax.broadcasted_iota(jnp.int32, (wide_n, wide_n), 1) & (size_y - 1)
    )

    def spread_matrix(piece):
        tall = jnp.dot(expand, piece, preferred_element_type=jnp.float32).astype(jnp.bfloat16)
        full = jnp.dot(tall, expand_t, preferred_element_type=jnp.float32)
        return jnp.where(same, full, 0.0).astype(jnp.bfloat16)

    for k, matrix in enumerate((stiffness, mass_matrix)):
        value = matrix[...]
        high = value.astype(jnp.bfloat16)
        low = (value - high.astype(jnp.float32)).astype(jnp.bfloat16)
        weights_hi[pl.ds(k * wide_n, wide_n), :] = spread_matrix(high)
        weights_lo[pl.ds(k * wide_n, wide_n), :] = spread_matrix(low)

    band = size_z // regions
    width, group_rows = size_z // ny, TRIALS // ny
    lane = lax.broadcasted_iota(jnp.int32, (group_rows, size_z), 1)
    lane8 = lax.broadcasted_iota(jnp.int32, (8, size_z), 1)
    slot_row = lax.broadcasted_iota(jnp.int32, (8, size_z), 0)
    group = lane // width
    pick = (
        lax.broadcasted_iota(jnp.int32, (regions, size_z), 1) // band
        == lax.broadcasted_iota(jnp.int32, (regions, size_z), 0)
    ).astype(jnp.float32).astype(jnp.bfloat16)
    rest = jnp.broadcast_to(fraction[...].reshape(1, regions), (8, regions))
    target = jnp.zeros((8, size_z), jnp.float32)
    for _ in range(3):
        piece = rest.astype(jnp.bfloat16)
        target = target + jnp.dot(piece, pick, preferred_element_type=jnp.float32)
        rest = rest - piece.astype(jnp.float32)
    target = target * float(grid_x * grid_y * band)
    own_target = jnp.where(lane8 // width == iy, target, 0.0)
    reach = width
    while reach < size_z:
        own_target = own_target + pltpu.roll(own_target, reach, 1)
        reach *= 2
    for r in range(group_rows):
        line = jnp.full((1, size_z), INVERSE_LEAVES[0], jnp.float32)
        for g in range(ny):
            j = min(g * group_rows + r + 1, TRIALS - 1)
            line = jnp.where(lane8[0:1] // width == g, INVERSE_LEAVES[j], line)
        leaf_table[pl.ds(r, 1), :] = line

    pl.semaphore_wait(barrier, (nx - 1) + (ny - 1) + corners)

    design_copies = edge_copies(0)
    edge_start(design_copies)
    basis_steps = ((-1, 0), (0, -1), (-1, -1))
    def basis_copies(pair):
        rows = pl.ds(pair * 6, 6)
        return [
            pltpu.make_async_remote_copy(
                src_ref=src.at[rows] if k < 2 else src.at[pair],
                dst_ref=dst.at[rows] if k < 2 else dst.at[pair],
                send_sem=basis_send_sem.at[pair, k],
                recv_sem=basis_recv_sem.at[pair, k],
                device_id=(ix + dx, iy + dy),
                device_id_type=MESH,
            )
            for k, ((dx, dy), src, dst) in enumerate(
                zip(basis_steps, (send_x, send_y, send_c), (recv_x, recv_y, recv_c))
            )
        ]

    for pair in range(pairs):
        for (dx, dy), copy in zip(basis_steps, basis_copies(pair)):
            @pl.when(there(dx, dy))
            def _(copy=copy):
                copy.start()

    for x in range(size_x):
        fields[:, x * pitch : x * pitch + size_y, :] = (
            basis[:, x * size_y : (x + 1) * size_y, :] * free[x * size_y : (x + 1) * size_y][None]
        )

    row_y = lax.broadcasted_iota(jnp.int32, (size_y, size_z), 0)

    def inside(plane, oy):
        at_x = ix * size_x + plane - 2
        at_y = row_y + (iy * size_y + oy)
        ok = (at_y >= 0) & (at_y < grid_y) & (at_x >= 0) & (at_x < grid_x)
        return jnp.where(ok, 1.0, 0.0)

    for x, tile in enumerate(stencil(inside, size_x)):
        weight_sum[pl.ds(x * size_y, size_y), :] = tile

    edge_receive(design_copies, 0)
    assemble(design, 0)
    for x, tile in enumerate(stencil(wide_rows, size_x)):
        at = pl.ds(x * size_y, size_y)
        physical[at, :] = jnp.where(passive[at, :] == 1, 1.0, tile / weight_sum[at, :])

    energy[...] = jnp.zeros((2 * cells, size_z), jnp.float32)

    def pair_step(pair, carry):
        rows = pl.ds(pair * 6, 6)
        buffers = (recv_x.at[rows], recv_y.at[rows], recv_c.at[pair])
        for (dx, dy), copy, buffer in zip(basis_steps, basis_copies(pair), buffers):
            @pl.when(there(-dx, -dy))
            def _(copy=copy):
                copy.wait_recv()

            @pl.when(jnp.logical_not(there(-dx, -dy)))
            def _(buffer=buffer):
                buffer[...] = jnp.zeros(buffer.shape, jnp.float32)

        fields[rows, size_x * pitch : size_x * pitch + size_y, :] = recv_x[rows]
        for k in range(6):
            f = pair * 6 + k
            fields[f, pl.ds(size_y, size_x, stride=pitch), :] = recv_y[f]
            fields[f, pl.ds(size_x * pitch + size_y, 1), :] = recv_c[pair, pl.ds(k, 1), :]

        def corner_tiles(member):
            tiles = {}
            for c in range(3):
                f = pair * 6 + member * 3 + c
                for x in range(size_x + 1):
                    for b in range(2):
                        tile = fields[f, x * pitch + b : x * pitch + b + size_y, :]
                        tiles[c, x, b, 0] = tile
                        tiles[c, x, b, 1] = z_shift(tile, 1)
            return tiles

        order = [(a, b, d, c) for a in range(2) for b in range(2) for d in range(2) for c in range(3)]
        adjoint = corner_tiles(1)
        operand = jnp.concatenate(
            [
                jnp.concatenate([adjoint[c, x + a, b, d] for x in range(size_x)], axis=1)
                for a, b, d, c in order
            ],
            axis=0,
        )
        high = operand.astype(jnp.bfloat16)
        low = (operand - high.astype(jnp.float32)).astype(jnp.bfloat16)
        product = (
            jnp.dot(weights_hi[...], high, preferred_element_type=jnp.float32)
            + jnp.dot(weights_hi[...], low, preferred_element_type=jnp.float32)
            + jnp.dot(weights_lo[...], high, preferred_element_type=jnp.float32)
        )
        state = corner_tiles(0)
        for x in range(size_x):
            for k in range(2):
                total = energy[pl.ds((k * size_x + x) * size_y, size_y), :]
                for r, (a, b, d, c) in enumerate(order):
                    at = k * wide_n + r * size_y
                    total = total + state[c, x + a, b, d] * product[at : at + size_y, x * size_z : (x + 1) * size_z]
                energy[pl.ds((k * size_x + x) * size_y, size_y), :] = total
        return carry

    lax.fori_loop(0, pairs, pair_step, 0)

    solid = passive[...] == 1
    density = physical[...]
    raw = -(
        PENALTY_SCALE * density * density * energy[0:cells, :]
        - OMEGA_SQUARED * energy[cells : 2 * cells, :]
    )
    scaled[...] = jnp.where(solid, 0.0, raw) / weight_sum[...]

    pack_edges(scaled, 1)
    scaled_copies = edge_copies(1)
    edge_start(scaled_copies)
    edge_receive(scaled_copies, 1)
    assemble(scaled, 1)
    for x, tile in enumerate(stencil(wide_rows, size_x)):
        benefit[pl.ds(x * size_y, size_y), :] = -tile
    benefit_out = pltpu.make_async_copy(benefit, benefit_hbm, out_sem)
    benefit_out.start()

    value = design[...]
    gain = value * jnp.sqrt(jnp.maximum(benefit[...], 0.0))
    floor_value = jnp.where(solid, 1.0, jnp.maximum(value - MOVE_LIMIT, 0.0))
    ceiling = jnp.where(solid, 1.0, jnp.minimum(value + MOVE_LIMIT, 1.0))

    def candidate(inverse_root):
        return jnp.minimum(ceiling, jnp.maximum(floor_value, gain * inverse_root))

    def total_over_x(j):
        trial = candidate(INVERSE_MIDDLES[j])
        return functools.reduce(
            lambda p, q: p + q, [trial[x * size_y : (x + 1) * size_y] for x in range(size_x)]
        )

    volumes = []
    for first in range(0, TRIALS, 8):
        tiles = [
            total_over_x(j) if j < TRIALS - 1 else jnp.zeros((8, size_z), jnp.float32)
            for j in range(first, first + 8)
        ]
        reach = 4
        while reach:
            lower = (slot_row & reach) == 0
            tiles = [
                jnp.where(lower, p, q)
                + jnp.where(lower, pltpu.roll(p, 8 - reach, 0), pltpu.roll(q, reach, 0))
                for p, q in zip(tiles[:reach], tiles[reach:])
            ]
            reach //= 2
        volumes.append(tiles[0])
    volumes = jnp.concatenate(volumes, axis=0)

    for q in range(ny):
        packed = jnp.zeros((group_rows, size_z), jnp.float32)
        for g in range(ny):
            part = volumes[g * group_rows : (g + 1) * group_rows]
            turn = (width * (g - q)) % size_z
            if turn:
                part = pltpu.roll(part, turn, 1)
            packed = jnp.where(group == g, part, packed)
        share_send[q] = packed
    share_recv[pl.ds(iy, 1)] = share_send[pl.ds(iy, 1)]
    pending = []

    def along(count, me, place, source, buffer, send_sem, recv_sem):
        copies = []
        for step in range(1, count):
            peer = lax.rem(me + step, count)
            copy = pltpu.make_async_remote_copy(
                src_ref=source(peer),
                dst_ref=buffer.at[me],
                send_sem=send_sem.at[step],
                recv_sem=recv_sem.at[step],
                device_id=place(peer),
                device_id_type=MESH,
            )
            copy.start()
            copies.append(copy)
        for copy in copies:
            copy.wait_recv()
        pending.extend(copies)

    along(ny, iy, lambda at: (ix, at), lambda at: share_send.at[at], share_recv, share_send_sem, share_recv_sem)
    share = functools.reduce(lambda p, q: p + q, [share_recv[k] for k in range(ny)])
    gather_x[pl.ds(ix, 1)] = share[None]
    along(nx, ix, lambda at: (at, iy), lambda at: gather_x.at[ix], gather_x, gx_send_sem, gx_recv_sem)
    share = functools.reduce(lambda p, q: p + q, [gather_x[k] for k in range(nx)])

    reach = 1
    while reach < band:
        share = share + jnp.where(
            (lane // reach) % 2 == 0,
            pltpu.roll(share, size_z - reach, 1),
            pltpu.roll(share, reach, 1),
        )
        reach *= 2
    chosen = jnp.where(share > own_target[0:1], leaf_table[...], INVERSE_LEAVES[0])
    chosen = jnp.min(chosen, axis=0, keepdims=True)
    reach = width
    while reach < size_z:
        chosen = jnp.minimum(chosen, pltpu.roll(chosen, reach, 1))
        reach *= 2
    gather_y[pl.ds(iy, 1)] = jnp.broadcast_to(chosen, (8, size_z))[None]
    along(ny, iy, lambda at: (ix, at), lambda at: gather_y.at[iy], gather_y, gy_send_sem, gy_recv_sem)
    multiplier = gather_y[0]
    for q in range(1, ny):
        multiplier = jnp.where(lane8 // width == q, gather_y[q], multiplier)
    chosen_out[...] = multiplier
    benefit_out.wait()

    edge_finish(design_copies)
    edge_finish(scaled_copies)
    for pair in range(pairs):
        for (dx, dy), copy in zip(basis_steps, basis_copies(pair)):
            @pl.when(there(dx, dy))
            def _(copy=copy):
                copy.wait_send()
    for copy in pending:
        copy.wait_send()


def shards(nx, ny, design, passive, basis_pairs, supports, stiffness, mass_matrix, volume_fraction):
    size_x, size_y, size_z = design.shape
    pairs = basis_pairs.shape[0]
    regions = volume_fraction.shape[0]
    cells = size_x * size_y
    fields_n = 6 * pairs
    flat = (cells, size_z)
    vmem = pl.BlockSpec(memory_space=pltpu.VMEM)
    f32, bf16 = jnp.float32, jnp.bfloat16
    dma = pltpu.SemaphoreType.DMA
    negated, inverse_root = pl.pallas_call(
        functools.partial(kernel, nx, ny, size_x, size_y, size_z, pairs, regions),
        out_shape=(jax.ShapeDtypeStruct(flat, f32), jax.ShapeDtypeStruct((size_y, size_z), f32)),
        in_specs=[pl.BlockSpec(memory_space=pltpu.HBM)] * 7,
        out_specs=(pl.BlockSpec(memory_space=pltpu.HBM), vmem),
        scratch_shapes=[
            pltpu.VMEM(flat, f32),
            pltpu.VMEM(flat, f32),
            pltpu.VMEM(flat, jnp.int32),
            pltpu.VMEM((fields_n, cells, size_z), f32),
            pltpu.VMEM(flat, jnp.int32),
            pltpu.VMEM(stiffness.shape, f32),
            pltpu.VMEM(mass_matrix.shape, f32),
            pltpu.VMEM((regions,), f32),
            pltpu.VMEM((fields_n, (size_x + 1) * 2 * size_y, size_z), f32),
            pltpu.VMEM((fields_n, size_y, size_z), f32),
            pltpu.VMEM((fields_n, size_x, size_z), f32),
            pltpu.VMEM((pairs, 6, size_z), f32),
            pltpu.VMEM((fields_n, size_y, size_z), f32),
            pltpu.VMEM((fields_n, size_x, size_z), f32),
            pltpu.VMEM((pairs, 6, size_z), f32),
            pltpu.VMEM((2, 4, 2, size_x, size_z), f32),
            pltpu.VMEM((2, 8, 2, size_y, size_z), f32),
            pltpu.VMEM(((size_x + 4) * 3 * size_y, size_z), f32),
            pltpu.VMEM(flat, f32),
            pltpu.VMEM((48 * size_y, 24 * size_y), bf16),
            pltpu.VMEM((48 * size_y, 24 * size_y), bf16),
            pltpu.VMEM(flat, f32),
            pltpu.VMEM(flat, f32),
            pltpu.VMEM((2 * cells, size_z), f32),
            pltpu.VMEM((ny, TRIALS // ny, size_z), f32),
            pltpu.VMEM((ny, TRIALS // ny, size_z), f32),
            pltpu.VMEM((nx, TRIALS // ny, size_z), f32),
            pltpu.VMEM((ny, 8, size_z), f32),
            pltpu.VMEM((TRIALS // ny, size_z), f32),
            dma((7,)),
            dma,
            dma((pairs, 3)),
            dma((pairs, 3)),
            dma((2, 8)),
            dma((2, 8)),
            dma((ny,)),
            dma((ny,)),
            dma((nx,)),
            dma((nx,)),
            dma((ny,)),
            dma((ny,)),
        ],
        compiler_params=pltpu.CompilerParams(
            collective_id=0, has_side_effects=True, vmem_limit_bytes=64 * 1024 * 1024
        ),
        name="sensitivity_update",
    )(
        design.reshape(flat),
        passive.reshape(flat),
        basis_pairs.reshape(fields_n, cells, size_z),
        supports.reshape(flat),
        stiffness,
        mass_matrix,
        volume_fraction,
    )
    negated = negated.reshape(design.shape)
    trial = design * jnp.sqrt(jnp.maximum(negated, 0.0)) * inverse_root[None]
    low = jnp.maximum(design - MOVE_LIMIT, 0.0)
    high = jnp.minimum(design + MOVE_LIMIT, 1.0)
    design_next = jnp.where(passive == 1, 1.0, jnp.minimum(high, jnp.maximum(low, trial)))
    return -negated, design_next


def solution(mesh):
    placed = (
        P("gx", "gy", None),
        P("gx", "gy", None),
        P(None, None, None, "gx", "gy", None),
        P("gx", "gy", None),
        P(),
        P(),
        P(),
    )
    return jax.shard_map(
        functools.partial(shards, mesh.shape["gx"], mesh.shape["gy"]),
        mesh=mesh,
        in_specs=placed,
        out_specs=(P("gx", "gy", None), P("gx", "gy", None)),
        check_vma=False,
    )
```

```python
import functools
import math

import jax
import jax.numpy as jnp
import numpy as np
from jax import lax
from jax.experimental import pallas as pl
from jax.experimental.pallas import tpu as pltpu
from jax.sharding import PartitionSpec as P

PENALTY_SCALE = 3.0 * (1.0 - 0.001)
OMEGA_SQUARED = 0.5
MOVE_LIMIT = 0.2
BISECT = 6
TRIALS = 2**BISECT
MESH = pl.DeviceIdType.MESH
AROUND = ((-1, 0), (1, 0), (0, -1), (0, 1), (-1, -1), (-1, 1), (1, -1), (1, 1))


def tree_ends():
    ends = [np.float32(1e-4), np.float32(1e4)]
    for _ in range(BISECT):
        inner = [np.sqrt(p * q) for p, q in zip(ends, ends[1:])]
        ends = [ends[0]] + [e for pair in zip(inner, ends[1:]) for e in pair]
    return ends


ENDS = tree_ends()
INVERSE_MIDDLES = [float(np.float32(1.0) / np.sqrt(e)) for e in ENDS[1:-1]]
INVERSE_LEAVES = [
    float(np.float32(1.0) / np.sqrt(np.sqrt(p * q))) for p, q in zip(ENDS, ENDS[1:])
]


def opposite(slot):
    dx, dy = AROUND[slot]
    return AROUND.index((-dx, -dy))


def z_shift(value, step):
    axis = value.ndim - 1
    size = value.shape[axis]
    lane = lax.broadcasted_iota(jnp.int32, value.shape, axis)
    moved = pltpu.roll(value, (-step) % size, axis)
    keep = lane < size - step if step > 0 else lane >= -step
    return jnp.where(keep, moved, 0.0)


def stencil(rows_at, size_x):
    spread = [[None] * (size_x + 4) for _ in range(3)]
    for plane in range(size_x + 4):
        tiles = [rows_at(plane, oy) for oy in range(-2, 3)]
        folded_y = (tiles[2], tiles[1] + tiles[3], tiles[0] + tiles[4])
        parts = [[], [], []]
        for cy, tile in enumerate(folded_y):
            folded_z = (
                tile,
                z_shift(tile, 1) + z_shift(tile, -1),
                z_shift(tile, 2) + z_shift(tile, -2),
            )
            for cz, entry in enumerate(folded_z):
                for cx in range(3):
                    weight = 3.0 - math.sqrt(cx * cx + cy * cy + cz * cz)
                    if weight > 0.0:
                        parts[cx].append(weight * entry)
        for cx in range(3):
            spread[cx][plane] = functools.reduce(lambda a, b: a + b, parts[cx])
    return [
        spread[0][i + 2]
        + (spread[1][i + 1] + spread[1][i + 3])
        + (spread[2][i] + spread[2][i + 4])
        for i in range(size_x)
    ]


def kernel(
    nx, ny, size_x, size_y, size_z, pairs, regions,
    design_hbm, passive_hbm, basis_hbm, supports_hbm, stiffness_hbm, mass_hbm, fraction_hbm,
    benefit_hbm, chosen_out,
    benefit, design, passive, basis, supports, stiffness, mass_matrix, fraction,
    fields, send_x, send_y, recv_x, recv_y,
    edge_send, edge_recv, wide, scaled, weights_hi, weights_lo, weight_sum, physical, energy,
    share_send, share_recv, gather_x, gather_y, leaf_table,
    load_sem, out_sem,
    basis_send_sem, basis_recv_sem, halo_send_sem, halo_recv_sem,
    share_send_sem, share_recv_sem, gx_send_sem, gx_recv_sem, gy_send_sem, gy_recv_sem,
):
    ix, iy = lax.axis_index("gx"), lax.axis_index("gy")
    pitch = 2 * size_y
    cells = size_x * size_y

    def there(dx, dy):
        return (
            (ix + dx >= 0) & (ix + dx < nx) & (iy + dy >= 0) & (iy + dy < ny)
        )

    barrier = pltpu.get_barrier_semaphore()
    for step in range(1, ny):
        pl.semaphore_signal(barrier, inc=1, device_id=(ix, lax.rem(iy + step, ny)), device_id_type=MESH)
    for step in range(1, nx):
        pl.semaphore_signal(barrier, inc=1, device_id=(lax.rem(ix + step, nx), iy), device_id_type=MESH)
    for dx, dy in AROUND[4:]:
        @pl.when(there(dx, dy))
        def _(dx=dx, dy=dy):
            pl.semaphore_signal(barrier, inc=1, device_id=(ix + dx, iy + dy), device_id_type=MESH)
    corners = sum(there(dx, dy).astype(jnp.int32) for dx, dy in AROUND[4:])

    loads = [
        pltpu.make_async_copy(src, dst, load_sem.at[k])
        for k, (src, dst) in enumerate((
            (supports_hbm, supports), (basis_hbm, basis), (design_hbm, design), (passive_hbm, passive),
            (stiffness_hbm, stiffness), (mass_hbm, mass_matrix), (fraction_hbm, fraction),
        ))
    ]
    for load in loads:
        load.start()
    for load in loads:
        load.wait()

    free = 1.0 - supports[...].astype(jnp.float32)
    send_x[...] = basis[:, 0:size_y, :] * free[0:size_y][None]
    free_y = 1.0 - supports[pl.ds(0, size_x, stride=size_y), :].astype(jnp.float32)
    send_y[...] = jnp.zeros(send_y.shape, jnp.float32)
    for f in range(6 * pairs):
        rows = basis[f, pl.ds(0, size_x, stride=size_y), :] * free_y
        send_y[f // 6, pl.ds(f % 6, size_x, stride=8), :] = rows

    def pack_edges(source, which):
        for x in range(2):
            edge_send[which, 2, x] = source[pl.ds(x * size_y, size_y), :]
            edge_send[which, 3, x] = source[pl.ds((size_x - 2 + x) * size_y, size_y), :]
        for y in range(2):
            edge_send[which, 0, y] = source[pl.ds(y, size_x, stride=size_y), :]
            edge_send[which, 1, y] = source[pl.ds(size_y - 2 + y, size_x, stride=size_y), :]

    def edge_copies(which):
        copies = []
        for slot, (dx, dy) in enumerate(AROUND):
            if dy == 0:
                src = edge_send.at[which, 2 if dx < 0 else 3]
            else:
                src = edge_send.at[which, 0 if dy < 0 else 1]
            copies.append(pltpu.make_async_remote_copy(
                src_ref=src,
                dst_ref=edge_recv.at[which, opposite(slot)],
                send_sem=halo_send_sem.at[which, slot],
                recv_sem=halo_recv_sem.at[which, opposite(slot)],
                device_id=(ix + dx, iy + dy),
                device_id_type=MESH,
            ))
        return copies

    def edge_start(copies):
        for (dx, dy), copy in zip(AROUND, copies):
            @pl.when(there(dx, dy))
            def _(copy=copy):
                copy.start()

    def edge_receive(copies, which):
        for slot, (dx, dy) in enumerate(AROUND):
            copy = copies[opposite(slot)]

            @pl.when(there(dx, dy))
            def _(copy=copy):
                copy.wait_recv()

            @pl.when(jnp.logical_not(there(dx, dy)))
            def _(slot=slot):
                edge_recv[which, slot] = jnp.zeros((2, size_y, size_z), jnp.float32)

    def edge_finish(copies):
        for (dx, dy), copy in zip(AROUND, copies):
            @pl.when(there(dx, dy))
            def _(copy=copy):
                copy.wait_send()

    span = 3 * size_y

    def assemble(source, which):
        for x in range(size_x):
            wide[pl.ds((x + 2) * span + size_y, size_y), :] = source[pl.ds(x * size_y, size_y), :]
        for x in range(2):
            wide[pl.ds(x * span + size_y, size_y), :] = edge_recv[which, 0, x]
            wide[pl.ds((size_x + 2 + x) * span + size_y, size_y), :] = edge_recv[which, 1, x]
        for y in range(2):
            low, high = size_y - 2 + y, 2 * size_y + y
            wide[pl.ds(2 * span + low, size_x, stride=span), :] = edge_recv[which, 2, y]
            wide[pl.ds(2 * span + high, size_x, stride=span), :] = edge_recv[which, 3, y]
            for x in range(2):
                for slot, row in ((4, low), (5, high)):
                    wide[pl.ds(x * span + row, 1), :] = edge_recv[which, slot, y, size_x - 2 + x : size_x - 1 + x, :]
                for slot, row in ((6, low), (7, high)):
                    wide[pl.ds((size_x + 2 + x) * span + row, 1), :] = edge_recv[which, slot, y, x : x + 1, :]

    def wide_rows(plane, oy):
        return wide[pl.ds(plane * span + size_y + oy, size_y), :]

    pack_edges(design, 0)

    grid_x, grid_y = nx * size_x, ny * size_y
    wide_n, narrow_n, depth = 24 * size_y, 24, 16 * size_y
    own_n = 12 * size_y
    bits_y = size_y.bit_length() - 1

    def spread_rows(shape, row_dim):
        at = lax.broadcasted_iota(jnp.int32, shape, row_dim)
        return lax.shift_right_logical(at, bits_y) == lax.broadcasted_iota(jnp.int32, shape, 1 - row_dim)

    expand = spread_rows((wide_n, narrow_n), 0).astype(jnp.float32).astype(jnp.bfloat16)
    col = lax.broadcasted_iota(jnp.int32, (narrow_n, depth), 1)
    tile_of = lax.shift_right_logical(col, bits_y)
    beyond = col >= own_n
    corner = jnp.where(beyond, tile_of - 12, lax.shift_right_logical(tile_of * 11, 5))
    component = jnp.where(beyond, (col & (size_y - 1)) - 3, tile_of - 3 * corner)
    usable = (component >= 0) & (component < 3)
    source_row = 12 * lax.shift_right_logical(corner, 1) + 3 * (corner & 1) + component
    at_row = lax.broadcasted_iota(jnp.int32, (narrow_n, depth), 0)
    gather = [
        (usable & (at_row == source_row + 6 * b)).astype(jnp.float32).astype(jnp.bfloat16)
        for b in range(2)
    ]
    at_y = lax.broadcasted_iota(jnp.int32, (wide_n, depth), 0) & (size_y - 1)
    at_col = lax.broadcasted_iota(jnp.int32, (wide_n, depth), 1)
    col_y = at_col & (size_y - 1)
    own = at_col < own_n
    keep = [
        own & (col_y == at_y),
        (own & (col_y == at_y + 1)) | (jnp.logical_not(own) & (at_y == size_y - 1)),
    ]

    def spread_matrix(piece):
        tall = jnp.dot(expand, piece, preferred_element_type=jnp.float32).astype(jnp.bfloat16)
        full = [jnp.dot(tall, g, preferred_element_type=jnp.float32) for g in gather]
        return jnp.where(keep[0], full[0], jnp.where(keep[1], full[1], 0.0)).astype(jnp.bfloat16)

    for k, matrix in enumerate((stiffness, mass_matrix)):
        value = matrix[...]
        high = value.astype(jnp.bfloat16)
        low = (value - high.astype(jnp.float32)).astype(jnp.bfloat16)
        spread_high = spread_matrix(high)
        weights_hi[pl.ds(k * wide_n, wide_n), :] = jnp.concatenate([spread_high, spread_high], axis=1)
        weights_lo[pl.ds(k * wide_n, wide_n), :] = spread_matrix(low)

    band = size_z // regions
    width, group_rows = size_z // ny, TRIALS // ny
    lane = lax.broadcasted_iota(jnp.int32, (group_rows, size_z), 1)
    lane8 = lax.broadcasted_iota(jnp.int32, (8, size_z), 1)
    slot_row = lax.broadcasted_iota(jnp.int32, (8, size_z), 0)
    group = lane // width
    pick = (
        lax.broadcasted_iota(jnp.int32, (regions, size_z), 1) // band
        == lax.broadcasted_iota(jnp.int32, (regions, size_z), 0)
    ).astype(jnp.float32).astype(jnp.bfloat16)
    rest = jnp.broadcast_to(fraction[...].reshape(1, regions), (8, regions))
    target = jnp.zeros((8, size_z), jnp.float32)
    for _ in range(3):
        piece = rest.astype(jnp.bfloat16)
        target = target + jnp.dot(piece, pick, preferred_element_type=jnp.float32)
        rest = rest - piece.astype(jnp.float32)
    target = target * float(grid_x * grid_y * band)
    own_target = jnp.where(lane8 // width == iy, target, 0.0)
    reach = width
    while reach < size_z:
        own_target = own_target + pltpu.roll(own_target, reach, 1)
        reach *= 2
    for r in range(group_rows):
        line = jnp.full((1, size_z), INVERSE_LEAVES[0], jnp.float32)
        for g in range(ny):
            j = min(g * group_rows + r + 1, TRIALS - 1)
            line = jnp.where(lane8[0:1] // width == g, INVERSE_LEAVES[j], line)
        leaf_table[pl.ds(r, 1), :] = line

    pl.semaphore_wait(barrier, (nx - 1) + (ny - 1) + corners)

    design_copies = edge_copies(0)
    basis_steps = ((-1, 0), (0, -1), (-1, -1))
    def basis_copies(pair):
        rows = pl.ds(pair * 6, 6)
        ends = (
            (send_x.at[rows], recv_x.at[rows]),
            (send_y.at[pair], recv_y.at[pair, pl.ds(0, 8 * size_x)]),
            (send_y.at[pair, pl.ds(0, 8)], recv_y.at[pair, pl.ds(8 * size_x, 8)]),
        )
        return [
            pltpu.make_async_remote_copy(
                src_ref=src,
                dst_ref=dst,
                send_sem=basis_send_sem.at[pair, k],
                recv_sem=basis_recv_sem.at[pair, k],
                device_id=(ix + dx, iy + dy),
                device_id_type=MESH,
            )
            for k, ((dx, dy), (src, dst)) in enumerate(zip(basis_steps, ends))
        ]

    def basis_start(pair):
        for (dx, dy), copy in zip(basis_steps, basis_copies(pair)):
            @pl.when(there(dx, dy))
            def _(copy=copy):
                copy.start()

    basis_start(0)
    edge_start(design_copies)
    for pair in range(1, pairs):
        basis_start(pair)

    for x in range(size_x):
        fields[:, x * pitch : x * pitch + size_y, :] = (
            basis[:, x * size_y : (x + 1) * size_y, :] * free[x * size_y : (x + 1) * size_y][None]
        )

    row_y = lax.broadcasted_iota(jnp.int32, (size_y, size_z), 0)

    def inside(plane, oy):
        at_x = ix * size_x + plane - 2
        at_y = row_y + (iy * size_y + oy)
        ok = (at_y >= 0) & (at_y < grid_y) & (at_x >= 0) & (at_x < grid_x)
        return jnp.where(ok, 1.0, 0.0)

    for x, tile in enumerate(stencil(inside, size_x)):
        weight_sum[pl.ds(x * size_y, size_y), :] = tile

    edge_receive(design_copies, 0)
    assemble(design, 0)
    for x, tile in enumerate(stencil(wide_rows, size_x)):
        at = pl.ds(x * size_y, size_y)
        physical[at, :] = jnp.where(passive[at, :] == 1, 1.0, tile / weight_sum[at, :])

    energy[...] = jnp.zeros((2 * cells, size_z), jnp.float32)

    order = [(a, b, d, c) for a in range(2) for b in range(2) for d in range(2) for c in range(3)]

    def pair_step(pair, carry):
        rows = pl.ds(pair * 6, 6)
        buffers = (
            recv_x.at[rows], recv_y.at[pair, pl.ds(0, 8 * size_x)], recv_y.at[pair, pl.ds(8 * size_x, 8)]
        )
        for (dx, dy), copy, buffer in zip(basis_steps, basis_copies(pair), buffers):
            @pl.when(there(-dx, -dy))
            def _(copy=copy):
                copy.wait_recv()

            @pl.when(jnp.logical_not(there(-dx, -dy)))
            def _(buffer=buffer):
                buffer[...] = jnp.zeros(buffer.shape, jnp.float32)

        fields[rows, size_x * pitch : size_x * pitch + size_y, :] = recv_x[rows]
        for k in range(3):
            fields[pair * 6 + k, pl.ds(size_y, size_x + 1, stride=pitch), :] = (
                recv_y[pair, pl.ds(k, size_x + 1, stride=8), :]
            )

        state, adjoint = {}, {}
        for x in range(size_x + 1):
            border = recv_y[pair, 8 * x : 8 * x + 8, :]
            adjoint[3, x, 0], adjoint[3, x, 1] = border, z_shift(border, 1)
            for c in range(3):
                tile = fields[pair * 6 + 3 + c, x * pitch : x * pitch + size_y, :]
                adjoint[c, x, 0], adjoint[c, x, 1] = tile, z_shift(tile, 1)
                for b in range(2):
                    tile = fields[pair * 6 + c, x * pitch + b : x * pitch + b + size_y, :]
                    state[c, x, b, 0], state[c, x, b, 1] = tile, z_shift(tile, 1)

        for first in range(0, size_x, 2):
            planes = range(first, min(first + 2, size_x))
            operand = jnp.concatenate(
                [
                    jnp.concatenate([adjoint[c, x + a, d] for x in planes], axis=1)
                    for a, d, c in (
                        [(a, d, c) for a in range(2) for d in range(2) for c in range(3)]
                        + [(a, d, 3) for a in range(2) for d in range(2)]
                    )
                ],
                axis=0,
            )
            high = operand.astype(jnp.bfloat16)
            low = (operand - high.astype(jnp.float32)).astype(jnp.bfloat16)
            product = jnp.dot(
                weights_hi[...], jnp.concatenate([high, low], axis=0), preferred_element_type=jnp.float32
            ) + jnp.dot(weights_lo[...], high, preferred_element_type=jnp.float32)
            for at_x, x in enumerate(planes):
                for k in range(2):
                    total = energy[pl.ds((k * size_x + x) * size_y, size_y), :]
                    for r, (a, b, d, c) in enumerate(order):
                        at = k * wide_n + r * size_y
                        total = total + (
                            state[c, x + a, b, d]
                            * product[at : at + size_y, at_x * size_z : (at_x + 1) * size_z]
                        )
                    energy[pl.ds((k * size_x + x) * size_y, size_y), :] = total
        return carry

    lax.fori_loop(0, pairs, pair_step, 0)

    solid = passive[...] == 1
    density = physical[...]
    raw = -(
        PENALTY_SCALE * density * density * energy[0:cells, :]
        - OMEGA_SQUARED * energy[cells : 2 * cells, :]
    )
    scaled[...] = jnp.where(solid, 0.0, raw) / weight_sum[...]

    pack_edges(scaled, 1)
    scaled_copies = edge_copies(1)
    edge_start(scaled_copies)
    edge_receive(scaled_copies, 1)
    assemble(scaled, 1)
    for x, tile in enumerate(stencil(wide_rows, size_x)):
        benefit[pl.ds(x * size_y, size_y), :] = -tile
    benefit_out = pltpu.make_async_copy(benefit, benefit_hbm, out_sem)
    benefit_out.start()

    value = design[...]
    gain = value * jnp.sqrt(jnp.maximum(benefit[...], 0.0))
    floor_value = jnp.where(solid, 1.0, jnp.maximum(value - MOVE_LIMIT, 0.0))
    ceiling = jnp.where(solid, 1.0, jnp.minimum(value + MOVE_LIMIT, 1.0))

    def candidate(inverse_root):
        return jnp.minimum(ceiling, jnp.maximum(floor_value, gain * inverse_root))

    def total_over_x(j):
        trial = candidate(INVERSE_MIDDLES[j])
        return functools.reduce(
            lambda p, q: p + q, [trial[x * size_y : (x + 1) * size_y] for x in range(size_x)]
        )

    volumes = []
    for first in range(0, TRIALS, 8):
        tiles = [
            total_over_x(j) if j < TRIALS - 1 else jnp.zeros((8, size_z), jnp.float32)
            for j in range(first, first + 8)
        ]
        reach = 4
        while reach:
            lower = (slot_row & reach) == 0
            tiles = [
                jnp.where(lower, p, q)
                + jnp.where(lower, pltpu.roll(p, 8 - reach, 0), pltpu.roll(q, reach, 0))
                for p, q in zip(tiles[:reach], tiles[reach:])
            ]
            reach //= 2
        volumes.append(tiles[0])
    volumes = jnp.concatenate(volumes, axis=0)

    for q in range(ny):
        packed = jnp.zeros((group_rows, size_z), jnp.float32)
        for g in range(ny):
            part = volumes[g * group_rows : (g + 1) * group_rows]
            turn = (width * (g - q)) % size_z
            if turn:
                part = pltpu.roll(part, turn, 1)
            packed = jnp.where(group == g, part, packed)
        share_send[q] = packed
    share_recv[pl.ds(iy, 1)] = share_send[pl.ds(iy, 1)]
    pending = []

    def along(count, me, place, source, buffer, send_sem, recv_sem):
        copies = []
        for step in range(1, count):
            peer = lax.rem(me + step, count)
            copy = pltpu.make_async_remote_copy(
                src_ref=source(peer),
                dst_ref=buffer.at[me],
                send_sem=send_sem.at[step],
                recv_sem=recv_sem.at[step],
                device_id=place(peer),
                device_id_type=MESH,
            )
            copy.start()
            copies.append(copy)
        for copy in copies:
            copy.wait_recv()
        pending.extend(copies)

    along(ny, iy, lambda at: (ix, at), lambda at: share_send.at[at], share_recv, share_send_sem, share_recv_sem)
    share = functools.reduce(lambda p, q: p + q, [share_recv[k] for k in range(ny)])
    gather_x[pl.ds(ix, 1)] = share[None]
    along(nx, ix, lambda at: (at, iy), lambda at: gather_x.at[ix], gather_x, gx_send_sem, gx_recv_sem)
    share = functools.reduce(lambda p, q: p + q, [gather_x[k] for k in range(nx)])

    reach = 1
    while reach < band:
        share = share + jnp.where(
            (lane // reach) % 2 == 0,
            pltpu.roll(share, size_z - reach, 1),
            pltpu.roll(share, reach, 1),
        )
        reach *= 2
    chosen = jnp.where(share > own_target[0:1], leaf_table[...], INVERSE_LEAVES[0])
    chosen = jnp.min(chosen, axis=0, keepdims=True)
    reach = width
    while reach < size_z:
        chosen = jnp.minimum(chosen, pltpu.roll(chosen, reach, 1))
        reach *= 2
    gather_y[pl.ds(iy, 1)] = jnp.broadcast_to(chosen, (8, size_z))[None]
    along(ny, iy, lambda at: (ix, at), lambda at: gather_y.at[iy], gather_y, gy_send_sem, gy_recv_sem)
    multiplier = gather_y[0]
    for q in range(1, ny):
        multiplier = jnp.where(lane8 // width == q, gather_y[q], multiplier)
    chosen_out[...] = multiplier
    benefit_out.wait()

    edge_finish(design_copies)
    edge_finish(scaled_copies)
    for pair in range(pairs):
        for (dx, dy), copy in zip(basis_steps, basis_copies(pair)):
            @pl.when(there(dx, dy))
            def _(copy=copy):
                copy.wait_send()
    for copy in pending:
        copy.wait_send()


def closing_kernel(negated, inverse_root, design, passive, sensitivity, design_next):
    benefit, value = negated[...], design[...]
    sensitivity[...] = -benefit
    trial = value * jnp.sqrt(jnp.maximum(benefit, 0.0)) * inverse_root[0:1, :]
    low = jnp.maximum(value - MOVE_LIMIT, 0.0)
    high = jnp.minimum(value + MOVE_LIMIT, 1.0)
    design_next[...] = jnp.where(passive[...] == 1, 1.0, jnp.minimum(high, jnp.maximum(low, trial)))


def shards(nx, ny, design, passive, basis_pairs, supports, stiffness, mass_matrix, volume_fraction):
    size_x, size_y, size_z = design.shape
    pairs = basis_pairs.shape[0]
    regions = volume_fraction.shape[0]
    cells = size_x * size_y
    fields_n = 6 * pairs
    flat = (cells, size_z)
    vmem = pl.BlockSpec(memory_space=pltpu.VMEM)
    f32, bf16 = jnp.float32, jnp.bfloat16
    dma = pltpu.SemaphoreType.DMA
    negated, inverse_root = pl.pallas_call(
        functools.partial(kernel, nx, ny, size_x, size_y, size_z, pairs, regions),
        out_shape=(jax.ShapeDtypeStruct(flat, f32), jax.ShapeDtypeStruct((size_y, size_z), f32)),
        in_specs=[pl.BlockSpec(memory_space=pltpu.HBM)] * 7,
        out_specs=(pl.BlockSpec(memory_space=pltpu.HBM), vmem),
        scratch_shapes=[
            pltpu.VMEM(flat, f32),
            pltpu.VMEM(flat, f32),
            pltpu.VMEM(flat, jnp.int32),
            pltpu.VMEM((fields_n, cells, size_z), f32),
            pltpu.VMEM(flat, jnp.int32),
            pltpu.VMEM(stiffness.shape, f32),
            pltpu.VMEM(mass_matrix.shape, f32),
            pltpu.VMEM((regions,), f32),
            pltpu.VMEM((fields_n, (size_x + 1) * 2 * size_y, size_z), f32),
            pltpu.VMEM((fields_n, size_y, size_z), f32),
            pltpu.VMEM((pairs, 8 * size_x, size_z), f32),
            pltpu.VMEM((fields_n, size_y, size_z), f32),
            pltpu.VMEM((pairs, 8 * (size_x + 1), size_z), f32),
            pltpu.VMEM((2, 4, 2, size_x, size_z), f32),
            pltpu.VMEM((2, 8, 2, size_y, size_z), f32),
            pltpu.VMEM(((size_x + 4) * 3 * size_y, size_z), f32),
            pltpu.VMEM(flat, f32),
            pltpu.VMEM((48 * size_y, 32 * size_y), bf16),
            pltpu.VMEM((48 * size_y, 16 * size_y), bf16),
            pltpu.VMEM(flat, f32),
            pltpu.VMEM(flat, f32),
            pltpu.VMEM((2 * cells, size_z), f32),
            pltpu.VMEM((ny, TRIALS // ny, size_z), f32),
            pltpu.VMEM((ny, TRIALS // ny, size_z), f32),
            pltpu.VMEM((nx, TRIALS // ny, size_z), f32),
            pltpu.VMEM((ny, 8, size_z), f32),
            pltpu.VMEM((TRIALS // ny, size_z), f32),
            dma((7,)),
            dma,
            dma((pairs, 3)),
            dma((pairs, 3)),
            dma((2, 8)),
            dma((2, 8)),
            dma((ny,)),
            dma((ny,)),
            dma((nx,)),
            dma((nx,)),
            dma((ny,)),
            dma((ny,)),
        ],
        compiler_params=pltpu.CompilerParams(
            collective_id=0, has_side_effects=True, vmem_limit_bytes=64 * 1024 * 1024
        ),
        name="sensitivity_update",
    )(
        design.reshape(flat),
        passive.reshape(flat),
        basis_pairs.reshape(fields_n, cells, size_z),
        supports.reshape(flat),
        stiffness,
        mass_matrix,
        volume_fraction,
    )
    sensitivity, design_next = pl.pallas_call(
        closing_kernel,
        out_shape=(jax.ShapeDtypeStruct(flat, f32), jax.ShapeDtypeStruct(flat, f32)),
        in_specs=[vmem] * 4,
        out_specs=(vmem, vmem),
        compiler_params=pltpu.CompilerParams(vmem_limit_bytes=64 * 1024 * 1024),
        name="design_update",
    )(negated, inverse_root, design.reshape(flat), passive.reshape(flat))
    return sensitivity.reshape(design.shape), design_next.reshape(design.shape)


def solution(mesh):
    placed = (
        P("gx", "gy", None),
        P("gx", "gy", None),
        P(None, None, None, "gx", "gy", None),
        P("gx", "gy", None),
        P(),
        P(),
        P(),
    )
    return jax.shard_map(
        functools.partial(shards, mesh.shape["gx"], mesh.shape["gy"]),
        mesh=mesh,
        in_specs=placed,
        out_specs=(P("gx", "gy", None), P("gx", "gy", None)),
        check_vma=False,
    )
```

```python
import functools
import math

import jax
import jax.numpy as jnp
import numpy as np
from jax import lax
from jax.experimental import pallas as pl
from jax.experimental.pallas import tpu as pltpu
from jax.sharding import PartitionSpec as P

PENALTY_SCALE = 3.0 * (1.0 - 0.001)
OMEGA_SQUARED = 0.5
MOVE_LIMIT = 0.2
BISECT = 6
TRIALS = 2**BISECT
MESH = pl.DeviceIdType.MESH
AROUND = ((-1, 0), (1, 0), (0, -1), (0, 1), (-1, -1), (-1, 1), (1, -1), (1, 1))


def tree_ends():
    ends = [np.float32(1e-4), np.float32(1e4)]
    for _ in range(BISECT):
        inner = [np.sqrt(p * q) for p, q in zip(ends, ends[1:])]
        ends = [ends[0]] + [e for pair in zip(inner, ends[1:]) for e in pair]
    return ends


ENDS = tree_ends()
INVERSE_MIDDLES = [float(np.float32(1.0) / np.sqrt(e)) for e in ENDS[1:-1]]
INVERSE_LEAVES = [
    float(np.float32(1.0) / np.sqrt(np.sqrt(p * q))) for p, q in zip(ENDS, ENDS[1:])
]


def opposite(slot):
    dx, dy = AROUND[slot]
    return AROUND.index((-dx, -dy))


def z_shift(value, step):
    axis = value.ndim - 1
    size = value.shape[axis]
    lane = lax.broadcasted_iota(jnp.int32, value.shape, axis)
    moved = pltpu.roll(value, (-step) % size, axis)
    keep = lane < size - step if step > 0 else lane >= -step
    return jnp.where(keep, moved, 0.0)


def stencil(rows_at, size_x):
    spread = [[None] * (size_x + 4) for _ in range(3)]
    for plane in range(size_x + 4):
        tiles = [rows_at(plane, oy) for oy in range(-2, 3)]
        folded_y = (tiles[2], tiles[1] + tiles[3], tiles[0] + tiles[4])
        parts = [[], [], []]
        for cy, tile in enumerate(folded_y):
            folded_z = (
                tile,
                z_shift(tile, 1) + z_shift(tile, -1),
                z_shift(tile, 2) + z_shift(tile, -2),
            )
            for cz, entry in enumerate(folded_z):
                for cx in range(3):
                    weight = 3.0 - math.sqrt(cx * cx + cy * cy + cz * cz)
                    if weight > 0.0:
                        parts[cx].append(weight * entry)
        for cx in range(3):
            spread[cx][plane] = functools.reduce(lambda a, b: a + b, parts[cx])
    return [
        spread[0][i + 2]
        + (spread[1][i + 1] + spread[1][i + 3])
        + (spread[2][i] + spread[2][i + 4])
        for i in range(size_x)
    ]


def kernel(
    nx, ny, size_x, size_y, size_z, pairs, regions,
    design_hbm, passive_hbm, basis_hbm, supports_hbm, stiffness_hbm, mass_hbm, fraction_hbm,
    benefit_hbm, chosen_out,
    benefit, design, passive, basis, supports, stiffness, mass_matrix, fraction,
    fields, send_x, send_y, recv_x, recv_y,
    edge_send, edge_recv, wide, scaled, weights_hi, weights_lo, border_hi, border_lo, weight_sum, physical, energy,
    share_send, share_recv, gather_x, gather_y, leaf_table,
    load_sem, out_sem,
    basis_send_sem, basis_recv_sem, halo_send_sem, halo_recv_sem,
    share_send_sem, share_recv_sem, gx_send_sem, gx_recv_sem, gy_send_sem, gy_recv_sem,
):
    ix, iy = lax.axis_index("gx"), lax.axis_index("gy")
    pitch = 2 * size_y
    cells = size_x * size_y

    def there(dx, dy):
        return (
            (ix + dx >= 0) & (ix + dx < nx) & (iy + dy >= 0) & (iy + dy < ny)
        )

    edge_recv[...] = jnp.zeros(edge_recv.shape, jnp.float32)
    recv_x[...] = jnp.zeros(recv_x.shape, jnp.float32)
    recv_y[...] = jnp.zeros(recv_y.shape, jnp.float32)
    barrier = pltpu.get_barrier_semaphore()
    for step in range(1, ny):
        pl.semaphore_signal(barrier, inc=1, device_id=(ix, lax.rem(iy + step, ny)), device_id_type=MESH)
    for step in range(1, nx):
        pl.semaphore_signal(barrier, inc=1, device_id=(lax.rem(ix + step, nx), iy), device_id_type=MESH)
    for dx, dy in AROUND[4:]:
        @pl.when(there(dx, dy))
        def _(dx=dx, dy=dy):
            pl.semaphore_signal(barrier, inc=1, device_id=(ix + dx, iy + dy), device_id_type=MESH)
    corners = sum(there(dx, dy).astype(jnp.int32) for dx, dy in AROUND[4:])

    loads = [
        pltpu.make_async_copy(src, dst, load_sem.at[k])
        for k, (src, dst) in enumerate((
            (supports_hbm, supports), (basis_hbm, basis), (design_hbm, design), (passive_hbm, passive),
            (stiffness_hbm, stiffness), (mass_hbm, mass_matrix), (fraction_hbm, fraction),
        ))
    ]
    for load in loads:
        load.start()
    send_y[...] = jnp.zeros(send_y.shape, jnp.float32)
    for load in loads[:2]:
        load.wait()

    free = 1.0 - supports[...].astype(jnp.float32)
    send_x[...] = basis[:, 0:size_y, :] * free[0:size_y][None]
    free_y = 1.0 - supports[pl.ds(0, size_x, stride=size_y), :].astype(jnp.float32)
    for f in range(6 * pairs):
        rows = basis[f, pl.ds(0, size_x, stride=size_y), :] * free_y
        send_y[f // 6, pl.ds(f % 6, size_x, stride=8), :] = rows

    def pack_edges(source, which):
        for x in range(2):
            edge_send[which, 2, x] = source[pl.ds(x * size_y, size_y), :]
            edge_send[which, 3, x] = source[pl.ds((size_x - 2 + x) * size_y, size_y), :]
        for y in range(2):
            edge_send[which, 0, y] = source[pl.ds(y, size_x, stride=size_y), :]
            edge_send[which, 1, y] = source[pl.ds(size_y - 2 + y, size_x, stride=size_y), :]

    def edge_copies(which):
        copies = []
        for slot, (dx, dy) in enumerate(AROUND):
            if dy == 0:
                src = edge_send.at[which, 2 if dx < 0 else 3]
            else:
                src = edge_send.at[which, 0 if dy < 0 else 1]
            copies.append(pltpu.make_async_remote_copy(
                src_ref=src,
                dst_ref=edge_recv.at[which, opposite(slot)],
                send_sem=halo_send_sem.at[which, slot],
                recv_sem=halo_recv_sem.at[which, opposite(slot)],
                device_id=(ix + dx, iy + dy),
                device_id_type=MESH,
            ))
        return copies

    def edge_each(copies, act):
        for slot, (dx, dy) in enumerate(AROUND):
            @pl.when(there(dx, dy))
            def _(slot=slot):
                act(copies, slot)

    def edge_receive(copies):
        edge_each(copies, lambda c, slot: c[opposite(slot)].wait_recv())

    span = 3 * size_y

    def assemble(source, which):
        for x in range(size_x):
            wide[pl.ds((x + 2) * span + size_y, size_y), :] = source[pl.ds(x * size_y, size_y), :]
        for x in range(2):
            wide[pl.ds(x * span + size_y, size_y), :] = edge_recv[which, 0, x]
            wide[pl.ds((size_x + 2 + x) * span + size_y, size_y), :] = edge_recv[which, 1, x]
        for y in range(2):
            low, high = size_y - 2 + y, 2 * size_y + y
            wide[pl.ds(2 * span + low, size_x, stride=span), :] = edge_recv[which, 2, y]
            wide[pl.ds(2 * span + high, size_x, stride=span), :] = edge_recv[which, 3, y]
            for x in range(2):
                for slot, row in ((4, low), (5, high)):
                    wide[pl.ds(x * span + row, 1), :] = edge_recv[which, slot, y, size_x - 2 + x : size_x - 1 + x, :]
                for slot, row in ((6, low), (7, high)):
                    wide[pl.ds((size_x + 2 + x) * span + row, 1), :] = edge_recv[which, slot, y, x : x + 1, :]

    def wide_rows(plane, oy):
        return wide[pl.ds(plane * span + size_y + oy, size_y), :]

    loads[2].wait()
    pack_edges(design, 0)

    pl.semaphore_wait(barrier, (nx - 1) + (ny - 1) + corners)

    design_copies = edge_copies(0)
    basis_copies = {
        slot: pltpu.make_async_remote_copy(
            src_ref=src,
            dst_ref=dst,
            send_sem=basis_send_sem.at[k],
            recv_sem=basis_recv_sem.at[k],
            device_id=(ix + AROUND[slot][0], iy + AROUND[slot][1]),
            device_id_type=MESH,
        )
        for k, (slot, src, dst) in enumerate((
            (0, send_x, recv_x),
            (2, send_y, recv_y.at[:, pl.ds(0, 8 * size_x)]),
            (4, send_y.at[:, pl.ds(0, 8)], recv_y.at[:, pl.ds(8 * size_x, 8)]),
        ))
    }

    def leave(copies, slot):
        if slot in basis_copies:
            basis_copies[slot].start()
        copies[slot].start()

    def left(copies, slot):
        if slot in basis_copies:
            basis_copies[slot].wait_send()
        copies[slot].wait_send()

    edge_each(design_copies, leave)
    for load in loads[3:]:
        load.wait()

    grid_x, grid_y = nx * size_x, ny * size_y
    wide_n, narrow_n, depth = 24 * size_y, 24, 12 * size_y
    bits_y = size_y.bit_length() - 1

    def spread_rows(shape, row_dim):
        at = lax.broadcasted_iota(jnp.int32, shape, row_dim)
        return lax.shift_right_logical(at, bits_y) == lax.broadcasted_iota(jnp.int32, shape, 1 - row_dim)

    expand = spread_rows((wide_n, narrow_n), 0).astype(jnp.float32).astype(jnp.bfloat16)
    col = lax.broadcasted_iota(jnp.int32, (narrow_n, depth), 1)
    tile_of = lax.shift_right_logical(col, bits_y)
    corner = lax.shift_right_logical(tile_of * 11, 5)
    component = tile_of - 3 * corner
    source_row = 12 * lax.shift_right_logical(corner, 1) + 3 * (corner & 1) + component
    at_row = lax.broadcasted_iota(jnp.int32, (narrow_n, depth), 0)
    gather = [
        (at_row == source_row + 6 * b).astype(jnp.float32).astype(jnp.bfloat16)
        for b in range(2)
    ]
    at_y = lax.broadcasted_iota(jnp.int32, (wide_n, depth), 0) & (size_y - 1)
    col_y = lax.broadcasted_iota(jnp.int32, (wide_n, depth), 1) & (size_y - 1)
    keep = [col_y == at_y, col_y == at_y + 1]
    expand_t = spread_rows((narrow_n, wide_n), 1).astype(jnp.float32).astype(jnp.bfloat16)
    same = (
        lax.broadcasted_iota(jnp.int32, (wide_n, wide_n), 0) & (size_y - 1)
    ) == (lax.broadcasted_iota(jnp.int32, (wide_n, wide_n), 1) & (size_y - 1))

    def spread_matrix(piece):
        tall = jnp.dot(expand, piece, preferred_element_type=jnp.float32).astype(jnp.bfloat16)
        full = [jnp.dot(tall, g, preferred_element_type=jnp.float32) for g in gather]
        banded = jnp.where(keep[0], full[0], jnp.where(keep[1], full[1], 0.0))
        plain = jnp.where(same, jnp.dot(tall, expand_t, preferred_element_type=jnp.float32), 0.0)
        return banded.astype(jnp.bfloat16), plain.astype(jnp.bfloat16)

    for k, matrix in enumerate((stiffness, mass_matrix)):
        value = matrix[...]
        high = value.astype(jnp.bfloat16)
        low = (value - high.astype(jnp.float32)).astype(jnp.bfloat16)
        at = pl.ds(k * wide_n, wide_n)
        banded, plain = spread_matrix(high)
        weights_hi[at, :] = jnp.concatenate([banded, banded], axis=1)
        border_hi[at, :] = plain
        weights_lo[at, :], border_lo[at, :] = spread_matrix(low)

    band = size_z // regions
    width, group_rows = size_z // ny, TRIALS // ny
    lane = lax.broadcasted_iota(jnp.int32, (group_rows, size_z), 1)
    lane8 = lax.broadcasted_iota(jnp.int32, (8, size_z), 1)
    slot_row = lax.broadcasted_iota(jnp.int32, (8, size_z), 0)
    group = lane // width
    pick = (
        lax.broadcasted_iota(jnp.int32, (regions, size_z), 1) // band
        == lax.broadcasted_iota(jnp.int32, (regions, size_z), 0)
    ).astype(jnp.float32).astype(jnp.bfloat16)
    rest = jnp.broadcast_to(fraction[...].reshape(1, regions), (8, regions))
    target = jnp.zeros((8, size_z), jnp.float32)
    for _ in range(3):
        piece = rest.astype(jnp.bfloat16)
        target = target + jnp.dot(piece, pick, preferred_element_type=jnp.float32)
        rest = rest - piece.astype(jnp.float32)
    target = target * float(grid_x * grid_y * band)
    own_target = jnp.where(lane8 // width == iy, target, 0.0)
    reach = width
    while reach < size_z:
        own_target = own_target + pltpu.roll(own_target, reach, 1)
        reach *= 2
    for r in range(group_rows):
        line = jnp.full((1, size_z), INVERSE_LEAVES[0], jnp.float32)
        for g in range(ny):
            j = min(g * group_rows + r + 1, TRIALS - 1)
            line = jnp.where(lane8[0:1] // width == g, INVERSE_LEAVES[j], line)
        leaf_table[pl.ds(r, 1), :] = line

    for x in range(size_x + 1):
        fields[:, x * pitch + size_y : (x + 1) * pitch, :] = jnp.zeros((6 * pairs, size_y, size_z), jnp.float32)
    for x in range(size_x):
        fields[:, x * pitch : x * pitch + size_y, :] = (
            basis[:, x * size_y : (x + 1) * size_y, :] * free[x * size_y : (x + 1) * size_y][None]
        )

    row_y = lax.broadcasted_iota(jnp.int32, (size_y, size_z), 0)

    def inside(plane, oy):
        at_x = ix * size_x + plane - 2
        at_y = row_y + (iy * size_y + oy)
        ok = (at_y >= 0) & (at_y < grid_y) & (at_x >= 0) & (at_x < grid_x)
        return jnp.where(ok, 1.0, 0.0)

    for x, tile in enumerate(stencil(inside, size_x)):
        weight_sum[pl.ds(x * size_y, size_y), :] = tile

    energy[...] = jnp.zeros((2 * cells, size_z), jnp.float32)
    order = [(a, b, d, c) for a in range(2) for b in range(2) for d in range(2) for c in range(3)]

    def beside(tiles):
        return tiles[0] if len(tiles) == 1 else jnp.concatenate(tiles, axis=1)

    def split(operand):
        high = operand.astype(jnp.bfloat16)
        return high, (operand - high.astype(jnp.float32)).astype(jnp.bfloat16)

    def contract(product, states):
        return [
            [
                functools.reduce(
                    lambda p, q: p + q,
                    [
                        state[key] * product[
                            k * wide_n + r * size_y : k * wide_n + (r + 1) * size_y,
                            n * size_z : (n + 1) * size_z,
                        ]
                        for r, key in enumerate(order)
                    ],
                )
                for k in range(2)
            ]
            for n, state in enumerate(states)
        ]

    def name_of(pair):
        return pair if isinstance(pair, int) else -1

    def own_columns(columns):
        adjoint, state = {}, {}
        for pair, x in columns:
            for c in range(3):
                for at_x in (x, x + 1):
                    key = (name_of(pair), at_x, c)
                    if key in adjoint:
                        continue
                    tile = fields[pair * 6 + 3 + c, at_x * pitch : at_x * pitch + size_y, :]
                    adjoint[key] = (tile, z_shift(tile, 1))
                    for b in range(2):
                        tile = fields[pair * 6 + c, at_x * pitch + b : at_x * pitch + b + size_y, :]
                        state[key + (b,)] = (tile, z_shift(tile, 1))
        high, low = split(jnp.concatenate(
            [
                beside([adjoint[name_of(pair), x + a, c][d] for pair, x in columns])
                for a in range(2) for d in range(2) for c in range(3)
            ],
            axis=0,
        ))
        product = jnp.dot(
            weights_hi[...], jnp.concatenate([high, low], axis=0), preferred_element_type=jnp.float32
        ) + jnp.dot(weights_lo[...], high, preferred_element_type=jnp.float32)
        states = [
            {(a, b, d, c): state[name_of(pair), x + a, c, b][d] for a, b, d, c in order} for pair, x in columns
        ]
        for (pair, x), parts in zip(columns, contract(product, states)):
            for k, part in enumerate(parts):
                at = pl.ds((k * size_x + x) * size_y, size_y)
                energy[at, :] = energy[at, :] + part

    def pair_step(pair, carry):
        for first in range(0, size_x - 1, 2):
            own_columns([(pair, x) for x in range(first, min(first + 2, size_x - 1))])
        return carry

    lax.fori_loop(0, pairs, pair_step, 0)

    edge_receive(design_copies)
    assemble(design, 0)
    for x, tile in enumerate(stencil(wide_rows, size_x)):
        at = pl.ds(x * size_y, size_y)
        physical[at, :] = jnp.where(passive[at, :] == 1, 1.0, tile / weight_sum[at, :])

    for slot in basis_copies:
        dx, dy = AROUND[slot]

        @pl.when(there(-dx, -dy))
        def _(slot=slot):
            basis_copies[slot].wait_recv()

    fields[:, size_x * pitch : size_x * pitch + size_y, :] = recv_x[...]
    for first in range(0, pairs, 2):
        own_columns([(pair, size_x - 1) for pair in range(first, min(first + 2, pairs))])

    def border_tiles(pair, member):
        tiles = {}
        for c in range(3):
            f, k = pair * 6 + member * 3 + c, member * 3 + c
            for a in range(2):
                for b in range(2):
                    if b == 0:
                        tile = fields[f, pl.ds(a * pitch + size_y - 1, size_x, stride=pitch), :]
                    else:
                        tile = recv_y[pair, pl.ds(8 * a + k, size_x, stride=8), :]
                    tiles[a, b, 0, c], tiles[a, b, 1, c] = tile, z_shift(tile, 1)
        return tiles

    border = [None, None]
    for first in range(0, pairs, 2):
        group_pairs = range(first, min(first + 2, pairs))
        adjoints = [border_tiles(pair, 1) for pair in group_pairs]
        high, low = split(jnp.concatenate([beside([t[key] for t in adjoints]) for key in order], axis=0))
        product = (
            jnp.dot(border_hi[...], high, preferred_element_type=jnp.float32)
            + jnp.dot(border_hi[...], low, preferred_element_type=jnp.float32)
            + jnp.dot(border_lo[...], high, preferred_element_type=jnp.float32)
        )
        for parts in contract(product, [border_tiles(pair, 0) for pair in group_pairs]):
            border = [p if e is None else e + p for e, p in zip(border, parts)]
    for k in range(2):
        energy[pl.ds(k * cells + size_y - 1, size_x, stride=size_y), :] = border[k]

    solid = passive[...] == 1
    density = physical[...]
    raw = -(
        PENALTY_SCALE * density * density * energy[0:cells, :]
        - OMEGA_SQUARED * energy[cells : 2 * cells, :]
    )
    scaled[...] = jnp.where(solid, 0.0, raw) / weight_sum[...]

    pack_edges(scaled, 1)
    scaled_copies = edge_copies(1)
    edge_each(scaled_copies, lambda c, slot: c[slot].start())
    edge_each(design_copies, left)
    edge_receive(scaled_copies)
    assemble(scaled, 1)
    for x, tile in enumerate(stencil(wide_rows, size_x)):
        benefit[pl.ds(x * size_y, size_y), :] = -tile
    benefit_out = pltpu.make_async_copy(benefit, benefit_hbm, out_sem)
    benefit_out.start()

    value = design[...]
    gain = value * jnp.sqrt(jnp.maximum(benefit[...], 0.0))
    floor_value = jnp.where(solid, 1.0, jnp.maximum(value - MOVE_LIMIT, 0.0))
    ceiling = jnp.where(solid, 1.0, jnp.minimum(value + MOVE_LIMIT, 1.0))

    def candidate(inverse_root):
        return jnp.minimum(ceiling, jnp.maximum(floor_value, gain * inverse_root))

    def total_over_x(j):
        trial = candidate(INVERSE_MIDDLES[j])
        return functools.reduce(
            lambda p, q: p + q, [trial[x * size_y : (x + 1) * size_y] for x in range(size_x)]
        )

    volumes = []
    for first in range(0, TRIALS, 8):
        tiles = [
            total_over_x(j) if j < TRIALS - 1 else jnp.zeros((8, size_z), jnp.float32)
            for j in range(first, first + 8)
        ]
        reach = 4
        while reach:
            lower = (slot_row & reach) == 0
            tiles = [
                jnp.where(lower, p, q)
                + jnp.where(lower, pltpu.roll(p, 8 - reach, 0), pltpu.roll(q, reach, 0))
                for p, q in zip(tiles[:reach], tiles[reach:])
            ]
            reach //= 2
        volumes.append(tiles[0])
    volumes = jnp.concatenate(volumes, axis=0)

    for q in range(ny):
        packed = jnp.zeros((group_rows, size_z), jnp.float32)
        for g in range(ny):
            part = volumes[g * group_rows : (g + 1) * group_rows]
            turn = (width * (g - q)) % size_z
            if turn:
                part = pltpu.roll(part, turn, 1)
            packed = jnp.where(group == g, part, packed)
        share_send[q] = packed
    share_recv[pl.ds(iy, 1)] = share_send[pl.ds(iy, 1)]
    pending = []

    def along(count, me, place, source, buffer, send_sem, recv_sem):
        copies = []
        for step in range(1, count):
            peer = lax.rem(me + step, count)
            copy = pltpu.make_async_remote_copy(
                src_ref=source(peer),
                dst_ref=buffer.at[me],
                send_sem=send_sem.at[step],
                recv_sem=recv_sem.at[step],
                device_id=place(peer),
                device_id_type=MESH,
            )
            copy.start()
            copies.append(copy)
        for copy in copies:
            copy.wait_recv()
        pending.extend(copies)

    along(ny, iy, lambda at: (ix, at), lambda at: share_send.at[at], share_recv, share_send_sem, share_recv_sem)
    share = functools.reduce(lambda p, q: p + q, [share_recv[k] for k in range(ny)])
    gather_x[pl.ds(ix, 1)] = share[None]
    along(nx, ix, lambda at: (at, iy), lambda at: gather_x.at[ix], gather_x, gx_send_sem, gx_recv_sem)
    share = functools.reduce(lambda p, q: p + q, [gather_x[k] for k in range(nx)])

    reach = 1
    while reach < band:
        share = share + jnp.where(
            (lane // reach) % 2 == 0,
            pltpu.roll(share, size_z - reach, 1),
            pltpu.roll(share, reach, 1),
        )
        reach *= 2
    chosen = jnp.where(share > own_target[0:1], leaf_table[...], INVERSE_LEAVES[0])
    chosen = jnp.min(chosen, axis=0, keepdims=True)
    reach = width
    while reach < size_z:
        chosen = jnp.minimum(chosen, pltpu.roll(chosen, reach, 1))
        reach *= 2
    gather_y[pl.ds(iy, 1)] = jnp.broadcast_to(chosen, (8, size_z))[None]
    along(ny, iy, lambda at: (ix, at), lambda at: gather_y.at[iy], gather_y, gy_send_sem, gy_recv_sem)
    multiplier = gather_y[0]
    for q in range(1, ny):
        multiplier = jnp.where(lane8 // width == q, gather_y[q], multiplier)
    chosen_out[...] = multiplier
    benefit_out.wait()

    edge_each(scaled_copies, lambda c, slot: c[slot].wait_send())
    for copy in pending:
        copy.wait_send()


def closing_kernel(negated, inverse_root, design, passive, sensitivity, design_next):
    benefit, value = negated[...], design[...]
    sensitivity[...] = -benefit
    trial = value * jnp.sqrt(jnp.maximum(benefit, 0.0)) * inverse_root[0:1, :]
    low = jnp.maximum(value - MOVE_LIMIT, 0.0)
    high = jnp.minimum(value + MOVE_LIMIT, 1.0)
    design_next[...] = jnp.where(passive[...] == 1, 1.0, jnp.minimum(high, jnp.maximum(low, trial)))


def shards(nx, ny, design, passive, basis_pairs, supports, stiffness, mass_matrix, volume_fraction):
    size_x, size_y, size_z = design.shape
    pairs = basis_pairs.shape[0]
    regions = volume_fraction.shape[0]
    cells = size_x * size_y
    fields_n = 6 * pairs
    flat = (cells, size_z)
    vmem = pl.BlockSpec(memory_space=pltpu.VMEM)
    f32, bf16 = jnp.float32, jnp.bfloat16
    dma = pltpu.SemaphoreType.DMA
    negated, inverse_root = pl.pallas_call(
        functools.partial(kernel, nx, ny, size_x, size_y, size_z, pairs, regions),
        out_shape=(jax.ShapeDtypeStruct(flat, f32), jax.ShapeDtypeStruct((size_y, size_z), f32)),
        in_specs=[pl.BlockSpec(memory_space=pltpu.HBM)] * 7,
        out_specs=(pl.BlockSpec(memory_space=pltpu.HBM), vmem),
        scratch_shapes=[
            pltpu.VMEM(flat, f32),
            pltpu.VMEM(flat, f32),
            pltpu.VMEM(flat, jnp.int32),
            pltpu.VMEM((fields_n, cells, size_z), f32),
            pltpu.VMEM(flat, jnp.int32),
            pltpu.VMEM(stiffness.shape, f32),
            pltpu.VMEM(mass_matrix.shape, f32),
            pltpu.VMEM((regions,), f32),
            pltpu.VMEM((fields_n, (size_x + 1) * 2 * size_y, size_z), f32),
            pltpu.VMEM((fields_n, size_y, size_z), f32),
            pltpu.VMEM((pairs, 8 * size_x, size_z), f32),
            pltpu.VMEM((fields_n, size_y, size_z), f32),
            pltpu.VMEM((pairs, 8 * (size_x + 1), size_z), f32),
            pltpu.VMEM((2, 4, 2, size_x, size_z), f32),
            pltpu.VMEM((2, 8, 2, size_y, size_z), f32),
            pltpu.VMEM(((size_x + 4) * 3 * size_y, size_z), f32),
            pltpu.VMEM(flat, f32),
            pltpu.VMEM((48 * size_y, 24 * size_y), bf16),
            pltpu.VMEM((48 * size_y, 12 * size_y), bf16),
            pltpu.VMEM((48 * size_y, 24 * size_y), bf16),
            pltpu.VMEM((48 * size_y, 24 * size_y), bf16),
            pltpu.VMEM(flat, f32),
            pltpu.VMEM(flat, f32),
            pltpu.VMEM((2 * cells, size_z), f32),
            pltpu.VMEM((ny, TRIALS // ny, size_z), f32),
            pltpu.VMEM((ny, TRIALS // ny, size_z), f32),
            pltpu.VMEM((nx, TRIALS // ny, size_z), f32),
            pltpu.VMEM((ny, 8, size_z), f32),
            pltpu.VMEM((TRIALS // ny, size_z), f32),
            dma((7,)),
            dma,
            dma((3,)),
            dma((3,)),
            dma((2, 8)),
            dma((2, 8)),
            dma((ny,)),
            dma((ny,)),
            dma((nx,)),
            dma((nx,)),
            dma((ny,)),
            dma((ny,)),
        ],
        compiler_params=pltpu.CompilerParams(
            collective_id=0, has_side_effects=True, vmem_limit_bytes=64 * 1024 * 1024
        ),
        name="sensitivity_update",
    )(
        design.reshape(flat),
        passive.reshape(flat),
        basis_pairs.reshape(fields_n, cells, size_z),
        supports.reshape(flat),
        stiffness,
        mass_matrix,
        volume_fraction,
    )
    sensitivity, design_next = pl.pallas_call(
        closing_kernel,
        out_shape=(jax.ShapeDtypeStruct(flat, f32), jax.ShapeDtypeStruct(flat, f32)),
        in_specs=[vmem] * 4,
        out_specs=(vmem, vmem),
        compiler_params=pltpu.CompilerParams(vmem_limit_bytes=64 * 1024 * 1024),
        name="design_update",
    )(negated, inverse_root, design.reshape(flat), passive.reshape(flat))
    return sensitivity.reshape(design.shape), design_next.reshape(design.shape)


def solution(mesh):
    placed = (
        P("gx", "gy", None),
        P("gx", "gy", None),
        P(None, None, None, "gx", "gy", None),
        P("gx", "gy", None),
        P(),
        P(),
        P(),
    )
    return jax.shard_map(
        functools.partial(shards, mesh.shape["gx"], mesh.shape["gy"]),
        mesh=mesh,
        in_specs=placed,
        out_specs=(P("gx", "gy", None), P("gx", "gy", None)),
        check_vma=False,
    )
```

```python
import functools
import math

import jax
import jax.numpy as jnp
import numpy as np
from jax import lax
from jax.experimental import pallas as pl
from jax.experimental.pallas import tpu as pltpu
from jax.sharding import PartitionSpec as P

PENALTY_SCALE = 3.0 * (1.0 - 0.001)
OMEGA_SQUARED = 0.5
MOVE_LIMIT = 0.2
BISECT = 6
TRIALS = 2**BISECT
CHUNK = 4
MESH = pl.DeviceIdType.MESH
AROUND = ((-1, 0), (1, 0), (0, -1), (0, 1), (-1, -1), (-1, 1), (1, -1), (1, 1))


def tree_ends():
    ends = [np.float32(1e-4), np.float32(1e4)]
    for _ in range(BISECT):
        inner = [np.sqrt(p * q) for p, q in zip(ends, ends[1:])]
        ends = [ends[0]] + [e for pair in zip(inner, ends[1:]) for e in pair]
    return ends


ENDS = tree_ends()
INVERSE_MIDDLES = [float(np.float32(1.0) / np.sqrt(e)) for e in ENDS[1:-1]]
INVERSE_LEAVES = [
    float(np.float32(1.0) / np.sqrt(np.sqrt(p * q))) for p, q in zip(ENDS, ENDS[1:])
]


def opposite(slot):
    dx, dy = AROUND[slot]
    return AROUND.index((-dx, -dy))


def z_shift(value, step):
    axis = value.ndim - 1
    size = value.shape[axis]
    lane = lax.broadcasted_iota(jnp.int32, value.shape, axis)
    moved = pltpu.roll(value, (-step) % size, axis)
    keep = lane < size - step if step > 0 else lane >= -step
    return jnp.where(keep, moved, 0.0)


def fold_plane(tiles):
    folded_y = (tiles[2], tiles[1] + tiles[3], tiles[0] + tiles[4])
    parts = [[], [], []]
    for cy, tile in enumerate(folded_y):
        folded_z = (
            tile,
            z_shift(tile, 1) + z_shift(tile, -1),
            z_shift(tile, 2) + z_shift(tile, -2),
        )
        for cz, entry in enumerate(folded_z):
            for cx in range(3):
                weight = 3.0 - math.sqrt(cx * cx + cy * cy + cz * cz)
                if weight > 0.0:
                    parts[cx].append(weight * entry)
    return [functools.reduce(lambda a, b: a + b, part) for part in parts]


def stencil(rows_at, size_x):
    planes = [
        fold_plane([rows_at(plane, oy) for oy in range(-2, 3)]) for plane in range(size_x + 4)
    ]
    spread = [[plane[cx] for plane in planes] for cx in range(3)]
    return [
        spread[0][i + 2]
        + (spread[1][i + 1] + spread[1][i + 3])
        + (spread[2][i] + spread[2][i + 4])
        for i in range(size_x)
    ]


def kernel(
    nx, ny, size_x, size_y, size_z, pairs, regions,
    design_hbm, passive_hbm, basis_hbm, supports_hbm, stiffness_hbm, mass_hbm, fraction_hbm,
    benefit_hbm, chosen_out,
    benefit, design, passive, basis, supports, stiffness, mass_matrix, fraction,
    fields, send_x, send_y, recv_x, recv_y,
    edge_send, edge_recv, wide, scaled, weights_hi, weights_lo, border_hi, border_lo, weight_sum, physical, energy,
    share_send, share_recv, gather_x, gather_y, leaf_table,
    load_sem, out_sem,
    basis_send_sem, basis_recv_sem, halo_send_sem, halo_recv_sem,
    share_send_sem, share_recv_sem, gx_send_sem, gx_recv_sem, gy_send_sem, gy_recv_sem,
):
    ix, iy = lax.axis_index("gx"), lax.axis_index("gy")
    pitch = 2 * size_y
    cells = size_x * size_y

    def there(dx, dy):
        return (
            (ix + dx >= 0) & (ix + dx < nx) & (iy + dy >= 0) & (iy + dy < ny)
        )

    edge_recv[...] = jnp.zeros(edge_recv.shape, jnp.float32)
    recv_x[...] = jnp.zeros(recv_x.shape, jnp.float32)
    recv_y[...] = jnp.zeros(recv_y.shape, jnp.float32)
    barrier = pltpu.get_barrier_semaphore()
    for step in range(1, ny):
        pl.semaphore_signal(barrier, inc=1, device_id=(ix, lax.rem(iy + step, ny)), device_id_type=MESH)
    for step in range(1, nx):
        pl.semaphore_signal(barrier, inc=1, device_id=(lax.rem(ix + step, nx), iy), device_id_type=MESH)
    for dx, dy in AROUND[4:]:
        @pl.when(there(dx, dy))
        def _(dx=dx, dy=dy):
            pl.semaphore_signal(barrier, inc=1, device_id=(ix + dx, iy + dy), device_id_type=MESH)
    corners = sum(there(dx, dy).astype(jnp.int32) for dx, dy in AROUND[4:])

    loads = [
        pltpu.make_async_copy(src, dst, load_sem.at[k])
        for k, (src, dst) in enumerate((
            (supports_hbm, supports), (basis_hbm, basis), (design_hbm, design), (passive_hbm, passive),
            (stiffness_hbm, stiffness), (mass_hbm, mass_matrix), (fraction_hbm, fraction),
        ))
    ]
    for load in loads:
        load.start()
    send_y[...] = jnp.zeros(send_y.shape, jnp.float32)
    for load in loads[:2]:
        load.wait()

    free = 1.0 - supports[...].astype(jnp.float32)
    send_x[...] = basis[:, 0:size_y, :] * free[0:size_y][None]
    free_y = 1.0 - supports[pl.ds(0, size_x, stride=size_y), :].astype(jnp.float32)
    for f in range(6 * pairs):
        rows = basis[f, pl.ds(0, size_x, stride=size_y), :] * free_y
        send_y[f // 6, pl.ds(f % 6, size_x, stride=8), :] = rows

    def pack_edges(source, which):
        for x in range(2):
            edge_send[which, 2, x] = source[pl.ds(x * size_y, size_y), :]
            edge_send[which, 3, x] = source[pl.ds((size_x - 2 + x) * size_y, size_y), :]
        for y in range(2):
            edge_send[which, 0, y] = source[pl.ds(y, size_x, stride=size_y), :]
            edge_send[which, 1, y] = source[pl.ds(size_y - 2 + y, size_x, stride=size_y), :]

    def edge_copies(which):
        copies = []
        for slot, (dx, dy) in enumerate(AROUND):
            if dy == 0:
                src = edge_send.at[which, 2 if dx < 0 else 3]
            else:
                src = edge_send.at[which, 0 if dy < 0 else 1]
            copies.append(pltpu.make_async_remote_copy(
                src_ref=src,
                dst_ref=edge_recv.at[which, opposite(slot)],
                send_sem=halo_send_sem.at[which, slot],
                recv_sem=halo_recv_sem.at[which, opposite(slot)],
                device_id=(ix + dx, iy + dy),
                device_id_type=MESH,
            ))
        return copies

    def edge_each(copies, act):
        for slot, (dx, dy) in enumerate(AROUND):
            @pl.when(there(dx, dy))
            def _(slot=slot):
                act(copies, slot)

    def edge_receive(copies):
        edge_each(copies, lambda c, slot: c[opposite(slot)].wait_recv())

    span = 3 * size_y

    def assemble(source, which):
        for x in range(size_x):
            wide[pl.ds((x + 2) * span + size_y, size_y), :] = source[pl.ds(x * size_y, size_y), :]
        for x in range(2):
            wide[pl.ds(x * span + size_y, size_y), :] = edge_recv[which, 0, x]
            wide[pl.ds((size_x + 2 + x) * span + size_y, size_y), :] = edge_recv[which, 1, x]
        for y in range(2):
            low, high = size_y - 2 + y, 2 * size_y + y
            wide[pl.ds(2 * span + low, size_x, stride=span), :] = edge_recv[which, 2, y]
            wide[pl.ds(2 * span + high, size_x, stride=span), :] = edge_recv[which, 3, y]
            for x in range(2):
                for slot, row in ((4, low), (5, high)):
                    wide[pl.ds(x * span + row, 1), :] = edge_recv[which, slot, y, size_x - 2 + x : size_x - 1 + x, :]
                for slot, row in ((6, low), (7, high)):
                    wide[pl.ds((size_x + 2 + x) * span + row, 1), :] = edge_recv[which, slot, y, x : x + 1, :]

    def wide_rows(plane, oy):
        return wide[pl.ds(plane * span + size_y + oy, size_y), :]

    loads[2].wait()
    pack_edges(design, 0)

    pl.semaphore_wait(barrier, (nx - 1) + (ny - 1) + corners)

    design_copies = edge_copies(0)
    basis_copies = {
        slot: pltpu.make_async_remote_copy(
            src_ref=src,
            dst_ref=dst,
            send_sem=basis_send_sem.at[k],
            recv_sem=basis_recv_sem.at[k],
            device_id=(ix + AROUND[slot][0], iy + AROUND[slot][1]),
            device_id_type=MESH,
        )
        for k, (slot, src, dst) in enumerate((
            (0, send_x, recv_x),
            (2, send_y, recv_y.at[:, pl.ds(0, 8 * size_x)]),
            (4, send_y.at[:, pl.ds(0, 8)], recv_y.at[:, pl.ds(8 * size_x, 8)]),
        ))
    }

    def leave(copies, slot):
        if slot in basis_copies:
            basis_copies[slot].start()
        copies[slot].start()

    def left(copies, slot):
        if slot in basis_copies:
            basis_copies[slot].wait_send()
        copies[slot].wait_send()

    edge_each(design_copies, leave)
    for load in loads[3:]:
        load.wait()

    grid_x, grid_y = nx * size_x, ny * size_y
    wide_n, narrow_n, depth = 24 * size_y, 24, 12 * size_y
    bits_y = size_y.bit_length() - 1

    def spread_rows(shape, row_dim):
        at = lax.broadcasted_iota(jnp.int32, shape, row_dim)
        return lax.shift_right_logical(at, bits_y) == lax.broadcasted_iota(jnp.int32, shape, 1 - row_dim)

    col = lax.broadcasted_iota(jnp.int32, (narrow_n, depth), 1)
    tile_of = lax.shift_right_logical(col, bits_y)
    corner = lax.shift_right_logical(tile_of * 11, 5)
    component = tile_of - 3 * corner
    source_row = 12 * lax.shift_right_logical(corner, 1) + 3 * (corner & 1) + component
    at_row = lax.broadcasted_iota(jnp.int32, (narrow_n, depth), 0)
    gather = [
        (at_row == source_row + 6 * b).astype(jnp.float32).astype(jnp.bfloat16)
        for b in range(2)
    ]
    at_y = lax.broadcasted_iota(jnp.int32, (wide_n, depth), 0) & (size_y - 1)
    col_y = lax.broadcasted_iota(jnp.int32, (wide_n, depth), 1) & (size_y - 1)
    keep = [col_y == at_y, col_y == at_y + 1]
    same = (
        lax.broadcasted_iota(jnp.int32, (wide_n, wide_n), 0) & (size_y - 1)
    ) == (lax.broadcasted_iota(jnp.int32, (wide_n, wide_n), 1) & (size_y - 1))

    pieces = []
    for matrix in (stiffness, mass_matrix):
        value = matrix[...]
        high = value.astype(jnp.bfloat16).astype(jnp.float32)
        pieces += [high, value - high]
    pieces = jnp.concatenate(pieces, axis=0).astype(jnp.bfloat16)
    expand = spread_rows((4 * wide_n, 4 * narrow_n), 0).astype(jnp.float32).astype(jnp.bfloat16)
    tall = jnp.dot(expand, pieces, preferred_element_type=jnp.float32).astype(jnp.bfloat16)
    plain_gather = spread_rows((narrow_n, wide_n), 1).astype(jnp.float32).astype(jnp.bfloat16)
    banded_full = [jnp.dot(tall, g, preferred_element_type=jnp.float32) for g in gather]
    plain_full = jnp.dot(tall, plain_gather, preferred_element_type=jnp.float32)
    for k in range(2):
        at = pl.ds(k * wide_n, wide_n)
        for half in range(2):
            rows = slice((2 * k + half) * wide_n, (2 * k + half + 1) * wide_n)
            banded = jnp.where(
                keep[0], banded_full[0][rows], jnp.where(keep[1], banded_full[1][rows], 0.0)
            ).astype(jnp.bfloat16)
            plain = jnp.where(same, plain_full[rows], 0.0).astype(jnp.bfloat16)
            if half == 0:
                weights_hi[at, :] = jnp.concatenate([banded, banded], axis=1)
                border_hi[at, :] = plain
            else:
                weights_lo[at, :] = banded
                border_lo[at, :] = plain

    for x in range(size_x + 1):
        fields[:, x * pitch + size_y : (x + 1) * pitch, :] = jnp.zeros((6 * pairs, size_y, size_z), jnp.float32)
    for x in range(size_x):
        fields[:, x * pitch : x * pitch + size_y, :] = (
            basis[:, x * size_y : (x + 1) * size_y, :] * free[x * size_y : (x + 1) * size_y][None]
        )

    row_y = lax.broadcasted_iota(jnp.int32, (size_y, size_z), 0)

    def inside_y(oy):
        at_y = row_y + (iy * size_y + oy)
        return jnp.where((at_y >= 0) & (at_y < grid_y), 1.0, 0.0)

    def inside_x(plane):
        at_x = jnp.full((size_y, size_z), ix * size_x + plane - 2, jnp.int32)
        return jnp.where((at_x >= 0) & (at_x < grid_x), 1.0, 0.0)

    share_of = fold_plane([inside_y(oy) for oy in range(-2, 3)])
    flags = [inside_x(plane) for plane in range(size_x + 4)]
    for x in range(size_x):
        weight_sum[pl.ds(x * size_y, size_y), :] = (
            share_of[0]
            + (flags[x + 1] + flags[x + 3]) * share_of[1]
            + (flags[x] + flags[x + 4]) * share_of[2]
        )

    energy[...] = jnp.zeros((2 * cells, size_z), jnp.float32)
    order = [(a, b, d, c) for a in range(2) for b in range(2) for d in range(2) for c in range(3)]

    def beside(tiles):
        return tiles[0] if len(tiles) == 1 else jnp.concatenate(tiles, axis=1)

    def split(operand):
        high = operand.astype(jnp.bfloat16)
        return high, (operand - high.astype(jnp.float32)).astype(jnp.bfloat16)

    def contract(product, states):
        return [
            [
                functools.reduce(
                    lambda p, q: p + q,
                    [
                        state[key] * product[
                            k * wide_n + r * size_y : k * wide_n + (r + 1) * size_y,
                            n * size_z : (n + 1) * size_z,
                        ]
                        for r, key in enumerate(order)
                    ],
                )
                for k in range(2)
            ]
            for n, state in enumerate(states)
        ]

    def own_columns(columns):
        adjoint, state = {}, {}
        for pair, x in columns:
            for c in range(3):
                for at_x in (x, x + 1):
                    key = (pair, at_x, c)
                    if key in adjoint:
                        continue
                    tile = fields[pair * 6 + 3 + c, at_x * pitch : at_x * pitch + size_y, :]
                    adjoint[key] = (tile, z_shift(tile, 1))
                    for b in range(2):
                        tile = fields[pair * 6 + c, at_x * pitch + b : at_x * pitch + b + size_y, :]
                        state[key + (b,)] = (tile, z_shift(tile, 1))
        high, low = split(jnp.concatenate(
            [
                beside([adjoint[pair, x + a, c][d] for pair, x in columns])
                for a in range(2) for d in range(2) for c in range(3)
            ],
            axis=0,
        ))
        product = jnp.dot(
            weights_hi[...], jnp.concatenate([high, low], axis=0), preferred_element_type=jnp.float32
        ) + jnp.dot(weights_lo[...], high, preferred_element_type=jnp.float32)
        states = [
            {(a, b, d, c): state[pair, x + a, c, b][d] for a, b, d, c in order} for pair, x in columns
        ]
        for (pair, x), parts in zip(columns, contract(product, states)):
            for k, part in enumerate(parts):
                at = pl.ds((k * size_x + x) * size_y, size_y)
                energy[at, :] = energy[at, :] + part

    for pair in range(pairs):
        for first in range(0, size_x - 1, CHUNK):
            own_columns([(pair, x) for x in range(first, min(first + CHUNK, size_x - 1))])

    edge_receive(design_copies)
    assemble(design, 0)
    for x, tile in enumerate(stencil(wide_rows, size_x)):
        at = pl.ds(x * size_y, size_y)
        physical[at, :] = jnp.where(passive[at, :] == 1, 1.0, tile / weight_sum[at, :])

    for slot in basis_copies:
        dx, dy = AROUND[slot]

        @pl.when(there(-dx, -dy))
        def _(slot=slot):
            basis_copies[slot].wait_recv()

    fields[:, size_x * pitch : size_x * pitch + size_y, :] = recv_x[...]
    for first in range(0, pairs, CHUNK):
        own_columns([(pair, size_x - 1) for pair in range(first, min(first + CHUNK, pairs))])

    def border_tiles(pair, member):
        tiles = {}
        for c in range(3):
            f, k = pair * 6 + member * 3 + c, member * 3 + c
            for a in range(2):
                for b in range(2):
                    if b == 0:
                        tile = fields[f, pl.ds(a * pitch + size_y - 1, size_x, stride=pitch), :]
                    else:
                        tile = recv_y[pair, pl.ds(8 * a + k, size_x, stride=8), :]
                    tiles[a, b, 0, c], tiles[a, b, 1, c] = tile, z_shift(tile, 1)
        return tiles

    border = [None, None]
    for first in range(0, pairs, CHUNK):
        group_pairs = range(first, min(first + CHUNK, pairs))
        adjoints = [border_tiles(pair, 1) for pair in group_pairs]
        high, low = split(jnp.concatenate([beside([t[key] for t in adjoints]) for key in order], axis=0))
        product = (
            jnp.dot(border_hi[...], high, preferred_element_type=jnp.float32)
            + jnp.dot(border_hi[...], low, preferred_element_type=jnp.float32)
            + jnp.dot(border_lo[...], high, preferred_element_type=jnp.float32)
        )
        for parts in contract(product, [border_tiles(pair, 0) for pair in group_pairs]):
            border = [p if e is None else e + p for e, p in zip(border, parts)]
    for k in range(2):
        energy[pl.ds(k * cells + size_y - 1, size_x, stride=size_y), :] = border[k]

    solid = passive[...] == 1
    density = physical[...]
    raw = -(
        PENALTY_SCALE * density * density * energy[0:cells, :]
        - OMEGA_SQUARED * energy[cells : 2 * cells, :]
    )
    scaled[...] = jnp.where(solid, 0.0, raw) / weight_sum[...]

    pack_edges(scaled, 1)
    scaled_copies = edge_copies(1)
    edge_each(scaled_copies, lambda c, slot: c[slot].start())
    edge_each(design_copies, left)

    band = size_z // regions
    width, group_rows = size_z // ny, TRIALS // ny
    lane = lax.broadcasted_iota(jnp.int32, (group_rows, size_z), 1)
    lane8 = lax.broadcasted_iota(jnp.int32, (8, size_z), 1)
    slot_row = lax.broadcasted_iota(jnp.int32, (8, size_z), 0)
    group = lane // width
    pick = (
        lax.broadcasted_iota(jnp.int32, (regions, size_z), 1) // band
        == lax.broadcasted_iota(jnp.int32, (regions, size_z), 0)
    ).astype(jnp.float32).astype(jnp.bfloat16)
    rest = jnp.broadcast_to(fraction[...].reshape(1, regions), (8, regions))
    target = jnp.zeros((8, size_z), jnp.float32)
    for _ in range(3):
        piece = rest.astype(jnp.bfloat16)
        target = target + jnp.dot(piece, pick, preferred_element_type=jnp.float32)
        rest = rest - piece.astype(jnp.float32)
    target = target * float(grid_x * grid_y * band)
    own_target = jnp.where(lane8 // width == iy, target, 0.0)
    reach = width
    while reach < size_z:
        own_target = own_target + pltpu.roll(own_target, reach, 1)
        reach *= 2
    for r in range(group_rows):
        line = jnp.full((1, size_z), INVERSE_LEAVES[0], jnp.float32)
        for g in range(ny):
            j = min(g * group_rows + r + 1, TRIALS - 1)
            line = jnp.where(lane8[0:1] // width == g, INVERSE_LEAVES[j], line)
        leaf_table[pl.ds(r, 1), :] = line

    edge_receive(scaled_copies)
    assemble(scaled, 1)
    for x, tile in enumerate(stencil(wide_rows, size_x)):
        benefit[pl.ds(x * size_y, size_y), :] = -tile
    benefit_out = pltpu.make_async_copy(benefit, benefit_hbm, out_sem)
    benefit_out.start()

    value = design[...]
    gain = value * jnp.sqrt(jnp.maximum(benefit[...], 0.0))
    floor_value = jnp.where(solid, 1.0, jnp.maximum(value - MOVE_LIMIT, 0.0))
    ceiling = jnp.where(solid, 1.0, jnp.minimum(value + MOVE_LIMIT, 1.0))

    def candidate(inverse_root):
        return jnp.minimum(ceiling, jnp.maximum(floor_value, gain * inverse_root))

    def total_over_x(j):
        trial = candidate(INVERSE_MIDDLES[j])
        return functools.reduce(
            lambda p, q: p + q, [trial[x * size_y : (x + 1) * size_y] for x in range(size_x)]
        )

    volumes = []
    for first in range(0, TRIALS, 8):
        tiles = [
            total_over_x(j) if j < TRIALS - 1 else jnp.zeros((8, size_z), jnp.float32)
            for j in range(first, first + 8)
        ]
        reach = 4
        while reach:
            lower = (slot_row & reach) == 0
            tiles = [
                jnp.where(lower, p, q)
                + jnp.where(lower, pltpu.roll(p, 8 - reach, 0), pltpu.roll(q, reach, 0))
                for p, q in zip(tiles[:reach], tiles[reach:])
            ]
            reach //= 2
        volumes.append(tiles[0])
    volumes = jnp.concatenate(volumes, axis=0)

    for q in range(ny):
        packed = jnp.zeros((group_rows, size_z), jnp.float32)
        for g in range(ny):
            part = volumes[g * group_rows : (g + 1) * group_rows]
            turn = (width * (g - q)) % size_z
            if turn:
                part = pltpu.roll(part, turn, 1)
            packed = jnp.where(group == g, part, packed)
        share_send[q] = packed
    share_recv[pl.ds(iy, 1)] = share_send[pl.ds(iy, 1)]
    pending = []

    def along(count, me, place, source, buffer, send_sem, recv_sem):
        copies = []
        for step in range(1, count):
            peer = lax.rem(me + step, count)
            copy = pltpu.make_async_remote_copy(
                src_ref=source(peer),
                dst_ref=buffer.at[me],
                send_sem=send_sem.at[step],
                recv_sem=recv_sem.at[step],
                device_id=place(peer),
                device_id_type=MESH,
            )
            copy.start()
            copies.append(copy)
        for copy in copies:
            copy.wait_recv()
        pending.extend(copies)

    along(ny, iy, lambda at: (ix, at), lambda at: share_send.at[at], share_recv, share_send_sem, share_recv_sem)
    share = functools.reduce(lambda p, q: p + q, [share_recv[k] for k in range(ny)])
    gather_x[pl.ds(ix, 1)] = share[None]
    along(nx, ix, lambda at: (at, iy), lambda at: gather_x.at[ix], gather_x, gx_send_sem, gx_recv_sem)
    share = functools.reduce(lambda p, q: p + q, [gather_x[k] for k in range(nx)])

    reach = 1
    while reach < band:
        share = share + jnp.where(
            (lane // reach) % 2 == 0,
            pltpu.roll(share, size_z - reach, 1),
            pltpu.roll(share, reach, 1),
        )
        reach *= 2
    chosen = jnp.where(share > own_target[0:1], leaf_table[...], INVERSE_LEAVES[0])
    chosen = jnp.min(chosen, axis=0, keepdims=True)
    reach = width
    while reach < size_z:
        chosen = jnp.minimum(chosen, pltpu.roll(chosen, reach, 1))
        reach *= 2
    gather_y[pl.ds(iy, 1)] = jnp.broadcast_to(chosen, (8, size_z))[None]
    along(ny, iy, lambda at: (ix, at), lambda at: gather_y.at[iy], gather_y, gy_send_sem, gy_recv_sem)
    multiplier = gather_y[0]
    for q in range(1, ny):
        multiplier = jnp.where(lane8 // width == q, gather_y[q], multiplier)
    chosen_out[...] = multiplier
    benefit_out.wait()

    edge_each(scaled_copies, lambda c, slot: c[slot].wait_send())
    for copy in pending:
        copy.wait_send()


def closing_kernel(negated, inverse_root, design, passive, sensitivity, design_next):
    benefit, value = negated[...], design[...]
    sensitivity[...] = -benefit
    trial = value * jnp.sqrt(jnp.maximum(benefit, 0.0)) * inverse_root[0:1, :]
    low = jnp.maximum(value - MOVE_LIMIT, 0.0)
    high = jnp.minimum(value + MOVE_LIMIT, 1.0)
    design_next[...] = jnp.where(passive[...] == 1, 1.0, jnp.minimum(high, jnp.maximum(low, trial)))


def shards(nx, ny, design, passive, basis_pairs, supports, stiffness, mass_matrix, volume_fraction):
    size_x, size_y, size_z = design.shape
    pairs = basis_pairs.shape[0]
    regions = volume_fraction.shape[0]
    cells = size_x * size_y
    fields_n = 6 * pairs
    flat = (cells, size_z)
    vmem = pl.BlockSpec(memory_space=pltpu.VMEM)
    f32, bf16 = jnp.float32, jnp.bfloat16
    dma = pltpu.SemaphoreType.DMA
    negated, inverse_root = pl.pallas_call(
        functools.partial(kernel, nx, ny, size_x, size_y, size_z, pairs, regions),
        out_shape=(jax.ShapeDtypeStruct(flat, f32), jax.ShapeDtypeStruct((size_y, size_z), f32)),
        in_specs=[pl.BlockSpec(memory_space=pltpu.HBM)] * 7,
        out_specs=(pl.BlockSpec(memory_space=pltpu.HBM), vmem),
        scratch_shapes=[
            pltpu.VMEM(flat, f32),
            pltpu.VMEM(flat, f32),
            pltpu.VMEM(flat, jnp.int32),
            pltpu.VMEM((fields_n, cells, size_z), f32),
            pltpu.VMEM(flat, jnp.int32),
            pltpu.VMEM(stiffness.shape, f32),
            pltpu.VMEM(mass_matrix.shape, f32),
            pltpu.VMEM((regions,), f32),
            pltpu.VMEM((fields_n, (size_x + 1) * 2 * size_y, size_z), f32),
            pltpu.VMEM((fields_n, size_y, size_z), f32),
            pltpu.VMEM((pairs, 8 * size_x, size_z), f32),
            pltpu.VMEM((fields_n, size_y, size_z), f32),
            pltpu.VMEM((pairs, 8 * (size_x + 1), size_z), f32),
            pltpu.VMEM((2, 4, 2, size_x, size_z), f32),
            pltpu.VMEM((2, 8, 2, size_y, size_z), f32),
            pltpu.VMEM(((size_x + 4) * 3 * size_y, size_z), f32),
            pltpu.VMEM(flat, f32),
            pltpu.VMEM((48 * size_y, 24 * size_y), bf16),
            pltpu.VMEM((48 * size_y, 12 * size_y), bf16),
            pltpu.VMEM((48 * size_y, 24 * size_y), bf16),
            pltpu.VMEM((48 * size_y, 24 * size_y), bf16),
            pltpu.VMEM(flat, f32),
            pltpu.VMEM(flat, f32),
            pltpu.VMEM((2 * cells, size_z), f32),
            pltpu.VMEM((ny, TRIALS // ny, size_z), f32),
            pltpu.VMEM((ny, TRIALS // ny, size_z), f32),
            pltpu.VMEM((nx, TRIALS // ny, size_z), f32),
            pltpu.VMEM((ny, 8, size_z), f32),
            pltpu.VMEM((TRIALS // ny, size_z), f32),
            dma((7,)),
            dma,
            dma((3,)),
            dma((3,)),
            dma((2, 8)),
            dma((2, 8)),
            dma((ny,)),
            dma((ny,)),
            dma((nx,)),
            dma((nx,)),
            dma((ny,)),
            dma((ny,)),
        ],
        compiler_params=pltpu.CompilerParams(
            collective_id=0, has_side_effects=True, vmem_limit_bytes=64 * 1024 * 1024
        ),
        name="sensitivity_update",
    )(
        design.reshape(flat),
        passive.reshape(flat),
        basis_pairs.reshape(fields_n, cells, size_z),
        supports.reshape(flat),
        stiffness,
        mass_matrix,
        volume_fraction,
    )
    sensitivity, design_next = pl.pallas_call(
        closing_kernel,
        out_shape=(jax.ShapeDtypeStruct(flat, f32), jax.ShapeDtypeStruct(flat, f32)),
        in_specs=[vmem] * 4,
        out_specs=(vmem, vmem),
        compiler_params=pltpu.CompilerParams(vmem_limit_bytes=64 * 1024 * 1024),
        name="design_update",
    )(negated, inverse_root, design.reshape(flat), passive.reshape(flat))
    return sensitivity.reshape(design.shape), design_next.reshape(design.shape)


def solution(mesh):
    placed = (
        P("gx", "gy", None),
        P("gx", "gy", None),
        P(None, None, None, "gx", "gy", None),
        P("gx", "gy", None),
        P(),
        P(),
        P(),
    )
    return jax.shard_map(
        functools.partial(shards, mesh.shape["gx"], mesh.shape["gy"]),
        mesh=mesh,
        in_specs=placed,
        out_specs=(P("gx", "gy", None), P("gx", "gy", None)),
        check_vma=False,
    )
```

```python
import functools
import math

import jax
import jax.numpy as jnp
import numpy as np
from jax import lax
from jax.experimental import pallas as pl
from jax.experimental.pallas import tpu as pltpu
from jax.sharding import PartitionSpec as P

PENALTY_SCALE = 3.0 * (1.0 - 0.001)
OMEGA_SQUARED = 0.5
MOVE_LIMIT = 0.2
BISECT = 6
TRIALS = 2**BISECT
CHUNK = 4
MESH = pl.DeviceIdType.MESH
AROUND = ((-1, 0), (1, 0), (0, -1), (0, 1), (-1, -1), (-1, 1), (1, -1), (1, 1))


def tree_ends():
    ends = [np.float32(1e-4), np.float32(1e4)]
    for _ in range(BISECT):
        inner = [np.sqrt(p * q) for p, q in zip(ends, ends[1:])]
        ends = [ends[0]] + [e for pair in zip(inner, ends[1:]) for e in pair]
    return ends


ENDS = tree_ends()
INVERSE_MIDDLES = [float(np.float32(1.0) / np.sqrt(e)) for e in ENDS[1:-1]]
INVERSE_LEAVES = [
    float(np.float32(1.0) / np.sqrt(np.sqrt(p * q))) for p, q in zip(ENDS, ENDS[1:])
]


def opposite(slot):
    dx, dy = AROUND[slot]
    return AROUND.index((-dx, -dy))


def z_shift(value, step):
    axis = value.ndim - 1
    size = value.shape[axis]
    lane = lax.broadcasted_iota(jnp.int32, value.shape, axis)
    moved = pltpu.roll(value, (-step) % size, axis)
    keep = lane < size - step if step > 0 else lane >= -step
    return jnp.where(keep, moved, 0.0)


def fold_plane(tiles):
    folded_y = (tiles[2], tiles[1] + tiles[3], tiles[0] + tiles[4])
    parts = [[], [], []]
    for cy, tile in enumerate(folded_y):
        folded_z = (
            tile,
            z_shift(tile, 1) + z_shift(tile, -1),
            z_shift(tile, 2) + z_shift(tile, -2),
        )
        for cz, entry in enumerate(folded_z):
            for cx in range(3):
                weight = 3.0 - math.sqrt(cx * cx + cy * cy + cz * cz)
                if weight > 0.0:
                    parts[cx].append(weight * entry)
    return [functools.reduce(lambda a, b: a + b, part) for part in parts]


def stencil(rows_at, size_x):
    planes = [
        fold_plane([rows_at(plane, oy) for oy in range(-2, 3)]) for plane in range(size_x + 4)
    ]
    spread = [[plane[cx] for plane in planes] for cx in range(3)]
    return [
        spread[0][i + 2]
        + (spread[1][i + 1] + spread[1][i + 3])
        + (spread[2][i] + spread[2][i + 4])
        for i in range(size_x)
    ]


def kernel(
    nx, ny, size_x, size_y, size_z, pairs, regions,
    design_hbm, passive_hbm, basis_hbm, supports_hbm, stiffness_hbm, mass_hbm, fraction_hbm,
    benefit_hbm, chosen_out,
    benefit, design, passive, basis, supports, stiffness, mass_matrix, fraction,
    fields, send_x, send_y, recv_x, recv_y,
    edge_send, edge_recv, wide, scaled, weights_hi, weights_lo, border_hi, border_lo, weight_sum, physical, energy,
    share_send, share_recv, gather_x, gather_y, leaf_table, middle_table, volume_table,
    load_sem, out_sem,
    basis_send_sem, basis_recv_sem, halo_send_sem, halo_recv_sem,
    share_send_sem, share_recv_sem, gx_send_sem, gx_recv_sem, gy_send_sem, gy_recv_sem,
):
    ix, iy = lax.axis_index("gx"), lax.axis_index("gy")
    pitch = 2 * size_y
    cells = size_x * size_y

    def there(dx, dy):
        return (
            (ix + dx >= 0) & (ix + dx < nx) & (iy + dy >= 0) & (iy + dy < ny)
        )

    edge_recv[...] = jnp.zeros(edge_recv.shape, jnp.float32)
    recv_x[...] = jnp.zeros(recv_x.shape, jnp.float32)
    recv_y[...] = jnp.zeros(recv_y.shape, jnp.float32)
    barrier = pltpu.get_barrier_semaphore()
    for step in range(1, ny):
        pl.semaphore_signal(barrier, inc=1, device_id=(ix, lax.rem(iy + step, ny)), device_id_type=MESH)
    for step in range(1, nx):
        pl.semaphore_signal(barrier, inc=1, device_id=(lax.rem(ix + step, nx), iy), device_id_type=MESH)
    for dx, dy in AROUND[4:]:
        @pl.when(there(dx, dy))
        def _(dx=dx, dy=dy):
            pl.semaphore_signal(barrier, inc=1, device_id=(ix + dx, iy + dy), device_id_type=MESH)
    corners = sum(there(dx, dy).astype(jnp.int32) for dx, dy in AROUND[4:])

    loads = [
        pltpu.make_async_copy(src, dst, load_sem.at[k])
        for k, (src, dst) in enumerate((
            (supports_hbm, supports), (basis_hbm, basis), (design_hbm, design), (passive_hbm, passive),
            (stiffness_hbm, stiffness), (mass_hbm, mass_matrix), (fraction_hbm, fraction),
        ))
    ]
    for load in loads:
        load.start()
    send_y[...] = jnp.zeros(send_y.shape, jnp.float32)
    for load in loads[:2]:
        load.wait()

    free = 1.0 - supports[...].astype(jnp.float32)
    send_x[...] = basis[:, 0:size_y, :] * free[0:size_y][None]
    free_y = 1.0 - supports[pl.ds(0, size_x, stride=size_y), :].astype(jnp.float32)
    for f in range(6 * pairs):
        rows = basis[f, pl.ds(0, size_x, stride=size_y), :] * free_y
        send_y[f // 6, pl.ds(f % 6, size_x, stride=8), :] = rows

    def pack_edges(source, which):
        for x in range(2):
            edge_send[which, 2, x] = source[pl.ds(x * size_y, size_y), :]
            edge_send[which, 3, x] = source[pl.ds((size_x - 2 + x) * size_y, size_y), :]
        for y in range(2):
            edge_send[which, 0, y] = source[pl.ds(y, size_x, stride=size_y), :]
            edge_send[which, 1, y] = source[pl.ds(size_y - 2 + y, size_x, stride=size_y), :]

    def edge_copies(which):
        copies = []
        for slot, (dx, dy) in enumerate(AROUND):
            if dy == 0:
                src = edge_send.at[which, 2 if dx < 0 else 3]
            else:
                src = edge_send.at[which, 0 if dy < 0 else 1]
            copies.append(pltpu.make_async_remote_copy(
                src_ref=src,
                dst_ref=edge_recv.at[which, opposite(slot)],
                send_sem=halo_send_sem.at[which, slot],
                recv_sem=halo_recv_sem.at[which, opposite(slot)],
                device_id=(ix + dx, iy + dy),
                device_id_type=MESH,
            ))
        return copies

    def edge_each(copies, act):
        for slot, (dx, dy) in enumerate(AROUND):
            @pl.when(there(dx, dy))
            def _(slot=slot):
                act(copies, slot)

    def edge_receive(copies):
        edge_each(copies, lambda c, slot: c[opposite(slot)].wait_recv())

    span = 3 * size_y

    def assemble(source, which):
        for x in range(size_x):
            wide[pl.ds((x + 2) * span + size_y, size_y), :] = source[pl.ds(x * size_y, size_y), :]
        for x in range(2):
            wide[pl.ds(x * span + size_y, size_y), :] = edge_recv[which, 0, x]
            wide[pl.ds((size_x + 2 + x) * span + size_y, size_y), :] = edge_recv[which, 1, x]
        for y in range(2):
            low, high = size_y - 2 + y, 2 * size_y + y
            wide[pl.ds(2 * span + low, size_x, stride=span), :] = edge_recv[which, 2, y]
            wide[pl.ds(2 * span + high, size_x, stride=span), :] = edge_recv[which, 3, y]
            for x in range(2):
                for slot, row in ((4, low), (5, high)):
                    wide[pl.ds(x * span + row, 1), :] = edge_recv[which, slot, y, size_x - 2 + x : size_x - 1 + x, :]
                for slot, row in ((6, low), (7, high)):
                    wide[pl.ds((size_x + 2 + x) * span + row, 1), :] = edge_recv[which, slot, y, x : x + 1, :]

    def wide_rows(plane, oy):
        return wide[pl.ds(plane * span + size_y + oy, size_y), :]

    loads[2].wait()
    pack_edges(design, 0)

    for load in loads[3:]:
        load.wait()

    grid_x, grid_y = nx * size_x, ny * size_y
    wide_n, narrow_n, depth = 24 * size_y, 24, 12 * size_y
    bits_y = size_y.bit_length() - 1

    def spread_rows(shape, row_dim):
        at = lax.broadcasted_iota(jnp.int32, shape, row_dim)
        return lax.shift_right_logical(at, bits_y) == lax.broadcasted_iota(jnp.int32, shape, 1 - row_dim)

    col = lax.broadcasted_iota(jnp.int32, (narrow_n, depth), 1)
    tile_of = lax.shift_right_logical(col, bits_y)
    corner = lax.shift_right_logical(tile_of * 11, 5)
    component = tile_of - 3 * corner
    source_row = 12 * lax.shift_right_logical(corner, 1) + 3 * (corner & 1) + component
    at_row = lax.broadcasted_iota(jnp.int32, (narrow_n, depth), 0)
    gather = [
        (at_row == source_row + 6 * b).astype(jnp.float32).astype(jnp.bfloat16)
        for b in range(2)
    ]
    at_y = lax.broadcasted_iota(jnp.int32, (wide_n, depth), 0) & (size_y - 1)
    col_y = lax.broadcasted_iota(jnp.int32, (wide_n, depth), 1) & (size_y - 1)
    keep = [col_y == at_y, col_y == at_y + 1]
    same = (
        lax.broadcasted_iota(jnp.int32, (wide_n, wide_n), 0) & (size_y - 1)
    ) == (lax.broadcasted_iota(jnp.int32, (wide_n, wide_n), 1) & (size_y - 1))

    pieces = []
    for matrix in (stiffness, mass_matrix):
        value = matrix[...]
        high = value.astype(jnp.bfloat16).astype(jnp.float32)
        pieces += [high, value - high]
    pieces = jnp.concatenate(pieces, axis=0).astype(jnp.bfloat16)
    expand = spread_rows((4 * wide_n, 4 * narrow_n), 0).astype(jnp.float32).astype(jnp.bfloat16)
    tall = jnp.dot(expand, pieces, preferred_element_type=jnp.float32).astype(jnp.bfloat16)
    plain_gather = spread_rows((narrow_n, wide_n), 1).astype(jnp.float32).astype(jnp.bfloat16)
    banded_full = [jnp.dot(tall, g, preferred_element_type=jnp.float32) for g in gather]
    plain_full = jnp.dot(tall, plain_gather, preferred_element_type=jnp.float32)
    for k in range(2):
        at = pl.ds(k * wide_n, wide_n)
        for half in range(2):
            rows = slice((2 * k + half) * wide_n, (2 * k + half + 1) * wide_n)
            banded = jnp.where(
                keep[0], banded_full[0][rows], jnp.where(keep[1], banded_full[1][rows], 0.0)
            ).astype(jnp.bfloat16)
            plain = jnp.where(same, plain_full[rows], 0.0).astype(jnp.bfloat16)
            if half == 0:
                weights_hi[at, :] = jnp.concatenate([banded, banded], axis=1)
                border_hi[at, :] = plain
            else:
                weights_lo[at, :] = banded
                border_lo[at, :] = plain

    for x in range(size_x + 1):
        fields[:, x * pitch + size_y : (x + 1) * pitch, :] = jnp.zeros((6 * pairs, size_y, size_z), jnp.float32)
    for x in range(size_x):
        fields[:, x * pitch : x * pitch + size_y, :] = (
            basis[:, x * size_y : (x + 1) * size_y, :] * free[x * size_y : (x + 1) * size_y][None]
        )

    row_y = lax.broadcasted_iota(jnp.int32, (size_y, size_z), 0)

    def inside_y(oy):
        at_y = row_y + (iy * size_y + oy)
        return jnp.where((at_y >= 0) & (at_y < grid_y), 1.0, 0.0)

    def inside_x(plane):
        at_x = jnp.full((size_y, size_z), ix * size_x + plane - 2, jnp.int32)
        return jnp.where((at_x >= 0) & (at_x < grid_x), 1.0, 0.0)

    share_of = fold_plane([inside_y(oy) for oy in range(-2, 3)])
    flags = [inside_x(plane) for plane in range(size_x + 4)]
    for x in range(size_x):
        weight_sum[pl.ds(x * size_y, size_y), :] = (
            share_of[0]
            + (flags[x + 1] + flags[x + 3]) * share_of[1]
            + (flags[x] + flags[x + 4]) * share_of[2]
        )

    for j in range(TRIALS - 1):
        middle_table[pl.ds(j, 1), :] = jnp.full((1, size_z), INVERSE_MIDDLES[j], jnp.float32)
    middle_table[pl.ds(TRIALS - 1, 1), :] = jnp.zeros((1, size_z), jnp.float32)

    pl.semaphore_wait(barrier, (nx - 1) + (ny - 1) + corners)

    design_copies = edge_copies(0)
    basis_copies = {
        slot: pltpu.make_async_remote_copy(
            src_ref=src,
            dst_ref=dst,
            send_sem=basis_send_sem.at[k],
            recv_sem=basis_recv_sem.at[k],
            device_id=(ix + AROUND[slot][0], iy + AROUND[slot][1]),
            device_id_type=MESH,
        )
        for k, (slot, src, dst) in enumerate((
            (0, send_x, recv_x),
            (2, send_y, recv_y.at[:, pl.ds(0, 8 * size_x)]),
            (4, send_y.at[:, pl.ds(0, 8)], recv_y.at[:, pl.ds(8 * size_x, 8)]),
        ))
    }

    def leave(copies, slot):
        if slot in basis_copies:
            basis_copies[slot].start()
        copies[slot].start()

    def left(copies, slot):
        if slot in basis_copies:
            basis_copies[slot].wait_send()
        copies[slot].wait_send()

    edge_each(design_copies, leave)
    energy[...] = jnp.zeros((2 * cells, size_z), jnp.float32)
    order = [(a, b, d, c) for a in range(2) for b in range(2) for d in range(2) for c in range(3)]

    def beside(tiles):
        return tiles[0] if len(tiles) == 1 else jnp.concatenate(tiles, axis=1)

    def split(operand):
        high = operand.astype(jnp.bfloat16)
        return high, (operand - high.astype(jnp.float32)).astype(jnp.bfloat16)

    def contract(product, states):
        return [
            [
                functools.reduce(
                    lambda p, q: p + q,
                    [
                        state[key] * product[
                            k * wide_n + r * size_y : k * wide_n + (r + 1) * size_y,
                            n * size_z : (n + 1) * size_z,
                        ]
                        for r, key in enumerate(order)
                    ],
                )
                for k in range(2)
            ]
            for n, state in enumerate(states)
        ]

    def name_of(pair):
        return pair if isinstance(pair, int) else -1

    def own_columns(columns):
        adjoint, state = {}, {}
        for pair, x in columns:
            for c in range(3):
                for at_x in (x, x + 1):
                    key = (name_of(pair), at_x, c)
                    if key in adjoint:
                        continue
                    tile = fields[pair * 6 + 3 + c, at_x * pitch : at_x * pitch + size_y, :]
                    adjoint[key] = (tile, z_shift(tile, 1))
                    for b in range(2):
                        tile = fields[pair * 6 + c, at_x * pitch + b : at_x * pitch + b + size_y, :]
                        state[key + (b,)] = (tile, z_shift(tile, 1))
        high, low = split(jnp.concatenate(
            [
                beside([adjoint[name_of(pair), x + a, c][d] for pair, x in columns])
                for a in range(2) for d in range(2) for c in range(3)
            ],
            axis=0,
        ))
        product = jnp.dot(
            weights_hi[...], jnp.concatenate([high, low], axis=0), preferred_element_type=jnp.float32
        ) + jnp.dot(weights_lo[...], high, preferred_element_type=jnp.float32)
        states = [
            {(a, b, d, c): state[name_of(pair), x + a, c, b][d] for a, b, d, c in order} for pair, x in columns
        ]
        for (pair, x), parts in zip(columns, contract(product, states)):
            for k, part in enumerate(parts):
                at = pl.ds((k * size_x + x) * size_y, size_y)
                energy[at, :] = energy[at, :] + part

    def pair_step(pair, carry):
        for first in range(0, size_x - 1, CHUNK):
            own_columns([(pair, x) for x in range(first, min(first + CHUNK, size_x - 1))])
        return carry

    lax.fori_loop(0, pairs, pair_step, 0)

    edge_receive(design_copies)
    assemble(design, 0)
    for x, tile in enumerate(stencil(wide_rows, size_x)):
        at = pl.ds(x * size_y, size_y)
        physical[at, :] = jnp.where(passive[at, :] == 1, 1.0, tile / weight_sum[at, :])

    for slot in basis_copies:
        dx, dy = AROUND[slot]

        @pl.when(there(-dx, -dy))
        def _(slot=slot):
            basis_copies[slot].wait_recv()

    fields[:, size_x * pitch : size_x * pitch + size_y, :] = recv_x[...]
    for first in range(0, pairs, CHUNK):
        own_columns([(pair, size_x - 1) for pair in range(first, min(first + CHUNK, pairs))])

    def border_tiles(pair, member):
        tiles = {}
        for c in range(3):
            f, k = pair * 6 + member * 3 + c, member * 3 + c
            for a in range(2):
                for b in range(2):
                    if b == 0:
                        tile = fields[f, pl.ds(a * pitch + size_y - 1, size_x, stride=pitch), :]
                    else:
                        tile = recv_y[pair, pl.ds(8 * a + k, size_x, stride=8), :]
                    tiles[a, b, 0, c], tiles[a, b, 1, c] = tile, z_shift(tile, 1)
        return tiles

    border = [None, None]
    for first in range(0, pairs, CHUNK):
        group_pairs = range(first, min(first + CHUNK, pairs))
        adjoints = [border_tiles(pair, 1) for pair in group_pairs]
        high, low = split(jnp.concatenate([beside([t[key] for t in adjoints]) for key in order], axis=0))
        product = (
            jnp.dot(border_hi[...], high, preferred_element_type=jnp.float32)
            + jnp.dot(border_hi[...], low, preferred_element_type=jnp.float32)
            + jnp.dot(border_lo[...], high, preferred_element_type=jnp.float32)
        )
        for parts in contract(product, [border_tiles(pair, 0) for pair in group_pairs]):
            border = [p if e is None else e + p for e, p in zip(border, parts)]
    for k in range(2):
        energy[pl.ds(k * cells + size_y - 1, size_x, stride=size_y), :] = border[k]

    solid = passive[...] == 1
    density = physical[...]
    raw = -(
        PENALTY_SCALE * density * density * energy[0:cells, :]
        - OMEGA_SQUARED * energy[cells : 2 * cells, :]
    )
    scaled[...] = jnp.where(solid, 0.0, raw) / weight_sum[...]

    pack_edges(scaled, 1)
    scaled_copies = edge_copies(1)
    edge_each(scaled_copies, lambda c, slot: c[slot].start())
    edge_each(design_copies, left)

    band = size_z // regions
    width, group_rows = size_z // ny, TRIALS // ny
    lane = lax.broadcasted_iota(jnp.int32, (group_rows, size_z), 1)
    lane8 = lax.broadcasted_iota(jnp.int32, (8, size_z), 1)
    slot_row = lax.broadcasted_iota(jnp.int32, (8, size_z), 0)
    group = lane // width
    pick = (
        lax.broadcasted_iota(jnp.int32, (regions, size_z), 1) // band
        == lax.broadcasted_iota(jnp.int32, (regions, size_z), 0)
    ).astype(jnp.float32).astype(jnp.bfloat16)
    rest = jnp.broadcast_to(fraction[...].reshape(1, regions), (8, regions))
    target = jnp.zeros((8, size_z), jnp.float32)
    for _ in range(3):
        piece = rest.astype(jnp.bfloat16)
        target = target + jnp.dot(piece, pick, preferred_element_type=jnp.float32)
        rest = rest - piece.astype(jnp.float32)
    target = target * float(grid_x * grid_y * band)
    own_target = jnp.where(lane8 // width == iy, target, 0.0)
    reach = width
    while reach < size_z:
        own_target = own_target + pltpu.roll(own_target, reach, 1)
        reach *= 2
    for r in range(group_rows):
        line = jnp.full((1, size_z), INVERSE_LEAVES[0], jnp.float32)
        for g in range(ny):
            j = min(g * group_rows + r + 1, TRIALS - 1)
            line = jnp.where(lane8[0:1] // width == g, INVERSE_LEAVES[j], line)
        leaf_table[pl.ds(r, 1), :] = line

    edge_receive(scaled_copies)
    assemble(scaled, 1)
    for x, tile in enumerate(stencil(wide_rows, size_x)):
        benefit[pl.ds(x * size_y, size_y), :] = -tile
    benefit_out = pltpu.make_async_copy(benefit, benefit_hbm, out_sem)
    benefit_out.start()

    value = design[...]
    gain = value * jnp.sqrt(jnp.maximum(benefit[...], 0.0))
    floor_value = jnp.where(solid, 1.0, jnp.maximum(value - MOVE_LIMIT, 0.0))
    ceiling = jnp.where(solid, 1.0, jnp.minimum(value + MOVE_LIMIT, 1.0))

    def candidate(inverse_root):
        return jnp.minimum(ceiling, jnp.maximum(floor_value, gain * inverse_root))

    def total_over_x(j):
        trial = candidate(middle_table[pl.ds(j, 1), :])
        return functools.reduce(
            lambda p, q: p + q, [trial[x * size_y : (x + 1) * size_y] for x in range(size_x)]
        )

    def trial_group(number, carry):
        first = pl.multiple_of(number * 8, 8)
        tiles = [total_over_x(first + j) for j in range(8)]
        reach = 4
        while reach:
            lower = (slot_row & reach) == 0
            tiles = [
                jnp.where(lower, p, q)
                + jnp.where(lower, pltpu.roll(p, 8 - reach, 0), pltpu.roll(q, reach, 0))
                for p, q in zip(tiles[:reach], tiles[reach:])
            ]
            reach //= 2
        unused = slot_row + first == TRIALS - 1
        volume_table[pl.ds(first, 8), :] = jnp.where(unused, 0.0, tiles[0])
        return carry

    lax.fori_loop(0, TRIALS // 8, trial_group, 0)
    volumes = volume_table[...]

    for q in range(ny):
        packed = jnp.zeros((group_rows, size_z), jnp.float32)
        for g in range(ny):
            part = volumes[g * group_rows : (g + 1) * group_rows]
            turn = (width * (g - q)) % size_z
            if turn:
                part = pltpu.roll(part, turn, 1)
            packed = jnp.where(group == g, part, packed)
        share_send[q] = packed
    share_recv[pl.ds(iy, 1)] = share_send[pl.ds(iy, 1)]
    pending = []

    def along(count, me, place, source, buffer, send_sem, recv_sem):
        copies = []
        for step in range(1, count):
            peer = lax.rem(me + step, count)
            copy = pltpu.make_async_remote_copy(
                src_ref=source(peer),
                dst_ref=buffer.at[me],
                send_sem=send_sem.at[step],
                recv_sem=recv_sem.at[step],
                device_id=place(peer),
                device_id_type=MESH,
            )
            copy.start()
            copies.append(copy)
        for copy in copies:
            copy.wait_recv()
        pending.extend(copies)

    along(ny, iy, lambda at: (ix, at), lambda at: share_send.at[at], share_recv, share_send_sem, share_recv_sem)
    share = functools.reduce(lambda p, q: p + q, [share_recv[k] for k in range(ny)])
    gather_x[pl.ds(ix, 1)] = share[None]
    along(nx, ix, lambda at: (at, iy), lambda at: gather_x.at[ix], gather_x, gx_send_sem, gx_recv_sem)
    share = functools.reduce(lambda p, q: p + q, [gather_x[k] for k in range(nx)])

    reach = 1
    while reach < band:
        share = share + jnp.where(
            (lane // reach) % 2 == 0,
            pltpu.roll(share, size_z - reach, 1),
            pltpu.roll(share, reach, 1),
        )
        reach *= 2
    chosen = jnp.where(share > own_target[0:1], leaf_table[...], INVERSE_LEAVES[0])
    chosen = jnp.min(chosen, axis=0, keepdims=True)
    reach = width
    while reach < size_z:
        chosen = jnp.minimum(chosen, pltpu.roll(chosen, reach, 1))
        reach *= 2
    gather_y[pl.ds(iy, 1)] = jnp.broadcast_to(chosen, (8, size_z))[None]
    along(ny, iy, lambda at: (ix, at), lambda at: gather_y.at[iy], gather_y, gy_send_sem, gy_recv_sem)
    multiplier = gather_y[0]
    for q in range(1, ny):
        multiplier = jnp.where(lane8 // width == q, gather_y[q], multiplier)
    chosen_out[...] = multiplier
    benefit_out.wait()

    edge_each(scaled_copies, lambda c, slot: c[slot].wait_send())
    for copy in pending:
        copy.wait_send()


def closing_kernel(negated, inverse_root, design, passive, sensitivity, design_next):
    benefit, value = negated[...], design[...]
    sensitivity[...] = -benefit
    trial = value * jnp.sqrt(jnp.maximum(benefit, 0.0)) * inverse_root[0:1, :]
    low = jnp.maximum(value - MOVE_LIMIT, 0.0)
    high = jnp.minimum(value + MOVE_LIMIT, 1.0)
    design_next[...] = jnp.where(passive[...] == 1, 1.0, jnp.minimum(high, jnp.maximum(low, trial)))


def shards(nx, ny, design, passive, basis_pairs, supports, stiffness, mass_matrix, volume_fraction):
    size_x, size_y, size_z = design.shape
    pairs = basis_pairs.shape[0]
    regions = volume_fraction.shape[0]
    cells = size_x * size_y
    fields_n = 6 * pairs
    flat = (cells, size_z)
    vmem = pl.BlockSpec(memory_space=pltpu.VMEM)
    f32, bf16 = jnp.float32, jnp.bfloat16
    dma = pltpu.SemaphoreType.DMA
    negated, inverse_root = pl.pallas_call(
        functools.partial(kernel, nx, ny, size_x, size_y, size_z, pairs, regions),
        out_shape=(jax.ShapeDtypeStruct(flat, f32), jax.ShapeDtypeStruct((size_y, size_z), f32)),
        in_specs=[pl.BlockSpec(memory_space=pltpu.HBM)] * 7,
        out_specs=(pl.BlockSpec(memory_space=pltpu.HBM), vmem),
        scratch_shapes=[
            pltpu.VMEM(flat, f32),
            pltpu.VMEM(flat, f32),
            pltpu.VMEM(flat, jnp.int32),
            pltpu.VMEM((fields_n, cells, size_z), f32),
            pltpu.VMEM(flat, jnp.int32),
            pltpu.VMEM(stiffness.shape, f32),
            pltpu.VMEM(mass_matrix.shape, f32),
            pltpu.VMEM((regions,), f32),
            pltpu.VMEM((fields_n, (size_x + 1) * 2 * size_y, size_z), f32),
            pltpu.VMEM((fields_n, size_y, size_z), f32),
            pltpu.VMEM((pairs, 8 * size_x, size_z), f32),
            pltpu.VMEM((fields_n, size_y, size_z), f32),
            pltpu.VMEM((pairs, 8 * (size_x + 1), size_z), f32),
            pltpu.VMEM((2, 4, 2, size_x, size_z), f32),
            pltpu.VMEM((2, 8, 2, size_y, size_z), f32),
            pltpu.VMEM(((size_x + 4) * 3 * size_y, size_z), f32),
            pltpu.VMEM(flat, f32),
            pltpu.VMEM((48 * size_y, 24 * size_y), bf16),
            pltpu.VMEM((48 * size_y, 12 * size_y), bf16),
            pltpu.VMEM((48 * size_y, 24 * size_y), bf16),
            pltpu.VMEM((48 * size_y, 24 * size_y), bf16),
            pltpu.VMEM(flat, f32),
            pltpu.VMEM(flat, f32),
            pltpu.VMEM((2 * cells, size_z), f32),
            pltpu.VMEM((ny, TRIALS // ny, size_z), f32),
            pltpu.VMEM((ny, TRIALS // ny, size_z), f32),
            pltpu.VMEM((nx, TRIALS // ny, size_z), f32),
            pltpu.VMEM((ny, 8, size_z), f32),
            pltpu.VMEM((TRIALS // ny, size_z), f32),
            pltpu.VMEM((TRIALS, size_z), f32),
            pltpu.VMEM((TRIALS, size_z), f32),
            dma((7,)),
            dma,
            dma((3,)),
            dma((3,)),
            dma((2, 8)),
            dma((2, 8)),
            dma((ny,)),
            dma((ny,)),
            dma((nx,)),
            dma((nx,)),
            dma((ny,)),
            dma((ny,)),
        ],
        compiler_params=pltpu.CompilerParams(
            collective_id=0, has_side_effects=True, vmem_limit_bytes=64 * 1024 * 1024
        ),
        name="sensitivity_update",
    )(
        design.reshape(flat),
        passive.reshape(flat),
        basis_pairs.reshape(fields_n, cells, size_z),
        supports.reshape(flat),
        stiffness,
        mass_matrix,
        volume_fraction,
    )
    sensitivity, design_next = pl.pallas_call(
        closing_kernel,
        out_shape=(jax.ShapeDtypeStruct(flat, f32), jax.ShapeDtypeStruct(flat, f32)),
        in_specs=[vmem] * 4,
        out_specs=(vmem, vmem),
        compiler_params=pltpu.CompilerParams(vmem_limit_bytes=64 * 1024 * 1024),
        name="design_update",
    )(negated, inverse_root, design.reshape(flat), passive.reshape(flat))
    return sensitivity.reshape(design.shape), design_next.reshape(design.shape)


def solution(mesh):
    placed = (
        P("gx", "gy", None),
        P("gx", "gy", None),
        P(None, None, None, "gx", "gy", None),
        P("gx", "gy", None),
        P(),
        P(),
        P(),
    )
    return jax.shard_map(
        functools.partial(shards, mesh.shape["gx"], mesh.shape["gy"]),
        mesh=mesh,
        in_specs=placed,
        out_specs=(P("gx", "gy", None), P("gx", "gy", None)),
        check_vma=False,
    )
```

```python
import functools
import math

import jax
import jax.numpy as jnp
import numpy as np
from jax import lax
from jax.experimental import pallas as pl
from jax.experimental.pallas import tpu as pltpu
from jax.sharding import PartitionSpec as P

PENALTY_SCALE = 3.0 * (1.0 - 0.001)
OMEGA_SQUARED = 0.5
MOVE_LIMIT = 0.2
BISECT = 6
TRIALS = 2**BISECT
CHUNK = 4
MESH = pl.DeviceIdType.MESH
AROUND = ((-1, 0), (1, 0), (0, -1), (0, 1), (-1, -1), (-1, 1), (1, -1), (1, 1))


def tree_ends():
    ends = [np.float32(1e-4), np.float32(1e4)]
    for _ in range(BISECT):
        inner = [np.sqrt(p * q) for p, q in zip(ends, ends[1:])]
        ends = [ends[0]] + [e for pair in zip(inner, ends[1:]) for e in pair]
    return ends


ENDS = tree_ends()
INVERSE_MIDDLES = [float(np.float32(1.0) / np.sqrt(e)) for e in ENDS[1:-1]]
INVERSE_LEAVES = [
    float(np.float32(1.0) / np.sqrt(np.sqrt(p * q))) for p, q in zip(ENDS, ENDS[1:])
]


def opposite(slot):
    dx, dy = AROUND[slot]
    return AROUND.index((-dx, -dy))


def z_shift(value, step):
    axis = value.ndim - 1
    size = value.shape[axis]
    lane = lax.broadcasted_iota(jnp.int32, value.shape, axis)
    moved = pltpu.roll(value, (-step) % size, axis)
    keep = lane < size - step if step > 0 else lane >= -step
    return jnp.where(keep, moved, 0.0)


def fold_plane(tiles):
    folded_y = (tiles[2], tiles[1] + tiles[3], tiles[0] + tiles[4])
    parts = [[], [], []]
    for cy, tile in enumerate(folded_y):
        folded_z = (
            tile,
            z_shift(tile, 1) + z_shift(tile, -1),
            z_shift(tile, 2) + z_shift(tile, -2),
        )
        for cz, entry in enumerate(folded_z):
            for cx in range(3):
                weight = 3.0 - math.sqrt(cx * cx + cy * cy + cz * cz)
                if weight > 0.0:
                    parts[cx].append(weight * entry)
    return [functools.reduce(lambda a, b: a + b, part) for part in parts]


def stencil(rows_at, size_x):
    planes = [
        fold_plane([rows_at(plane, oy) for oy in range(-2, 3)]) for plane in range(size_x + 4)
    ]
    spread = [[plane[cx] for plane in planes] for cx in range(3)]
    return [
        spread[0][i + 2]
        + (spread[1][i + 1] + spread[1][i + 3])
        + (spread[2][i] + spread[2][i + 4])
        for i in range(size_x)
    ]


def kernel(
    nx, ny, size_x, size_y, size_z, pairs, regions,
    design_hbm, passive_hbm, basis_hbm, supports_hbm, stiffness_hbm, mass_hbm, fraction_hbm,
    benefit_hbm, chosen_out,
    benefit, design, passive, basis, supports, stiffness, mass_matrix, fraction,
    fields, send_x, send_y, recv_x, recv_y,
    edge_send, edge_recv, wide, scaled, weights_hi, weights_lo, border_hi, border_lo, weight_sum, physical, energy,
    share_send, share_recv, gather_x, gather_y, leaf_table,
    load_sem, out_sem,
    basis_send_sem, basis_recv_sem, halo_send_sem, halo_recv_sem,
    share_send_sem, share_recv_sem, gx_send_sem, gx_recv_sem, gy_send_sem, gy_recv_sem,
):
    ix, iy = lax.axis_index("gx"), lax.axis_index("gy")
    pitch = 2 * size_y
    cells = size_x * size_y

    def there(dx, dy):
        return (
            (ix + dx >= 0) & (ix + dx < nx) & (iy + dy >= 0) & (iy + dy < ny)
        )

    edge_recv[...] = jnp.zeros(edge_recv.shape, jnp.float32)
    recv_x[...] = jnp.zeros(recv_x.shape, jnp.float32)
    recv_y[...] = jnp.zeros(recv_y.shape, jnp.float32)
    barrier = pltpu.get_barrier_semaphore()
    for step in range(1, ny):
        pl.semaphore_signal(barrier, inc=1, device_id=(ix, lax.rem(iy + step, ny)), device_id_type=MESH)
    for step in range(1, nx):
        pl.semaphore_signal(barrier, inc=1, device_id=(lax.rem(ix + step, nx), iy), device_id_type=MESH)
    for dx, dy in AROUND[4:]:
        @pl.when(there(dx, dy))
        def _(dx=dx, dy=dy):
            pl.semaphore_signal(barrier, inc=1, device_id=(ix + dx, iy + dy), device_id_type=MESH)
    corners = sum(there(dx, dy).astype(jnp.int32) for dx, dy in AROUND[4:])

    loads = [
        pltpu.make_async_copy(src, dst, load_sem.at[k])
        for k, (src, dst) in enumerate((
            (supports_hbm, supports), (basis_hbm, basis), (design_hbm, design), (passive_hbm, passive),
            (stiffness_hbm, stiffness), (mass_hbm, mass_matrix), (fraction_hbm, fraction),
        ))
    ]
    for load in loads:
        load.start()
    send_y[...] = jnp.zeros(send_y.shape, jnp.float32)
    for load in loads[:2]:
        load.wait()

    free = 1.0 - supports[...].astype(jnp.float32)
    send_x[...] = basis[:, 0:size_y, :] * free[0:size_y][None]
    free_y = 1.0 - supports[pl.ds(0, size_x, stride=size_y), :].astype(jnp.float32)
    for f in range(6 * pairs):
        rows = basis[f, pl.ds(0, size_x, stride=size_y), :] * free_y
        send_y[f // 6, pl.ds(f % 6, size_x, stride=8), :] = rows

    def pack_edges(source, which):
        for x in range(2):
            edge_send[which, 2, x] = source[pl.ds(x * size_y, size_y), :]
            edge_send[which, 3, x] = source[pl.ds((size_x - 2 + x) * size_y, size_y), :]
        for y in range(2):
            edge_send[which, 0, y] = source[pl.ds(y, size_x, stride=size_y), :]
            edge_send[which, 1, y] = source[pl.ds(size_y - 2 + y, size_x, stride=size_y), :]

    def edge_copies(which):
        copies = []
        for slot, (dx, dy) in enumerate(AROUND):
            if dy == 0:
                src = edge_send.at[which, 2 if dx < 0 else 3]
            else:
                src = edge_send.at[which, 0 if dy < 0 else 1]
            copies.append(pltpu.make_async_remote_copy(
                src_ref=src,
                dst_ref=edge_recv.at[which, opposite(slot)],
                send_sem=halo_send_sem.at[which, slot],
                recv_sem=halo_recv_sem.at[which, opposite(slot)],
                device_id=(ix + dx, iy + dy),
                device_id_type=MESH,
            ))
        return copies

    def edge_each(copies, act):
        for slot, (dx, dy) in enumerate(AROUND):
            @pl.when(there(dx, dy))
            def _(slot=slot):
                act(copies, slot)

    def edge_receive(copies):
        edge_each(copies, lambda c, slot: c[opposite(slot)].wait_recv())

    span = 3 * size_y

    def assemble(source, which):
        for x in range(size_x):
            wide[pl.ds((x + 2) * span + size_y, size_y), :] = source[pl.ds(x * size_y, size_y), :]
        for x in range(2):
            wide[pl.ds(x * span + size_y, size_y), :] = edge_recv[which, 0, x]
            wide[pl.ds((size_x + 2 + x) * span + size_y, size_y), :] = edge_recv[which, 1, x]
        for y in range(2):
            low, high = size_y - 2 + y, 2 * size_y + y
            wide[pl.ds(2 * span + low, size_x, stride=span), :] = edge_recv[which, 2, y]
            wide[pl.ds(2 * span + high, size_x, stride=span), :] = edge_recv[which, 3, y]
            for x in range(2):
                for slot, row in ((4, low), (5, high)):
                    wide[pl.ds(x * span + row, 1), :] = edge_recv[which, slot, y, size_x - 2 + x : size_x - 1 + x, :]
                for slot, row in ((6, low), (7, high)):
                    wide[pl.ds((size_x + 2 + x) * span + row, 1), :] = edge_recv[which, slot, y, x : x + 1, :]

    def wide_rows(plane, oy):
        return wide[pl.ds(plane * span + size_y + oy, size_y), :]

    loads[2].wait()
    pack_edges(design, 0)

    pl.semaphore_wait(barrier, (nx - 1) + (ny - 1) + corners)

    design_copies = edge_copies(0)
    basis_copies = {
        slot: pltpu.make_async_remote_copy(
            src_ref=src,
            dst_ref=dst,
            send_sem=basis_send_sem.at[k],
            recv_sem=basis_recv_sem.at[k],
            device_id=(ix + AROUND[slot][0], iy + AROUND[slot][1]),
            device_id_type=MESH,
        )
        for k, (slot, src, dst) in enumerate((
            (0, send_x, recv_x),
            (2, send_y, recv_y.at[:, pl.ds(0, 8 * size_x)]),
            (4, send_y.at[:, pl.ds(0, 8)], recv_y.at[:, pl.ds(8 * size_x, 8)]),
        ))
    }

    def leave(copies, slot):
        if slot in basis_copies:
            basis_copies[slot].start()
        copies[slot].start()

    def left(copies, slot):
        if slot in basis_copies:
            basis_copies[slot].wait_send()
        copies[slot].wait_send()

    edge_each(design_copies, leave)
    for load in loads[3:]:
        load.wait()

    grid_x, grid_y = nx * size_x, ny * size_y
    wide_n, narrow_n, depth = 24 * size_y, 24, 12 * size_y
    bits_y = size_y.bit_length() - 1

    def spread_rows(shape, row_dim):
        at = lax.broadcasted_iota(jnp.int32, shape, row_dim)
        return lax.shift_right_logical(at, bits_y) == lax.broadcasted_iota(jnp.int32, shape, 1 - row_dim)

    col = lax.broadcasted_iota(jnp.int32, (narrow_n, depth), 1)
    tile_of = lax.shift_right_logical(col, bits_y)
    corner = lax.shift_right_logical(tile_of * 11, 5)
    component = tile_of - 3 * corner
    source_row = 12 * lax.shift_right_logical(corner, 1) + 3 * (corner & 1) + component
    at_row = lax.broadcasted_iota(jnp.int32, (narrow_n, depth), 0)
    gather = [
        (at_row == source_row + 6 * b).astype(jnp.float32).astype(jnp.bfloat16)
        for b in range(2)
    ]
    at_y = lax.broadcasted_iota(jnp.int32, (wide_n, depth), 0) & (size_y - 1)
    col_y = lax.broadcasted_iota(jnp.int32, (wide_n, depth), 1) & (size_y - 1)
    keep = [col_y == at_y, col_y == at_y + 1]
    same = (
        lax.broadcasted_iota(jnp.int32, (wide_n, wide_n), 0) & (size_y - 1)
    ) == (lax.broadcasted_iota(jnp.int32, (wide_n, wide_n), 1) & (size_y - 1))

    pieces = []
    for matrix in (stiffness, mass_matrix):
        value = matrix[...]
        high = value.astype(jnp.bfloat16).astype(jnp.float32)
        pieces += [high, value - high]
    pieces = jnp.concatenate(pieces, axis=0).astype(jnp.bfloat16)
    expand = spread_rows((4 * wide_n, 4 * narrow_n), 0).astype(jnp.float32).astype(jnp.bfloat16)
    tall = jnp.dot(expand, pieces, preferred_element_type=jnp.float32).astype(jnp.bfloat16)
    plain_gather = spread_rows((narrow_n, wide_n), 1).astype(jnp.float32).astype(jnp.bfloat16)
    banded_full = [jnp.dot(tall, g, preferred_element_type=jnp.float32) for g in gather]
    plain_full = jnp.dot(tall, plain_gather, preferred_element_type=jnp.float32)
    for k in range(2):
        at = pl.ds(k * wide_n, wide_n)
        for half in range(2):
            rows = slice((2 * k + half) * wide_n, (2 * k + half + 1) * wide_n)
            banded = jnp.where(
                keep[0], banded_full[0][rows], jnp.where(keep[1], banded_full[1][rows], 0.0)
            ).astype(jnp.bfloat16)
            plain = jnp.where(same, plain_full[rows], 0.0).astype(jnp.bfloat16)
            if half == 0:
                weights_hi[at, :] = jnp.concatenate([banded, banded], axis=1)
                border_hi[at, :] = plain
            else:
                weights_lo[at, :] = banded
                border_lo[at, :] = plain

    for x in range(size_x + 1):
        fields[:, x * pitch + size_y : (x + 1) * pitch, :] = jnp.zeros((6 * pairs, size_y, size_z), jnp.float32)
    for x in range(size_x):
        fields[:, x * pitch : x * pitch + size_y, :] = (
            basis[:, x * size_y : (x + 1) * size_y, :] * free[x * size_y : (x + 1) * size_y][None]
        )

    row_y = lax.broadcasted_iota(jnp.int32, (size_y, size_z), 0)

    def inside_y(oy):
        at_y = row_y + (iy * size_y + oy)
        return jnp.where((at_y >= 0) & (at_y < grid_y), 1.0, 0.0)

    def inside_x(plane):
        at_x = jnp.full((size_y, size_z), ix * size_x + plane - 2, jnp.int32)
        return jnp.where((at_x >= 0) & (at_x < grid_x), 1.0, 0.0)

    share_of = fold_plane([inside_y(oy) for oy in range(-2, 3)])
    flags = [inside_x(plane) for plane in range(size_x + 4)]
    for x in range(size_x):
        weight_sum[pl.ds(x * size_y, size_y), :] = (
            share_of[0]
            + (flags[x + 1] + flags[x + 3]) * share_of[1]
            + (flags[x] + flags[x + 4]) * share_of[2]
        )

    energy[...] = jnp.zeros((2 * cells, size_z), jnp.float32)
    order = [(a, b, d, c) for a in range(2) for b in range(2) for d in range(2) for c in range(3)]

    def beside(tiles):
        return tiles[0] if len(tiles) == 1 else jnp.concatenate(tiles, axis=1)

    def split(operand):
        high = operand.astype(jnp.bfloat16)
        return high, (operand - high.astype(jnp.float32)).astype(jnp.bfloat16)

    def contract(product, states):
        return [
            [
                functools.reduce(
                    lambda p, q: p + q,
                    [
                        state[key] * product[
                            k * wide_n + r * size_y : k * wide_n + (r + 1) * size_y,
                            n * size_z : (n + 1) * size_z,
                        ]
                        for r, key in enumerate(order)
                    ],
                )
                for k in range(2)
            ]
            for n, state in enumerate(states)
        ]

    def own_columns(columns):
        adjoint, state = {}, {}
        for pair, x in columns:
            for c in range(3):
                for at_x in (x, x + 1):
                    key = (pair, at_x, c)
                    if key in adjoint:
                        continue
                    tile = fields[pair * 6 + 3 + c, at_x * pitch : at_x * pitch + size_y, :]
                    adjoint[key] = (tile, z_shift(tile, 1))
                    for b in range(2):
                        tile = fields[pair * 6 + c, at_x * pitch + b : at_x * pitch + b + size_y, :]
                        state[key + (b,)] = (tile, z_shift(tile, 1))
        high, low = split(jnp.concatenate(
            [
                beside([adjoint[pair, x + a, c][d] for pair, x in columns])
                for a in range(2) for d in range(2) for c in range(3)
            ],
            axis=0,
        ))
        product = jnp.dot(
            weights_hi[...], jnp.concatenate([high, low], axis=0), preferred_element_type=jnp.float32
        ) + jnp.dot(weights_lo[...], high, preferred_element_type=jnp.float32)
        states = [
            {(a, b, d, c): state[pair, x + a, c, b][d] for a, b, d, c in order} for pair, x in columns
        ]
        for (pair, x), parts in zip(columns, contract(product, states)):
            for k, part in enumerate(parts):
                at = pl.ds((k * size_x + x) * size_y, size_y)
                energy[at, :] = energy[at, :] + part

    for pair in range(pairs):
        for first in range(0, size_x - 1, CHUNK):
            own_columns([(pair, x) for x in range(first, min(first + CHUNK, size_x - 1))])

    edge_receive(design_copies)
    assemble(design, 0)
    for x, tile in enumerate(stencil(wide_rows, size_x)):
        at = pl.ds(x * size_y, size_y)
        physical[at, :] = jnp.where(passive[at, :] == 1, 1.0, tile / weight_sum[at, :])

    for slot in basis_copies:
        dx, dy = AROUND[slot]

        @pl.when(there(-dx, -dy))
        def _(slot=slot):
            basis_copies[slot].wait_recv()

    fields[:, size_x * pitch : size_x * pitch + size_y, :] = recv_x[...]
    for first in range(0, pairs, CHUNK):
        own_columns([(pair, size_x - 1) for pair in range(first, min(first + CHUNK, pairs))])

    def border_tiles(pair, member):
        tiles = {}
        for c in range(3):
            f, k = pair * 6 + member * 3 + c, member * 3 + c
            for a in range(2):
                for b in range(2):
                    if b == 0:
                        tile = fields[f, pl.ds(a * pitch + size_y - 1, size_x, stride=pitch), :]
                    else:
                        tile = recv_y[pair, pl.ds(8 * a + k, size_x, stride=8), :]
                    tiles[a, b, 0, c], tiles[a, b, 1, c] = tile, z_shift(tile, 1)
        return tiles

    border = [None, None]
    for first in range(0, pairs, CHUNK):
        group_pairs = range(first, min(first + CHUNK, pairs))
        adjoints = [border_tiles(pair, 1) for pair in group_pairs]
        high, low = split(jnp.concatenate([beside([t[key] for t in adjoints]) for key in order], axis=0))
        product = (
            jnp.dot(border_hi[...], high, preferred_element_type=jnp.float32)
            + jnp.dot(border_hi[...], low, preferred_element_type=jnp.float32)
            + jnp.dot(border_lo[...], high, preferred_element_type=jnp.float32)
        )
        for parts in contract(product, [border_tiles(pair, 0) for pair in group_pairs]):
            border = [p if e is None else e + p for e, p in zip(border, parts)]
    for k in range(2):
        energy[pl.ds(k * cells + size_y - 1, size_x, stride=size_y), :] = border[k]

    solid = passive[...] == 1
    density = physical[...]
    raw = -(
        PENALTY_SCALE * density * density * energy[0:cells, :]
        - OMEGA_SQUARED * energy[cells : 2 * cells, :]
    )
    scaled[...] = jnp.where(solid, 0.0, raw) / weight_sum[...]

    pack_edges(scaled, 1)
    scaled_copies = edge_copies(1)
    edge_each(scaled_copies, lambda c, slot: c[slot].start())
    edge_each(design_copies, left)

    band = size_z // regions
    width, group_rows = size_z // ny, TRIALS // ny
    part_rows = group_rows // band
    lane = lax.broadcasted_iota(jnp.int32, (part_rows, size_z), 1)
    lane8 = lax.broadcasted_iota(jnp.int32, (8, size_z), 1)
    slot_row = lax.broadcasted_iota(jnp.int32, (8, size_z), 0)
    group = lane // width
    pick = (
        lax.broadcasted_iota(jnp.int32, (regions, size_z), 1) // band
        == lax.broadcasted_iota(jnp.int32, (regions, size_z), 0)
    ).astype(jnp.float32).astype(jnp.bfloat16)
    rest = jnp.broadcast_to(fraction[...].reshape(1, regions), (8, regions))
    target = jnp.zeros((8, size_z), jnp.float32)
    for _ in range(3):
        piece = rest.astype(jnp.bfloat16)
        target = target + jnp.dot(piece, pick, preferred_element_type=jnp.float32)
        rest = rest - piece.astype(jnp.float32)
    target = target * float(grid_x * grid_y * band)
    own_target = jnp.where(lane8 // width == iy, target, 0.0)
    reach = width
    while reach < size_z:
        own_target = own_target + pltpu.roll(own_target, reach, 1)
        reach *= 2
    for r in range(part_rows):
        line = jnp.full((1, size_z), INVERSE_LEAVES[0], jnp.float32)
        for g in range(ny):
            for place in range(band):
                j = min(g * group_rows + place * part_rows + r + 1, TRIALS - 1)
                here = (lane8[0:1] // width == g) & ((lane8[0:1] & (band - 1)) == place)
                line = jnp.where(here, INVERSE_LEAVES[j], line)
        leaf_table[pl.ds(r, 1), :] = line

    edge_receive(scaled_copies)
    assemble(scaled, 1)
    for x, tile in enumerate(stencil(wide_rows, size_x)):
        benefit[pl.ds(x * size_y, size_y), :] = -tile
    benefit_out = pltpu.make_async_copy(benefit, benefit_hbm, out_sem)
    benefit_out.start()

    value = design[...]
    gain = value * jnp.sqrt(jnp.maximum(benefit[...], 0.0))
    floor_value = jnp.where(solid, 1.0, jnp.maximum(value - MOVE_LIMIT, 0.0))
    ceiling = jnp.where(solid, 1.0, jnp.minimum(value + MOVE_LIMIT, 1.0))

    def candidate(inverse_root):
        return jnp.minimum(ceiling, jnp.maximum(floor_value, gain * inverse_root))

    def total_over_x(j):
        trial = candidate(INVERSE_MIDDLES[j])
        return functools.reduce(
            lambda p, q: p + q, [trial[x * size_y : (x + 1) * size_y] for x in range(size_x)]
        )

    volumes = []
    for first in range(0, TRIALS, 8):
        tiles = [
            total_over_x(j) if j < TRIALS - 1 else jnp.zeros((8, size_z), jnp.float32)
            for j in range(first, first + 8)
        ]
        reach = 4
        while reach:
            lower = (slot_row & reach) == 0
            tiles = [
                jnp.where(lower, p, q)
                + jnp.where(lower, pltpu.roll(p, 8 - reach, 0), pltpu.roll(q, reach, 0))
                for p, q in zip(tiles[:reach], tiles[reach:])
            ]
            reach //= 2
        volumes.append(tiles[0])
    volumes = jnp.concatenate(volumes, axis=0)

    reach = 1
    lane_all = lax.broadcasted_iota(jnp.int32, volumes.shape, 1)
    while reach < band:
        volumes = volumes + jnp.where(
            (lane_all & reach) == 0,
            pltpu.roll(volumes, size_z - reach, 1),
            pltpu.roll(volumes, reach, 1),
        )
        reach *= 2

    for q in range(ny):
        packed = jnp.zeros((part_rows, size_z), jnp.float32)
        for g in range(ny):
            part = volumes[g * group_rows : g * group_rows + part_rows]
            for place in range(1, band):
                first = g * group_rows + place * part_rows
                part = jnp.where((lane & (band - 1)) == place, volumes[first : first + part_rows], part)
            turn = (width * (g - q)) % size_z
            if turn:
                part = pltpu.roll(part, turn, 1)
            packed = jnp.where(group == g, part, packed)
        share_send[q] = packed
    share_recv[pl.ds(iy, 1)] = share_send[pl.ds(iy, 1)]
    pending = []

    def along(count, me, place, source, buffer, send_sem, recv_sem):
        copies = []
        for step in range(1, count):
            peer = lax.rem(me + step, count)
            copy = pltpu.make_async_remote_copy(
                src_ref=source(peer),
                dst_ref=buffer.at[me],
                send_sem=send_sem.at[step],
                recv_sem=recv_sem.at[step],
                device_id=place(peer),
                device_id_type=MESH,
            )
            copy.start()
            copies.append(copy)
        for copy in copies:
            copy.wait_recv()
        pending.extend(copies)

    along(ny, iy, lambda at: (ix, at), lambda at: share_send.at[at], share_recv, share_send_sem, share_recv_sem)
    share = functools.reduce(lambda p, q: p + q, [share_recv[k] for k in range(ny)])
    gather_x[pl.ds(ix, 1)] = share[None]
    along(nx, ix, lambda at: (at, iy), lambda at: gather_x.at[ix], gather_x, gx_send_sem, gx_recv_sem)
    share = functools.reduce(lambda p, q: p + q, [gather_x[k] for k in range(nx)])

    chosen = jnp.where(share > own_target[0:1], leaf_table[...], INVERSE_LEAVES[0])
    chosen = jnp.min(chosen, axis=0, keepdims=True)
    reach = 1
    while reach < band:
        chosen = jnp.minimum(chosen, jnp.where(
            (lane8[0:1] & reach) == 0,
            pltpu.roll(chosen, size_z - reach, 1),
            pltpu.roll(chosen, reach, 1),
        ))
        reach *= 2
    reach = width
    while reach < size_z:
        chosen = jnp.minimum(chosen, pltpu.roll(chosen, reach, 1))
        reach *= 2
    gather_y[pl.ds(iy, 1)] = jnp.broadcast_to(chosen, (8, size_z))[None]
    along(ny, iy, lambda at: (ix, at), lambda at: gather_y.at[iy], gather_y, gy_send_sem, gy_recv_sem)
    multiplier = gather_y[0]
    for q in range(1, ny):
        multiplier = jnp.where(lane8 // width == q, gather_y[q], multiplier)
    chosen_out[...] = multiplier
    benefit_out.wait()

    edge_each(scaled_copies, lambda c, slot: c[slot].wait_send())
    for copy in pending:
        copy.wait_send()


def closing_kernel(negated, inverse_root, design, passive, sensitivity, design_next):
    benefit, value = negated[...], design[...]
    sensitivity[...] = -benefit
    trial = value * jnp.sqrt(jnp.maximum(benefit, 0.0)) * inverse_root[0:1, :]
    low = jnp.maximum(value - MOVE_LIMIT, 0.0)
    high = jnp.minimum(value + MOVE_LIMIT, 1.0)
    design_next[...] = jnp.where(passive[...] == 1, 1.0, jnp.minimum(high, jnp.maximum(low, trial)))


def shards(nx, ny, design, passive, basis_pairs, supports, stiffness, mass_matrix, volume_fraction):
    size_x, size_y, size_z = design.shape
    pairs = basis_pairs.shape[0]
    regions = volume_fraction.shape[0]
    cells = size_x * size_y
    fields_n = 6 * pairs
    flat = (cells, size_z)
    share_rows = TRIALS // ny * regions // size_z
    vmem = pl.BlockSpec(memory_space=pltpu.VMEM)
    f32, bf16 = jnp.float32, jnp.bfloat16
    dma = pltpu.SemaphoreType.DMA
    negated, inverse_root = pl.pallas_call(
        functools.partial(kernel, nx, ny, size_x, size_y, size_z, pairs, regions),
        out_shape=(jax.ShapeDtypeStruct(flat, f32), jax.ShapeDtypeStruct((size_y, size_z), f32)),
        in_specs=[pl.BlockSpec(memory_space=pltpu.HBM)] * 7,
        out_specs=(pl.BlockSpec(memory_space=pltpu.HBM), vmem),
        scratch_shapes=[
            pltpu.VMEM(flat, f32),
            pltpu.VMEM(flat, f32),
            pltpu.VMEM(flat, jnp.int32),
            pltpu.VMEM((fields_n, cells, size_z), f32),
            pltpu.VMEM(flat, jnp.int32),
            pltpu.VMEM(stiffness.shape, f32),
            pltpu.VMEM(mass_matrix.shape, f32),
            pltpu.VMEM((regions,), f32),
            pltpu.VMEM((fields_n, (size_x + 1) * 2 * size_y, size_z), f32),
            pltpu.VMEM((fields_n, size_y, size_z), f32),
            pltpu.VMEM((pairs, 8 * size_x, size_z), f32),
            pltpu.VMEM((fields_n, size_y, size_z), f32),
            pltpu.VMEM((pairs, 8 * (size_x + 1), size_z), f32),
            pltpu.VMEM((2, 4, 2, size_x, size_z), f32),
            pltpu.VMEM((2, 8, 2, size_y, size_z), f32),
            pltpu.VMEM(((size_x + 4) * 3 * size_y, size_z), f32),
            pltpu.VMEM(flat, f32),
            pltpu.VMEM((48 * size_y, 24 * size_y), bf16),
            pltpu.VMEM((48 * size_y, 12 * size_y), bf16),
            pltpu.VMEM((48 * size_y, 24 * size_y), bf16),
            pltpu.VMEM((48 * size_y, 24 * size_y), bf16),
            pltpu.VMEM(flat, f32),
            pltpu.VMEM(flat, f32),
            pltpu.VMEM((2 * cells, size_z), f32),
            pltpu.VMEM((ny, share_rows, size_z), f32),
            pltpu.VMEM((ny, share_rows, size_z), f32),
            pltpu.VMEM((nx, share_rows, size_z), f32),
            pltpu.VMEM((ny, 8, size_z), f32),
            pltpu.VMEM((share_rows, size_z), f32),
            dma((7,)),
            dma,
            dma((3,)),
            dma((3,)),
            dma((2, 8)),
            dma((2, 8)),
            dma((ny,)),
            dma((ny,)),
            dma((nx,)),
            dma((nx,)),
            dma((ny,)),
            dma((ny,)),
        ],
        compiler_params=pltpu.CompilerParams(
            collective_id=0, has_side_effects=True, vmem_limit_bytes=64 * 1024 * 1024
        ),
        name="sensitivity_update",
    )(
        design.reshape(flat),
        passive.reshape(flat),
        basis_pairs.reshape(fields_n, cells, size_z),
        supports.reshape(flat),
        stiffness,
        mass_matrix,
        volume_fraction,
    )
    sensitivity, design_next = pl.pallas_call(
        closing_kernel,
        out_shape=(jax.ShapeDtypeStruct(flat, f32), jax.ShapeDtypeStruct(flat, f32)),
        in_specs=[vmem] * 4,
        out_specs=(vmem, vmem),
        compiler_params=pltpu.CompilerParams(vmem_limit_bytes=64 * 1024 * 1024),
        name="design_update",
    )(negated, inverse_root, design.reshape(flat), passive.reshape(flat))
    return sensitivity.reshape(design.shape), design_next.reshape(design.shape)


def solution(mesh):
    placed = (
        P("gx", "gy", None),
        P("gx", "gy", None),
        P(None, None, None, "gx", "gy", None),
        P("gx", "gy", None),
        P(),
        P(),
        P(),
    )
    return jax.shard_map(
        functools.partial(shards, mesh.shape["gx"], mesh.shape["gy"]),
        mesh=mesh,
        in_specs=placed,
        out_specs=(P("gx", "gy", None), P("gx", "gy", None)),
        check_vma=False,
    )
```
